32 devices in a mesh: groups: 2 (over y), story: 4 (over z), rec: 2 (over x), blk: 2 (over core).
Axes of the slice: x: 2, y: 2, z: 4, core: 2. Of those that a mesh axis runs over, the one named last changes fastest.
Arguments:
- record_ids: int32 [128], P('groups'), parts along dimension 0, may hold values from 0 to 511
- ground_table: float32 [512], replicated, may hold values from -6 to 6
- mass_int: float32 [8, 2048], P(('groups', 'story'), ('rec', 'blk')), parts along dimension 0, may hold values from 0.5 to 2
- mass_face: float32 [8, 1536], P(('groups', 'story'), ('rec', 'blk')), parts along dimension 0, may hold values from 0.5 to 2
- pattern_int: float32 [8, 2048], P(('groups', 'story'), ('rec', 'blk')), parts along dimension 0, may hold values from -1 to 1
- pattern_face: float32 [8, 1536], P(('groups', 'story'), ('rec', 'blk')), parts along dimension 0, may hold values from -1 to 1
- disp_int: float32 [8, 2048, 64], P(('groups', 'story'), ('rec', 'blk')), parts along dimension 0, may hold values from -4 to 4
- vel_int: float32 [8, 2048, 64], P(('groups', 'story'), ('rec', 'blk')), parts along dimension 0, may hold values from -4 to 4
- acc_int: float32 [8, 2048, 64], P(('groups', 'story'), ('rec', 'blk')), parts along dimension 0, may hold values from -4 to 4
- disp_face: float32 [8, 1536, 64], P(('groups', 'story'), ('rec', 'blk')), parts along dimension 0, may hold values from -4 to 4
- vel_face: float32 [8, 1536, 64], P(('groups', 'story'), ('rec', 'blk')), parts along dimension 0, may hold values from -4 to 4
- acc_face: float32 [8, 1536, 64], P(('groups', 'story'), ('rec', 'blk')), parts along dimension 0, may hold values from -4 to 4
- interior_inverse: float32 [8, 2048, 2048], P(('groups', 'story'), ('rec', 'blk')), parts along dimension 0, may hold values from -0.125 to 0.125
- couple_below: float32 [8, 2048, 1536], P(('groups', 'story'), ('rec', 'blk')), parts along dimension 0, may hold values from -0.125 to 0.125
- couple_above: float32 [8, 2048, 1536], P(('groups', 'story'), ('rec', 'blk')), parts along dimension 0, may hold values from -0.125 to 0.125
- lower: float32 [8, 1536, 1536], P(('groups', 'story'), ('rec', 'blk')), parts along dimension 0, may hold values from -0.122474484 to 0.122474484
- pivot: float32 [8, 1536, 1536], P(('groups', 'story'), ('rec', 'blk')), parts along dimension 0, may hold values from -0.07654656 to 0.07654656
- upper: float32 [8, 1536, 1536], P(('groups', 'story'), ('rec', 'blk')), parts along dimension 0, may hold values from -0.122474484 to 0.122474484
Outputs:
- disp_int_new: float32 [8, 2048, 64], P(('groups', 'story'), ('rec', 'blk')), parts along dimension 0
- vel_int_new: float32 [8, 2048, 64], P(('groups', 'story'), ('rec', 'blk')), parts along dimension 0
- acc_int_new: float32 [8, 2048, 64], P(('groups', 'story'), ('rec', 'blk')), parts along dimension 0
- disp_face_new: float32 [8, 1536, 64], P(('groups', 'story'), ('rec', 'blk')), parts along dimension 0
- vel_face_new: float32 [8, 1536, 64], P(('groups', 'story'), ('rec', 'blk')), parts along dimension 0
- acc_face_new: float32 [8, 1536, 64], P(('groups', 'story'), ('rec', 'blk')), parts along dimension 0
The draws below stay inside these ranges and needn't reach their ends.
There are 2 independent parts, one for each index of `groups`. The reference program is written for one: setup_inputs(seed, part) draws one part's arguments, and reference() takes and returns one part's arrays. A program takes and returns all parts, laid end to end along the dimension named above; an argument that names none is the same for every part. Nothing has to cross between parts.
Inputs may be any that keep to these rules, and one draw needn't show every extreme that they name: `record_ids`: each entry indexes ground_table.
All inputs are finite; a program needn't handle non-finite values.
Results may differ from the reference program's by a relative error of at most 0.0001.
Values sent between devices are 32-bit elements; how exact they have to be, the bound alone decides.
No kernel may reach another device: no remote copies, remote signals or barrier semaphores. Data moves between devices by JAX's collectives and lax.ppermute only.
A program may use at most 64 MiB of HBM per device.

```python
import math
import jax
import jax.numpy as jnp
from jax import lax

NG = 1536
NI = 2048
R = 64
LIB = 512
GROUPS = 4


def place_ends(entries, rng, smallest, high):
    place = [jax.random.randint(jax.random.fold_in(rng, axis), (), 0, length) for axis, length in enumerate(entries.shape)]
    longest = entries.shape.index(max(entries.shape))
    beside = place[:longest] + [(place[longest] + 1) % entries.shape[longest]] + place[longest + 1:]
    return entries.at[tuple(place)].set(smallest).at[tuple(beside)].set(high)


def block_scale(rng, extent, pieces, low, largest):
    level, own = 1.0, jax.random.fold_in(rng, 6)
    for axis_at, parts in pieces:
        heights = jnp.exp(jax.random.uniform(jax.random.fold_in(own, axis_at), (parts,), jnp.float32, low / len(pieces), largest / len(pieces)))
        level = level * jnp.repeat(heights, extent[axis_at] // parts).reshape([-1 if axis == axis_at else 1 for axis in range(len(extent))])
    return level


def gaussian(rng, extent, spread, most, shards=(), held_as=jnp.bfloat16):
    drawn = jax.random.normal(rng, extent, jnp.float32) * spread
    if len(shards) > 0:
        drawn = block_scale(rng, extent, shards, -0.22, 0.18) * drawn
    return jnp.clip(drawn, min=-most, max=most).astype(held_as)


def setup_inputs(seed: int = 0, part: int = 0) -> dict:
    streams_of = jax.random.split(jax.random.key(seed), 19)
    own_keys = jax.random.split(jax.random.fold_in(streams_of[18], part), 19)
    record_ids = place_ends(jax.random.randint(own_keys[0], (R,), 0, LIB), jax.random.fold_in(own_keys[0], 1), 0, LIB - 1).astype(jnp.int32)
    ground_table = gaussian(streams_of[1], (LIB,), 1.0, 6.0, (), jnp.float32)
    mass_int = jnp.clip(jnp.exp(math.log(2.0) - 1.3862944 * jax.random.uniform(own_keys[2], (GROUPS, NI), jnp.float32) ** block_scale(own_keys[2], (GROUPS, NI), ((0, 4), (1, 4)), -0.2, 0.2)), 0.5, 2.0)
    mass_face = jnp.clip(jnp.exp(math.log(2.0) - 1.3862944 * jax.random.uniform(own_keys[3], (GROUPS, NG), jnp.float32) ** block_scale(own_keys[3], (GROUPS, NG), ((0, 4), (1, 4)), -0.2, 0.2)), 0.5, 2.0)
    pattern_int = jnp.clip(jax.random.uniform(own_keys[4], (GROUPS, NI), jnp.float32, -1.0, 1.0) * block_scale(own_keys[4], (GROUPS, NI), ((0, 4), (1, 4)), -0.4, 0.0), -1.0, 1.0)
    pattern_face = jnp.clip(jax.random.uniform(own_keys[5], (GROUPS, NG), jnp.float32, -1.0, 1.0) * block_scale(own_keys[5], (GROUPS, NG), ((0, 4), (1, 4)), -0.4, 0.0), -1.0, 1.0)
    disp_int = gaussian(own_keys[6], (GROUPS, NI, R), 0.5, 4.0, ((0, 4), (1, 4)), jnp.float32)
    vel_int = gaussian(own_keys[7], (GROUPS, NI, R), 0.5, 4.0, ((0, 4), (1, 4)), jnp.float32)
    acc_int = gaussian(own_keys[8], (GROUPS, NI, R), 0.5, 4.0, ((0, 4), (1, 4)), jnp.float32)
    disp_face = gaussian(own_keys[9], (GROUPS, NG, R), 0.5, 4.0, ((0, 4), (1, 4)), jnp.float32)
    vel_face = gaussian(own_keys[10], (GROUPS, NG, R), 0.5, 4.0, ((0, 4), (1, 4)), jnp.float32)
    acc_face = gaussian(own_keys[11], (GROUPS, NG, R), 0.5, 4.0, ((0, 4), (1, 4)), jnp.float32)
    interior_inverse = gaussian(own_keys[12], (GROUPS, NI, NI), NI ** -0.5, 0.125, ((0, 4), (1, 4)), jnp.float32)
    couple_below = gaussian(own_keys[13], (GROUPS, NI, NG), NI ** -0.5, 0.125, ((0, 4), (1, 4)), jnp.float32)
    couple_above = gaussian(own_keys[14], (GROUPS, NI, NG), NI ** -0.5, 0.125, ((0, 4), (1, 4)), jnp.float32)
    lower = gaussian(own_keys[15], (GROUPS, NG, NG), (0.8 / NG ** 0.5), 0.122474484, ((0, 4), (1, 4)), jnp.float32)
    pivot = gaussian(own_keys[16], (GROUPS, NG, NG), (0.5 / NG ** 0.5), 0.07654656, ((0, 4), (1, 4)), jnp.float32)
    upper = gaussian(own_keys[17], (GROUPS, NG, NG), (0.8 / NG ** 0.5), 0.122474484, ((0, 4), (1, 4)), jnp.float32)
    return dict(record_ids=record_ids, ground_table=ground_table, mass_int=mass_int, mass_face=mass_face, pattern_int=pattern_int, pattern_face=pattern_face, disp_int=disp_int, vel_int=vel_int, acc_int=acc_int, disp_face=disp_face, vel_face=vel_face, acc_face=acc_face, interior_inverse=interior_inverse, couple_below=couple_below, couple_above=couple_above, lower=lower, pivot=pivot, upper=upper)


def product(left, right):
    return jnp.dot(left, right, precision=lax.Precision.HIGHEST, preferred_element_type=jnp.float32)


def newmark_load(mass, pattern, disp, vel, acc, ground):
    return mass[:, :, None] * (disp + 2.0 * vel + acc - pattern[:, :, None] * ground[None, None, :])


def reference(record_ids, ground_table, mass_int, mass_face, pattern_int, pattern_face, disp_int, vel_int, acc_int, disp_face, vel_face, acc_face, interior_inverse, couple_below, couple_above, lower, pivot, upper):
    ground = ground_table[record_ids.astype(jnp.int32)]
    load_int = newmark_load(mass_int, pattern_int, disp_int, vel_int, acc_int, ground)
    load_face = newmark_load(mass_face, pattern_face, disp_face, vel_face, acc_face, ground)
    groups = load_int.shape[0]
    interior_part = [product(interior_inverse[s], load_int[s]) for s in range(groups)]
    condensed = []
    for s in range(groups):
        term = load_face[s] - product(couple_above[s].T, interior_part[s])
        if s + 1 < groups:
            term = term - product(couple_below[s + 1].T, interior_part[s + 1])
        condensed.append(term)
    forward = [condensed[0]]
    for s in range(1, groups):
        forward.append(condensed[s] - product(lower[s], forward[s - 1]))
    pivoted = [product(pivot[s], forward[s]) for s in range(groups)]
    faces = [None] * groups
    faces[groups - 1] = pivoted[groups - 1]
    for s in range(groups - 2, -1, -1):
        faces[s] = pivoted[s] - product(upper[s], faces[s + 1])
    interiors = []
    for s in range(groups):
        coupled = product(couple_above[s], faces[s])
        if s > 0:
            coupled = product(couple_below[s], faces[s - 1]) + coupled
        interiors.append(product(interior_inverse[s], load_int[s] - coupled))
    disp_face_new = jnp.stack(faces)
    disp_int_new = jnp.stack(interiors)
    acc_int_new = (disp_int_new - disp_int) - 2.0 * vel_int - acc_int
    acc_face_new = (disp_face_new - disp_face) - 2.0 * vel_face - acc_face
    vel_int_new = vel_int + acc_int + acc_int_new
    vel_face_new = vel_face + acc_face + acc_face_new
    return disp_int_new, vel_int_new, acc_int_new, disp_face_new, vel_face_new, acc_face_new
```

```python
import jax
import jax.numpy as jnp
from jax import lax
from jax.sharding import PartitionSpec as P

AXES = ("story", "rec", "blk")


def product(left, right):
    return lax.dot_general(
        left,
        right,
        (((1,), (1,)), ((), ())),
        precision=lax.Precision.HIGH,
        preferred_element_type=jnp.float32,
    )


def product_plain(left, right):
    return lax.dot_general(
        left,
        right,
        (((1,), (0,)), ((), ())),
        precision=lax.Precision.HIGH,
        preferred_element_type=jnp.float32,
    )


class Moves:
    def __init__(self):
        self.stories = lax.axis_size("story")
        self.chips = lax.axis_size("rec")
        self.cores = lax.axis_size("blk")
        assert self.cores == 2 and self.chips & (self.chips - 1) == 0
        self.s = lax.axis_index("story")
        self.r = lax.axis_index("rec")
        self.b = lax.axis_index("blk")

    def permute(self, value, target):
        pairs = []
        for s in range(self.stories):
            for r in range(self.chips):
                for b in range(self.cores):
                    t, q, c = target(s, r, b)
                    pairs.append(
                        (
                            (s * self.chips + r) * self.cores + b,
                            (t * self.chips + q) * self.cores + c,
                        )
                    )
        return lax.ppermute(value, AXES, pairs)

    def core(self, value):
        return self.permute(value, lambda s, r, b: (s, r, 1 - b))

    def chip(self, value, j):
        return self.permute(value, lambda s, r, b: (s, r ^ j, b))

    def story(self, value, parity, j):
        def target(s, r, b):
            t = s ^ 1 if parity == 0 else ((s - 1) ^ 1) + 1
            if t < 0 or t >= self.stories:
                return s, r, 1 - b
            return t, r ^ j, b

        return self.permute(value, target)

    def by_core(self, own, other, axis):
        first = jnp.where(self.b == 0, own, other)
        second = jnp.where(self.b == 0, other, own)
        return jnp.concatenate([first, second], axis=axis)

    def by_chip(self, pieces, axis=1):
        bit = 1
        while bit < self.chips:
            swap = (self.r & bit) != 0
            pieces = [jnp.where(swap, pieces[j ^ bit], pieces[j]) for j in range(self.chips)]
            bit *= 2
        return jnp.concatenate(pieces, axis=axis)

    def gather_chips(self, value):
        return self.by_chip([value] + [self.chip(value, j) for j in range(1, self.chips)])

    def gather_story(self, value, parity):
        return self.by_chip([self.story(value, parity, j) for j in range(self.chips)])

    def half(self, value, which, axis=0):
        width = value.shape[axis] // 2
        return lax.dynamic_slice_in_dim(value, which * width, width, axis)

    def to_half(self, value):
        other = self.core(self.half(value, 1 - self.b))
        return self.by_core(self.half(value, self.b), other, 1)

    def from_half(self, value):
        other = self.core(self.half(value, 1 - self.b, 1))
        return self.by_core(self.half(value, self.b, 1), other, 0)


def shards(
    record_ids,
    ground_table,
    mass_int,
    mass_face,
    pattern_int,
    pattern_face,
    disp_int,
    vel_int,
    acc_int,
    disp_face,
    vel_face,
    acc_face,
    interior_inverse,
    couple_below,
    couple_above,
    lower,
    pivot,
    upper,
):
    mv = Moves()
    s, r, b = mv.s, mv.r, mv.b
    last = mv.stories - 1
    library = ground_table.shape[0]
    picked = record_ids[:, None] == jnp.arange(library, dtype=jnp.int32)[None, :]
    ground = jnp.sum(jnp.where(picked, ground_table[None, :], 0.0), axis=1)
    d_i, v_i, a_i = disp_int[0].T, vel_int[0].T, acc_int[0].T
    d_f, v_f, a_f = disp_face[0].T, vel_face[0].T, acc_face[0].T
    load_int = mass_int * (d_i + 2.0 * v_i + a_i - pattern_int * ground[:, None])
    load_face = mass_face * (d_f + 2.0 * v_f + a_f - pattern_face * ground[:, None])

    def chip_rows(matrix):
        own = matrix[0]
        return own, mv.core(own)

    def chip_product(left, rows):
        return mv.by_core(product(left, rows[0]), product(left, rows[1]), 1)

    across = [mv.chip(load_int, j) for j in range(1, mv.chips)]
    beside = [mv.core(piece) for piece in [load_int] + across]
    load_full = mv.by_chip(
        [mv.by_core(own, other, 1) for own, other in zip([load_int] + across, beside)]
    )
    interior_part = product(load_full, interior_inverse[0])
    forces = jnp.stack(
        [product_plain(interior_part, couple_above[0]), product_plain(interior_part, couple_below[0])]
    )
    forces = mv.half(forces, b, 1) + mv.core(mv.half(forces, 1 - b, 1))
    width = forces.shape[2] // mv.chips

    def chunk(which, j):
        return lax.dynamic_slice_in_dim(forces[which], (r ^ j) * width, width, 1)

    above_force = chunk(0, 0)
    for j in range(1, mv.chips):
        above_force = above_force + mv.chip(chunk(0, j), j)
    below_force = []
    for parity in range(2):
        total = mv.story(chunk(1, 0), parity, 0)
        for j in range(1, mv.chips):
            total = total + mv.story(chunk(1, j), parity, j)
        below_force.append(total)
    below_force = jnp.where(s % 2 == 0, below_force[0], below_force[1])
    below_force = jnp.where(s == last, 0.0, below_force)
    condensed = mv.to_half(load_face) - above_force - below_force

    lower_rows, pivot_rows, upper_rows = chip_rows(lower), chip_rows(pivot), chip_rows(upper)
    forward = condensed
    for k in range(1, mv.stories):
        came = mv.gather_story(forward, (k - 1) % 2)
        forward = jnp.where(s == k, condensed - chip_product(came, lower_rows), forward)
    pivoted = chip_product(mv.gather_chips(forward), pivot_rows)
    face = pivoted
    for k in range(mv.stories - 2, -1, -1):
        came = mv.gather_story(face, k % 2)
        face = jnp.where(s == k, pivoted - chip_product(came, upper_rows), face)

    below_rows, above_rows = chip_rows(couple_below), chip_rows(couple_above)
    inverse_rows = chip_rows(interior_inverse)
    even = mv.gather_story(face, 0)
    odd = mv.gather_story(face, 1)
    face_below = jnp.where(s % 2 == 1, even, odd)
    face_below = jnp.where(s == 0, 0.0, face_below)
    coupled = chip_product(mv.gather_chips(face), above_rows) + chip_product(face_below, below_rows)
    reduced = mv.to_half(load_int) - coupled
    interior = chip_product(mv.gather_chips(reduced), inverse_rows)

    u_i, u_f = mv.from_half(interior), mv.from_half(face)
    new_a_i = u_i - d_i - 2.0 * v_i - a_i
    new_a_f = u_f - d_f - 2.0 * v_f - a_f
    new_v_i = v_i + a_i + new_a_i
    new_v_f = v_f + a_f + new_a_f
    return tuple(out.T[None] for out in (u_i, new_v_i, new_a_i, u_f, new_v_f, new_a_f))


def solution(mesh):
    whole, rows, cube = P(), P(("groups", "story"), ("rec", "blk")), P(("groups", "story"), ("rec", "blk"), None)
    in_specs = (P("groups"), whole) + (rows,) * 4 + (cube,) * 12
    return jax.shard_map(shards, mesh=mesh, in_specs=in_specs, out_specs=(cube,) * 6, check_vma=False)
```

```python
import functools

import jax
import jax.numpy as jnp
from jax import lax
from jax.experimental import pallas as pl
from jax.experimental.pallas import tpu as pltpu
from jax.sharding import PartitionSpec as P

AXES = ("story", "rec", "blk")
TILE = 256
VMEM = pl.BlockSpec(memory_space=pltpu.VMEM)


def split(value):
    high = value.astype(jnp.bfloat16)
    return high, (value - high.astype(jnp.float32)).astype(jnp.bfloat16)


def stacked(value):
    return jnp.concatenate(split(value), axis=0)


def matmul(left, right, over):
    rows = left.shape[0] // 2
    total = None
    for part in reversed(split(right)):
        both = lax.dot_general(
            left, part, (((1,), (over,)), ((), ())), preferred_element_type=jnp.float32
        )
        both = both[rows:] + both[:rows]
        total = both if total is None else total + both
    return total


def times_rows(left, *refs):
    left = stacked(left)
    count = refs[0].shape[0]
    ends = count * len(refs)
    columns = []
    for start in range(0, ends, TILE):
        stop = min(start + TILE, ends)
        blocks = []
        for i, ref in enumerate(refs):
            low, high = max(start - i * count, 0), min(stop - i * count, count)
            if low < high:
                blocks.append(ref[low:high, :])
        columns.append(matmul(left, jnp.concatenate(blocks, axis=0), 1))
    return jnp.concatenate(columns, axis=1)


def times(left, ref):
    left = stacked(left)
    width = ref.shape[1]
    columns = [matmul(left, ref[:, n : min(n + TILE, width)], 0) for n in range(0, width, TILE)]
    return jnp.concatenate(columns, axis=1)


def in_order(pieces, own):
    bit = 1
    while bit < len(pieces):
        swap = (own & bit) != 0
        pieces = [jnp.where(swap, pieces[j ^ bit], pieces[j]) for j in range(len(pieces))]
        bit *= 2
    return pieces


def joined(refs, axis="rec"):
    own = lax.axis_index(axis) if len(refs) > 1 else 0
    return jnp.concatenate(in_order([ref[...] for ref in refs], own), axis=1)


def store_rows(ref, value):
    half = value.shape[1] // 2
    swap = lax.axis_index("blk") == 1
    own, other = value[:, :half], value[:, half:]
    ref[...] = jnp.concatenate([jnp.where(swap, other, own), jnp.where(swap, own, other)], axis=1)


def call(kernel, shapes, *groups):
    flat = [value for group in groups for value in group]

    def body(*refs):
        at, parts = 0, []
        for group in groups:
            parts.append(refs[at : at + len(group)])
            at += len(group)
        kernel(*parts, *refs[at:])

    out = [jax.ShapeDtypeStruct(shape, jnp.float32) for shape in shapes]
    return pl.pallas_call(
        body,
        in_specs=[VMEM] * len(flat),
        out_specs=[VMEM] * len(out),
        out_shape=out,
        compiler_params=pltpu.CompilerParams(vmem_limit_bytes=40 << 20),
    )(*flat)


def forces_kernel(swap_chips, pieces, matrices, mine, theirs):
    inverse, above, below = matrices
    if swap_chips:
        chips = len(pieces) // 2
        core = lax.axis_index("blk")
        sets = [in_order([pieces[2 * j][...], pieces[2 * j + 1][...]], core) for j in range(chips)]
        sets = [jnp.concatenate(pair, axis=1) for pair in sets]
        full = jnp.concatenate(in_order(sets, lax.axis_index("rec")), axis=1)
    else:
        full = pieces[0][...]
    part = times_rows(full, inverse)
    half = part.shape[0] // 2
    second = lax.axis_index("blk") == 1
    for i, matrix in enumerate((above, below)):
        force = times(part, matrix)
        mine[i] = jnp.where(second, force[half:], force[:half])
        theirs[i] = jnp.where(second, force[:half], force[half:])


def chunks_kernel(inputs, *outs):
    mine, came = inputs
    chips = len(outs) // 2
    for i in range(2):
        total = mine[i] + came[i]
        width = total.shape[1] // chips
        pieces = [total[:, j * width : (j + 1) * width] for j in range(chips)]
        for j, piece in enumerate(in_order(pieces, lax.axis_index("rec"))):
            outs[i * chips + j][...] = piece


def step_kernel(story, pieces, rows, terms, out):
    first, latest = terms

    @pl.when(lax.axis_index("story") == story)
    def _():
        store_rows(out, times_rows(joined(pieces), *rows))
        out[...] = first[...] - out[...]

    @pl.when(lax.axis_index("story") != story)
    def _():
        out[...] = latest[...]


def rows_kernel(pieces, rows, out):
    store_rows(out, times_rows(joined(pieces), *rows))


def coupled_kernel(load, early, here, even, odd, above, below, out):
    story = lax.axis_index("story")

    @pl.when(story == 0)
    def _():
        store_rows(out, times_rows(joined(here), *above))
        out[...] = load[0][...] - out[...]

    @pl.when(story > 0)
    def _():
        use = lax.rem(story, 2) == 1
        refs = [jnp.where(use, e[...], o[...]) for e, o in zip(even, odd)]
        own = lax.axis_index("rec") if len(refs) > 1 else 0
        value = jnp.concatenate(in_order(refs, own), axis=1)
        store_rows(out, times_rows(value, *below))
        out[...] = load[0][...] - early[0][...] - out[...]


def last_kernel(pieces, rows, mine, theirs):
    value = times_rows(joined(pieces), *rows)
    half = value.shape[1] // 2
    mine[...] = value[:, :half]
    theirs[...] = value[:, half:]


class Moves:
    def __init__(self):
        self.stories = lax.axis_size("story")
        self.chips = lax.axis_size("rec")
        self.cores = lax.axis_size("blk")
        assert self.cores == 2 and self.chips & (self.chips - 1) == 0
        self.s = lax.axis_index("story")
        self.r = lax.axis_index("rec")
        self.b = lax.axis_index("blk")

    def permute(self, value, target):
        pairs = []
        for s in range(self.stories):
            for r in range(self.chips):
                for b in range(self.cores):
                    t, q, c = target(s, r, b)
                    pairs.append(
                        (
                            (s * self.chips + r) * self.cores + b,
                            (t * self.chips + q) * self.cores + c,
                        )
                    )
        return lax.ppermute(value, AXES, pairs)

    def core(self, value):
        return self.permute(value, lambda s, r, b: (s, r, 1 - b))

    def chip(self, value, j):
        return self.permute(value, lambda s, r, b: (s, r ^ j, b))

    def story(self, value, parity, j):
        def target(s, r, b):
            t = s ^ 1 if parity == 0 else ((s - 1) ^ 1) + 1
            if t < 0 or t >= self.stories:
                return (s, r ^ 1, b) if self.chips > 1 else (s, r, 1 - b)
            return t, r ^ j, b

        return self.permute(value, target)

    def by_core(self, own, other, axis):
        first = jnp.where(self.b == 0, own, other)
        second = jnp.where(self.b == 0, other, own)
        return jnp.concatenate([first, second], axis=axis)

    def by_chip(self, pieces, axis=1):
        bit = 1
        while bit < self.chips:
            swap = (self.r & bit) != 0
            pieces = [jnp.where(swap, pieces[j ^ bit], pieces[j]) for j in range(self.chips)]
            bit *= 2
        return jnp.concatenate(pieces, axis=axis)

    def pieces(self, pieces):
        return pieces if pieces[0].shape[1] % 128 == 0 else [self.by_chip(pieces)]

    def gather_chips(self, value):
        return self.pieces([value] + [self.chip(value, j) for j in range(1, self.chips)])

    def gather_story(self, value, parity):
        return self.pieces([self.story(value, parity, j) for j in range(self.chips)])

    def half(self, value, which, axis=0):
        width = value.shape[axis] // 2
        return lax.dynamic_slice_in_dim(value, which * width, width, axis)

    def to_half(self, value):
        other = self.core(self.half(value, 1 - self.b))
        return self.by_core(self.half(value, self.b), other, 1)

    def from_half(self, value):
        other = self.core(self.half(value, 1 - self.b, 1))
        return self.by_core(self.half(value, self.b, 1), other, 0)


def shards(
    record_ids,
    ground_table,
    mass_int,
    mass_face,
    pattern_int,
    pattern_face,
    disp_int,
    vel_int,
    acc_int,
    disp_face,
    vel_face,
    acc_face,
    interior_inverse,
    couple_below,
    couple_above,
    lower,
    pivot,
    upper,
):
    mv = Moves()
    s, r, b = mv.s, mv.r, mv.b
    last = mv.stories - 1
    library = ground_table.shape[0]
    picked = record_ids[:, None] == jnp.arange(library, dtype=jnp.int32)[None, :]
    ground = jnp.sum(jnp.where(picked, ground_table[None, :], 0.0), axis=1)
    d_i, v_i, a_i = disp_int[0].T, vel_int[0].T, acc_int[0].T
    d_f, v_f, a_f = disp_face[0].T, vel_face[0].T, acc_face[0].T
    load_int = mass_int * (d_i + 2.0 * v_i + a_i - pattern_int * ground[:, None])
    load_face = mass_face * (d_f + 2.0 * v_f + a_f - pattern_face * ground[:, None])

    records = load_int.shape[0]
    half = records // 2
    rows_int, rows_face = 2 * load_int.shape[1], 2 * load_face.shape[1]
    faces = couple_above.shape[2]

    def chip_rows(matrix):
        own = matrix[0]
        return [own, mv.core(own)]

    across = [mv.chip(load_int, j) for j in range(1, mv.chips)]
    beside = [mv.core(piece) for piece in [load_int] + across]
    pieces = [piece for pair in zip([load_int] + across, beside) for piece in pair]
    aligned = load_int.shape[1] % 128 == 0
    if not aligned:
        pieces = [
            mv.by_chip([mv.by_core(pieces[2 * j], pieces[2 * j + 1], 1) for j in range(mv.chips)])
        ]
    mine, theirs = call(
        functools.partial(forces_kernel, aligned),
        [(2, half, faces)] * 2,
        pieces,
        [interior_inverse[0], couple_above[0], couple_below[0]],
    )
    chunks = call(
        chunks_kernel,
        [(half, faces // mv.chips)] * (2 * mv.chips),
        [mine, mv.core(theirs)],
    )
    above_force = chunks[0]
    for j in range(1, mv.chips):
        above_force = above_force + mv.chip(chunks[j], j)
    below_force = []
    for parity in range(2):
        total = mv.story(chunks[mv.chips], parity, 0)
        for j in range(1, mv.chips):
            total = total + mv.story(chunks[mv.chips + j], parity, j)
        below_force.append(total)
    condensed = mv.to_half(load_face) - above_force
    condensed = jnp.where((s % 2 == 0) & (s != last), condensed - below_force[0], condensed)

    lower_rows, pivot_rows, upper_rows = chip_rows(lower), chip_rows(pivot), chip_rows(upper)
    shape = [(half, rows_face)]
    forward = condensed
    for k in range(1, mv.stories):
        came = mv.gather_story(forward, (k - 1) % 2)
        if k == 1:
            condensed = jnp.where((s % 2 == 1) & (s != last), condensed - below_force[1], condensed)
        (forward,) = call(
            functools.partial(step_kernel, k), shape, came, lower_rows, [condensed, forward]
        )
    (pivoted,) = call(rows_kernel, shape, mv.gather_chips(forward), pivot_rows)

    below_rows, above_rows = chip_rows(couple_below), chip_rows(couple_above)
    inverse_rows = chip_rows(interior_inverse)
    shape_int = [(half, rows_int)]
    face = pivoted
    for k in range(mv.stories - 2, -1, -1):
        came = mv.gather_story(face, k % 2)
        if k == 0:
            odd = mv.gather_story(face, 1)
            (early,) = call(rows_kernel, shape_int, mv.gather_chips(face), above_rows)
        (face,) = call(functools.partial(step_kernel, k), shape, came, upper_rows, [pivoted, face])

    even = mv.gather_story(face, 0)
    (reduced,) = call(
        coupled_kernel,
        shape_int,
        [mv.to_half(load_int)],
        [early],
        mv.gather_chips(face),
        even,
        odd,
        above_rows,
        below_rows,
    )
    mine, theirs = call(
        last_kernel,
        [(half, rows_int // 2)] * 2,
        mv.gather_chips(reduced),
        inverse_rows,
    )

    u_f = mv.from_half(face)
    u_i = mv.by_core(mine, mv.core(theirs), 0)
    new_a_i = u_i - d_i - 2.0 * v_i - a_i
    new_a_f = u_f - d_f - 2.0 * v_f - a_f
    new_v_i = v_i + a_i + new_a_i
    new_v_f = v_f + a_f + new_a_f
    return tuple(out.T[None] for out in (u_i, new_v_i, new_a_i, u_f, new_v_f, new_a_f))


def solution(mesh):
    whole, rows, cube = P(), P(("groups", "story"), ("rec", "blk")), P(("groups", "story"), ("rec", "blk"), None)
    in_specs = (P("groups"), whole) + (rows,) * 4 + (cube,) * 12
    return jax.shard_map(shards, mesh=mesh, in_specs=in_specs, out_specs=(cube,) * 6, check_vma=False)
```

```python
import functools

import jax
import jax.numpy as jnp
from jax import lax
from jax.experimental import pallas as pl
from jax.experimental.pallas import tpu as pltpu
from jax.sharding import PartitionSpec as P

AXES = ("story", "rec", "blk")
TILE = 256
VMEM = pl.BlockSpec(memory_space=pltpu.VMEM)


def split(value):
    high = value.astype(jnp.bfloat16)
    return high, (value - high.astype(jnp.float32)).astype(jnp.bfloat16)


def stacked(value):
    return jnp.concatenate(split(value), axis=0)


def matmul(left, right, over):
    rows = left.shape[0] // 2
    total = None
    for part in reversed(split(right)):
        both = lax.dot_general(
            left, part, (((1,), (over,)), ((), ())), preferred_element_type=jnp.float32
        )
        both = both[rows:] + both[:rows]
        total = both if total is None else total + both
    return total


class Rows:
    def __init__(self, refs, buffer, sems, first_sem=0):
        self.buffer, self.blocks = buffer, []
        count = refs[0].shape[0]
        self.ends = count * len(refs)
        for start in range(0, self.ends, TILE):
            stop = min(start + TILE, self.ends)
            copies = []
            for i, ref in enumerate(refs):
                low, high = max(start - i * count, 0), min(stop - i * count, count)
                if low < high:
                    copies.append(
                        pltpu.make_async_copy(
                            ref.at[pl.ds(low, high - low), :],
                            buffer.at[pl.ds(low + i * count, high - low), :],
                            sems.at[first_sem],
                        )
                    )
                    first_sem += 1
            self.blocks.append((start, stop, copies))
        self.next_sem = first_sem

    def start(self):
        for _, _, copies in self.blocks:
            for copy in copies:
                copy.start()

    def times(self, left):
        left = stacked(left)
        columns = []
        for start, stop, copies in self.blocks:
            for copy in copies:
                copy.wait()
            columns.append(matmul(left, self.buffer[start:stop, :], 1))
        return jnp.concatenate(columns, axis=1)

    def weigh(self, left):
        total = None
        for start, stop, copies in self.blocks:
            for copy in copies:
                copy.wait()
            part = matmul(stacked(left[:, start:stop]), self.buffer[start:stop, :], 0)
            total = part if total is None else total + part
        return total


def fetches(count, matrices):
    return sum(
        1
        for start in range(0, count * matrices, TILE)
        for i in range(matrices)
        if max(start, i * count) < min(start + TILE, (i + 1) * count)
    )


def in_order(pieces, own):
    bit = 1
    while bit < len(pieces):
        swap = (own & bit) != 0
        pieces = [jnp.where(swap, pieces[j ^ bit], pieces[j]) for j in range(len(pieces))]
        bit *= 2
    return pieces


def joined(refs, axis="rec"):
    own = lax.axis_index(axis) if len(refs) > 1 else 0
    return jnp.concatenate(in_order([ref[...] for ref in refs], own), axis=1)


def store_rows(ref, value):
    half = value.shape[1] // 2
    swap = lax.axis_index("blk") == 1
    own, other = value[:, :half], value[:, half:]
    ref[...] = jnp.concatenate([jnp.where(swap, other, own), jnp.where(swap, own, other)], axis=1)


def call(kernel, shapes, matrices, *groups):
    flat = [value for group in matrices for value in group]
    arrays = [value for group in groups for value in group]
    outs = len(shapes)
    buffers, sems = [], 0
    for group in matrices:
        count, width = group[0].shape
        buffers.append(pltpu.VMEM((count * len(group), width), jnp.float32))
        sems += fetches(count, len(group))
    scratch = buffers + [pltpu.SemaphoreType.DMA((sems,))] if matrices else []

    def body(*refs):
        at, rows, parts, sem = 0, [], [], 0
        held = refs[len(flat) + len(arrays) + outs :]
        for i, group in enumerate(matrices):
            rows.append(Rows(refs[at : at + len(group)], held[i], held[-1], sem))
            sem = rows[-1].next_sem
            at += len(group)
        for group in groups:
            parts.append(refs[at : at + len(group)])
            at += len(group)
        kernel(*rows, *parts, *refs[at : at + outs])

    out = [jax.ShapeDtypeStruct(shape, jnp.float32) for shape in shapes]
    return pl.pallas_call(
        body,
        in_specs=[pl.BlockSpec(memory_space=pl.ANY)] * len(flat) + [VMEM] * len(arrays),
        out_specs=[VMEM] * outs,
        out_shape=out,
        scratch_shapes=scratch,
        compiler_params=pltpu.CompilerParams(vmem_limit_bytes=24 << 20),
    )(*flat, *arrays)


def forces_kernel(aligned, inverse, above, below, pieces, mine, theirs):
    for rows in (inverse, above, below):
        rows.start()
    if aligned:
        chips = len(pieces) // 2
        core = lax.axis_index("blk")
        sets = [in_order([pieces[2 * j][...], pieces[2 * j + 1][...]], core) for j in range(chips)]
        sets = [jnp.concatenate(pair, axis=1) for pair in sets]
        full = jnp.concatenate(in_order(sets, lax.axis_index("rec")), axis=1)
    else:
        full = pieces[0][...]
    part = inverse.times(full)
    half = part.shape[0] // 2
    second = lax.axis_index("blk") == 1
    for i, rows in enumerate((above, below)):
        force = rows.weigh(part)
        mine[i] = jnp.where(second, force[half:], force[:half])
        theirs[i] = jnp.where(second, force[:half], force[half:])


def chunks_kernel(inputs, *outs):
    mine, came = inputs
    chips = len(outs) // 2
    for i in range(2):
        total = mine[i] + came[i]
        width = total.shape[1] // chips
        pieces = [total[:, j * width : (j + 1) * width] for j in range(chips)]
        for j, piece in enumerate(in_order(pieces, lax.axis_index("rec"))):
            outs[i * chips + j][...] = piece


def step_kernel(story, rows, pieces, terms, out):
    first, latest = terms

    @pl.when(lax.axis_index("story") == story)
    def _():
        rows.start()
        store_rows(out, rows.times(joined(pieces)))
        out[...] = first[...] - out[...]

    @pl.when(lax.axis_index("story") != story)
    def _():
        out[...] = latest[...]


def rows_kernel(rows, pieces, out):
    rows.start()
    store_rows(out, rows.times(joined(pieces)))


def coupled_kernel(above, below, load, early, here, even, odd, out):
    story = lax.axis_index("story")

    @pl.when(story == 0)
    def _():
        above.start()
        store_rows(out, above.times(joined(here)))
        out[...] = load[0][...] - out[...]

    @pl.when(story > 0)
    def _():
        below.start()
        use = lax.rem(story, 2) == 1
        refs = [jnp.where(use, e[...], o[...]) for e, o in zip(even, odd)]
        own = lax.axis_index("rec") if len(refs) > 1 else 0
        value = jnp.concatenate(in_order(refs, own), axis=1)
        store_rows(out, below.times(value))
        out[...] = load[0][...] - early[0][...] - out[...]


def last_kernel(rows, pieces, mine, theirs):
    rows.start()
    value = rows.times(joined(pieces))
    half = value.shape[1] // 2
    mine[...] = value[:, :half]
    theirs[...] = value[:, half:]


class Moves:
    def __init__(self):
        self.stories = lax.axis_size("story")
        self.chips = lax.axis_size("rec")
        self.cores = lax.axis_size("blk")
        assert self.cores == 2 and self.chips & (self.chips - 1) == 0
        self.s = lax.axis_index("story")
        self.r = lax.axis_index("rec")
        self.b = lax.axis_index("blk")

    def permute(self, value, target):
        pairs = []
        for s in range(self.stories):
            for r in range(self.chips):
                for b in range(self.cores):
                    t, q, c = target(s, r, b)
                    pairs.append(
                        (
                            (s * self.chips + r) * self.cores + b,
                            (t * self.chips + q) * self.cores + c,
                        )
                    )
        return lax.ppermute(value, AXES, pairs)

    def core(self, value):
        return self.permute(value, lambda s, r, b: (s, r, 1 - b))

    def chip(self, value, j):
        return self.permute(value, lambda s, r, b: (s, r ^ j, b))

    def story(self, value, parity, j):
        def target(s, r, b):
            t = s ^ 1 if parity == 0 else ((s - 1) ^ 1) + 1
            if t < 0 or t >= self.stories:
                return (s, r ^ 1, b) if self.chips > 1 else (s, r, 1 - b)
            return t, r ^ j, b

        return self.permute(value, target)

    def by_core(self, own, other, axis):
        first = jnp.where(self.b == 0, own, other)
        second = jnp.where(self.b == 0, other, own)
        return jnp.concatenate([first, second], axis=axis)

    def by_chip(self, pieces, axis=1):
        bit = 1
        while bit < self.chips:
            swap = (self.r & bit) != 0
            pieces = [jnp.where(swap, pieces[j ^ bit], pieces[j]) for j in range(self.chips)]
            bit *= 2
        return jnp.concatenate(pieces, axis=axis)

    def pieces(self, pieces):
        return pieces if pieces[0].shape[1] % 128 == 0 else [self.by_chip(pieces)]

    def gather_chips(self, value):
        return self.pieces([value] + [self.chip(value, j) for j in range(1, self.chips)])

    def gather_story(self, value, parity):
        return self.pieces([self.story(value, parity, j) for j in range(self.chips)])

    def half(self, value, which, axis=0):
        width = value.shape[axis] // 2
        return lax.dynamic_slice_in_dim(value, which * width, width, axis)

    def to_half(self, value):
        other = self.core(self.half(value, 1 - self.b))
        return self.by_core(self.half(value, self.b), other, 1)

    def from_half(self, value):
        other = self.core(self.half(value, 1 - self.b, 1))
        return self.by_core(self.half(value, self.b, 1), other, 0)


def shards(
    record_ids,
    ground_table,
    mass_int,
    mass_face,
    pattern_int,
    pattern_face,
    disp_int,
    vel_int,
    acc_int,
    disp_face,
    vel_face,
    acc_face,
    interior_inverse,
    couple_below,
    couple_above,
    lower,
    pivot,
    upper,
):
    mv = Moves()
    s, r, b = mv.s, mv.r, mv.b
    last = mv.stories - 1
    library = ground_table.shape[0]
    picked = record_ids[:, None] == jnp.arange(library, dtype=jnp.int32)[None, :]
    ground = jnp.sum(jnp.where(picked, ground_table[None, :], 0.0), axis=1)
    d_i, v_i, a_i = disp_int[0].T, vel_int[0].T, acc_int[0].T
    d_f, v_f, a_f = disp_face[0].T, vel_face[0].T, acc_face[0].T
    load_int = mass_int * (d_i + 2.0 * v_i + a_i - pattern_int * ground[:, None])
    load_face = mass_face * (d_f + 2.0 * v_f + a_f - pattern_face * ground[:, None])

    records = load_int.shape[0]
    half = records // 2
    rows_int, rows_face = 2 * load_int.shape[1], 2 * load_face.shape[1]
    faces = couple_above.shape[2]

    def chip_rows(matrix):
        own = matrix[0]
        return [own, mv.core(own)]

    across = [mv.chip(load_int, j) for j in range(1, mv.chips)]
    beside = [mv.core(piece) for piece in [load_int] + across]
    pieces = [piece for pair in zip([load_int] + across, beside) for piece in pair]
    aligned = load_int.shape[1] % 128 == 0
    if not aligned:
        pieces = [
            mv.by_chip([mv.by_core(pieces[2 * j], pieces[2 * j + 1], 1) for j in range(mv.chips)])
        ]
    mine, theirs = call(
        functools.partial(forces_kernel, aligned),
        [(2, half, faces)] * 2,
        [[interior_inverse[0]], [couple_above[0]], [couple_below[0]]],
        pieces,
    )
    chunks = call(
        chunks_kernel,
        [(half, faces // mv.chips)] * (2 * mv.chips),
        [],
        [mine, mv.core(theirs)],
    )
    above_force = chunks[0]
    for j in range(1, mv.chips):
        above_force = above_force + mv.chip(chunks[j], j)

    def from_above(parts, parity):
        total = mv.story(parts[0], parity, 0)
        for j in range(1, mv.chips):
            total = total + mv.story(parts[j], parity, j)
        return total

    condensed = mv.to_half(load_face) - above_force
    below_parts = chunks[mv.chips :]
    below_force = from_above(below_parts, 0)
    condensed = jnp.where((s % 2 == 0) & (s != last), condensed - below_force, condensed)
    condensed, *below_parts = lax.optimization_barrier([condensed, *below_parts])

    lower_rows, pivot_rows, upper_rows = chip_rows(lower), chip_rows(pivot), chip_rows(upper)
    shape = [(half, rows_face)]
    forward = condensed
    for k in range(1, mv.stories):
        came = mv.gather_story(forward, (k - 1) % 2)
        if k == 1:
            below_force = from_above(below_parts, 1)
            condensed = jnp.where((s % 2 == 1) & (s != last), condensed - below_force, condensed)
        (forward,) = call(
            functools.partial(step_kernel, k), shape, [lower_rows], came, [condensed, forward]
        )
    (pivoted,) = call(rows_kernel, shape, [pivot_rows], mv.gather_chips(forward))

    below_rows, above_rows = chip_rows(couple_below), chip_rows(couple_above)
    inverse_rows = chip_rows(interior_inverse)
    shape_int = [(half, rows_int)]
    face = pivoted
    for k in range(mv.stories - 2, -1, -1):
        came = mv.gather_story(face, k % 2)
        if k == 0:
            odd = mv.gather_story(face, 1)
            (early,) = call(rows_kernel, shape_int, [above_rows], mv.gather_chips(face))
            *came, early = lax.optimization_barrier([*came, early])
        (face,) = call(
            functools.partial(step_kernel, k), shape, [upper_rows], came, [pivoted, face]
        )

    even = mv.gather_story(face, 0)
    (reduced,) = call(
        coupled_kernel,
        shape_int,
        [above_rows, below_rows],
        [mv.to_half(load_int)],
        [early],
        mv.gather_chips(face),
        even,
        odd,
    )
    mine, theirs = call(
        last_kernel,
        [(half, rows_int // 2)] * 2,
        [inverse_rows],
        mv.gather_chips(reduced),
    )

    u_f = mv.from_half(face)
    u_i = mv.by_core(mine, mv.core(theirs), 0)
    new_a_i = u_i - d_i - 2.0 * v_i - a_i
    new_a_f = u_f - d_f - 2.0 * v_f - a_f
    new_v_i = v_i + a_i + new_a_i
    new_v_f = v_f + a_f + new_a_f
    return tuple(out.T[None] for out in (u_i, new_v_i, new_a_i, u_f, new_v_f, new_a_f))


def solution(mesh):
    whole, rows, cube = P(), P(("groups", "story"), ("rec", "blk")), P(("groups", "story"), ("rec", "blk"), None)
    in_specs = (P("groups"), whole) + (rows,) * 4 + (cube,) * 12
    return jax.shard_map(shards, mesh=mesh, in_specs=in_specs, out_specs=(cube,) * 6, check_vma=False)
```

```python
import functools

import jax
import jax.numpy as jnp
from jax import lax
from jax.experimental import pallas as pl
from jax.experimental.pallas import tpu as pltpu
from jax.sharding import PartitionSpec as P

AXES = ("story", "rec", "blk")
TILE = 256
VMEM = pl.BlockSpec(memory_space=pltpu.VMEM)


def split(value):
    high = value.astype(jnp.bfloat16)
    return high, (value - high.astype(jnp.float32)).astype(jnp.bfloat16)


def stacked(value):
    return jnp.concatenate(split(value), axis=0)


def matmul(left, right, over):
    rows = left.shape[0] // 2
    total = None
    for part in reversed(split(right)):
        both = lax.dot_general(
            left, part, (((1,), (over,)), ((), ())), preferred_element_type=jnp.float32
        )
        both = both[rows:] + both[:rows]
        total = both if total is None else total + both
    return total


def times_rows(left, *refs):
    left = stacked(left)
    count = refs[0].shape[0]
    ends = count * len(refs)
    columns = []
    for start in range(0, ends, TILE):
        stop = min(start + TILE, ends)
        blocks = []
        for i, ref in enumerate(refs):
            low, high = max(start - i * count, 0), min(stop - i * count, count)
            if low < high:
                blocks.append(ref[low:high, :])
        columns.append(matmul(left, jnp.concatenate(blocks, axis=0), 1))
    return jnp.concatenate(columns, axis=1)


def times(left, ref):
    left = stacked(left)
    width = ref.shape[1]
    columns = [matmul(left, ref[:, n : min(n + TILE, width)], 0) for n in range(0, width, TILE)]
    return jnp.concatenate(columns, axis=1)


def in_order(pieces, own):
    bit = 1
    while bit < len(pieces):
        swap = (own & bit) != 0
        pieces = [jnp.where(swap, pieces[j ^ bit], pieces[j]) for j in range(len(pieces))]
        bit *= 2
    return pieces


def joined(refs, axis="rec"):
    own = lax.axis_index(axis) if len(refs) > 1 else 0
    return jnp.concatenate(in_order([ref[...] for ref in refs], own), axis=1)


def store_rows(ref, value):
    half = value.shape[1] // 2
    swap = lax.axis_index("blk") == 1
    own, other = value[:, :half], value[:, half:]
    ref[...] = jnp.concatenate([jnp.where(swap, other, own), jnp.where(swap, own, other)], axis=1)


def call(kernel, shapes, *groups):
    flat = [value for group in groups for value in group]

    def body(*refs):
        at, parts = 0, []
        for group in groups:
            parts.append(refs[at : at + len(group)])
            at += len(group)
        kernel(*parts, *refs[at:])

    out = [jax.ShapeDtypeStruct(shape, jnp.float32) for shape in shapes]
    return pl.pallas_call(
        body,
        in_specs=[VMEM] * len(flat),
        out_specs=[VMEM] * len(out),
        out_shape=out,
        compiler_params=pltpu.CompilerParams(vmem_limit_bytes=24 << 20),
    )(*flat)


def staged(*matrices, after):
    held = lax.optimization_barrier([*matrices, *after])[: len(matrices)]

    def body(*refs):
        count = len(held)
        sems = refs[-1]
        copies = [
            pltpu.make_async_copy(refs[i], refs[count + i], sems.at[i]) for i in range(count)
        ]
        for copy in copies:
            copy.start()
        for copy in copies:
            copy.wait()

    return pl.pallas_call(
        body,
        in_specs=[pl.BlockSpec(memory_space=pltpu.HBM)] * len(held),
        out_specs=[VMEM] * len(held),
        out_shape=[pltpu.VMEM(matrix.shape, matrix.dtype) for matrix in held],
        scratch_shapes=[pltpu.SemaphoreType.DMA((len(held),))],
        compiler_params=pltpu.CompilerParams(vmem_limit_bytes=24 << 20),
    )(*held)


def forces_kernel(swap_chips, pieces, matrices, mine, theirs):
    inverse, above, below = matrices
    if swap_chips:
        chips = len(pieces) // 2
        core = lax.axis_index("blk")
        sets = [in_order([pieces[2 * j][...], pieces[2 * j + 1][...]], core) for j in range(chips)]
        sets = [jnp.concatenate(pair, axis=1) for pair in sets]
        full = jnp.concatenate(in_order(sets, lax.axis_index("rec")), axis=1)
    else:
        full = pieces[0][...]
    part = times_rows(full, inverse)
    half = part.shape[0] // 2
    second = lax.axis_index("blk") == 1
    for i, matrix in enumerate((above, below)):
        force = times(part, matrix)
        mine[i] = jnp.where(second, force[half:], force[:half])
        theirs[i] = jnp.where(second, force[:half], force[half:])


def chunks_kernel(inputs, *outs):
    mine, came = inputs
    chips = len(outs) // 2
    for i in range(2):
        total = mine[i] + came[i]
        width = total.shape[1] // chips
        pieces = [total[:, j * width : (j + 1) * width] for j in range(chips)]
        for j, piece in enumerate(in_order(pieces, lax.axis_index("rec"))):
            outs[i * chips + j][...] = piece


def step_kernel(story, pieces, rows, terms, out):
    first, latest = terms

    @pl.when(lax.axis_index("story") == story)
    def _():
        store_rows(out, times_rows(joined(pieces), *rows))
        out[...] = first[...] - out[...]

    @pl.when(lax.axis_index("story") != story)
    def _():
        out[...] = latest[...]


def rows_kernel(pieces, rows, out):
    store_rows(out, times_rows(joined(pieces), *rows))


def coupled_kernel(load, early, here, even, odd, above, below, out):
    story = lax.axis_index("story")

    @pl.when(story == 0)
    def _():
        store_rows(out, times_rows(joined(here), *above))
        out[...] = load[0][...] - out[...]

    @pl.when(story > 0)
    def _():
        use = lax.rem(story, 2) == 1
        refs = [jnp.where(use, e[...], o[...]) for e, o in zip(even, odd)]
        own = lax.axis_index("rec") if len(refs) > 1 else 0
        value = jnp.concatenate(in_order(refs, own), axis=1)
        store_rows(out, times_rows(value, *below))
        out[...] = load[0][...] - early[0][...] - out[...]


def last_kernel(pieces, rows, mine, theirs):
    value = times_rows(joined(pieces), *rows)
    half = value.shape[1] // 2
    mine[...] = value[:, :half]
    theirs[...] = value[:, half:]


class Moves:
    def __init__(self):
        self.stories = lax.axis_size("story")
        self.chips = lax.axis_size("rec")
        self.cores = lax.axis_size("blk")
        assert self.cores == 2 and self.chips & (self.chips - 1) == 0
        self.s = lax.axis_index("story")
        self.r = lax.axis_index("rec")
        self.b = lax.axis_index("blk")

    def permute(self, value, target):
        pairs = []
        for s in range(self.stories):
            for r in range(self.chips):
                for b in range(self.cores):
                    t, q, c = target(s, r, b)
                    pairs.append(
                        (
                            (s * self.chips + r) * self.cores + b,
                            (t * self.chips + q) * self.cores + c,
                        )
                    )
        return lax.ppermute(value, AXES, pairs)

    def core(self, value):
        return self.permute(value, lambda s, r, b: (s, r, 1 - b))

    def chip(self, value, j):
        return self.permute(value, lambda s, r, b: (s, r ^ j, b))

    def story(self, value, parity, j):
        def target(s, r, b):
            t = s ^ 1 if parity == 0 else ((s - 1) ^ 1) + 1
            if t < 0 or t >= self.stories:
                return (s, r ^ 1, b) if self.chips > 1 else (s, r, 1 - b)
            return t, r ^ j, b

        return self.permute(value, target)

    def by_core(self, own, other, axis):
        first = jnp.where(self.b == 0, own, other)
        second = jnp.where(self.b == 0, other, own)
        return jnp.concatenate([first, second], axis=axis)

    def by_chip(self, pieces, axis=1):
        bit = 1
        while bit < self.chips:
            swap = (self.r & bit) != 0
            pieces = [jnp.where(swap, pieces[j ^ bit], pieces[j]) for j in range(self.chips)]
            bit *= 2
        return jnp.concatenate(pieces, axis=axis)

    def pieces(self, pieces):
        return pieces if pieces[0].shape[1] % 128 == 0 else [self.by_chip(pieces)]

    def below(self, value, j):
        pairs = []
        for s in range(1, self.stories):
            for r in range(self.chips):
                for b in range(self.cores):
                    pairs.append(
                        (
                            (s * self.chips + r) * self.cores + b,
                            ((s - 1) * self.chips + (r ^ j)) * self.cores + b,
                        )
                    )
        return lax.ppermute(value, AXES, pairs)

    def gather_chips(self, value):
        return self.pieces([value] + [self.chip(value, j) for j in range(1, self.chips)])

    def gather_story(self, value, parity):
        return self.pieces([self.story(value, parity, j) for j in range(self.chips)])

    def half(self, value, which, axis=0):
        width = value.shape[axis] // 2
        return lax.dynamic_slice_in_dim(value, which * width, width, axis)

    def to_half(self, value):
        other = self.core(self.half(value, 1 - self.b))
        return self.by_core(self.half(value, self.b), other, 1)

    def from_half(self, value):
        other = self.core(self.half(value, 1 - self.b, 1))
        return self.by_core(self.half(value, self.b, 1), other, 0)


def shards(
    record_ids,
    ground_table,
    mass_int,
    mass_face,
    pattern_int,
    pattern_face,
    disp_int,
    vel_int,
    acc_int,
    disp_face,
    vel_face,
    acc_face,
    interior_inverse,
    couple_below,
    couple_above,
    lower,
    pivot,
    upper,
):
    mv = Moves()
    s, r, b = mv.s, mv.r, mv.b
    last = mv.stories - 1
    library = ground_table.shape[0]
    picked = record_ids[:, None] == jnp.arange(library, dtype=jnp.int32)[None, :]
    ground = jnp.sum(jnp.where(picked, ground_table[None, :], 0.0), axis=1)
    d_i, v_i, a_i = disp_int[0].T, vel_int[0].T, acc_int[0].T
    d_f, v_f, a_f = disp_face[0].T, vel_face[0].T, acc_face[0].T
    load_int = mass_int * (d_i + 2.0 * v_i + a_i - pattern_int * ground[:, None])
    load_face = mass_face * (d_f + 2.0 * v_f + a_f - pattern_face * ground[:, None])

    records = load_int.shape[0]
    half = records // 2
    rows_int, rows_face = 2 * load_int.shape[1], 2 * load_face.shape[1]
    faces = couple_above.shape[2]

    def others(matrix, after):
        return mv.core(lax.optimization_barrier([matrix, *after])[0])

    inverse_own, above_own, below_own = interior_inverse[0], couple_above[0], couple_below[0]
    lower_other = mv.core(lower[0])
    across = [mv.chip(load_int, j) for j in range(1, mv.chips)]
    inverse_own, above_own, below_own = staged(
        inverse_own, above_own, below_own, after=[load_int]
    )
    inverse_own, above_own, below_own, *across = lax.optimization_barrier(
        [inverse_own, above_own, below_own, *across]
    )
    beside = [mv.core(piece) for piece in [load_int] + across]
    pieces = [piece for pair in zip([load_int] + across, beside) for piece in pair]
    aligned = load_int.shape[1] % 128 == 0
    if not aligned:
        pieces = [
            mv.by_chip([mv.by_core(pieces[2 * j], pieces[2 * j + 1], 1) for j in range(mv.chips)])
        ]
    mine, theirs = call(
        functools.partial(forces_kernel, aligned),
        [(2, half, faces)] * 2,
        pieces,
        [inverse_own, above_own, below_own],
    )
    load_face_half, load_int_half = mv.to_half(load_face), mv.to_half(load_int)
    chunks = call(
        chunks_kernel,
        [(half, faces // mv.chips)] * (2 * mv.chips),
        [mine, mv.core(theirs)],
    )
    pivot_other = others(pivot[0], [chunks[0]])
    upper_other = others(upper[0], [chunks[0]])
    above_force = chunks[0]
    below_force = mv.below(chunks[mv.chips], 0)
    for j in range(1, mv.chips):
        above_force = above_force + mv.chip(chunks[j], j)
        below_force = below_force + mv.below(chunks[mv.chips + j], j)
    lower_rows = staged(lower[0], lower_other, after=[chunks[0]])
    condensed = load_face_half - above_force - below_force
    condensed, *lower_rows = lax.optimization_barrier([condensed, *lower_rows])

    shape = [(half, rows_face)]
    forward = condensed
    for k in range(1, mv.stories):
        came = mv.gather_story(forward, (k - 1) % 2)
        if k == 1:
            pivot_rows = staged(pivot[0], pivot_other, after=[forward])
            *came, p0, p1 = lax.optimization_barrier([*came, *pivot_rows])
            pivot_rows = [p0, p1]
            above_other = others(couple_above[0], [forward])
            below_other = others(couple_below[0], [forward])
            inverse_other = others(interior_inverse[0], [forward])
        if k == mv.stories - 1:
            upper_rows = staged(upper[0], upper_other, after=[forward])
            *came, u0, u1 = lax.optimization_barrier([*came, *upper_rows])
            upper_rows = [u0, u1]
        (forward,) = call(
            functools.partial(step_kernel, k), shape, came, lower_rows, [condensed, forward]
        )
    (pivoted,) = call(rows_kernel, shape, mv.gather_chips(forward), pivot_rows)

    shape_int = [(half, rows_int)]
    face = pivoted
    for k in range(mv.stories - 2, -1, -1):
        came = mv.gather_story(face, k % 2)
        if k == mv.stories - 2:
            (above_other,) = staged(above_other, after=[face])
            *came, above_other = lax.optimization_barrier([*came, above_other])
        if k == max(mv.stories - 3, 0):
            (below_other,) = staged(below_other, after=[face])
            *came, below_other = lax.optimization_barrier([*came, below_other])
        if k == 0:
            odd = mv.gather_story(face, 1)
            (early,) = call(
                rows_kernel, shape_int, mv.gather_chips(face), [above_own, above_other]
            )
            *came, early = lax.optimization_barrier([*came, early])
        (face,) = call(
            functools.partial(step_kernel, k), shape, came, upper_rows, [pivoted, face]
        )

    even = mv.gather_story(face, 0)
    (inverse_other,) = staged(inverse_other, after=[face])
    *even, inverse_other = lax.optimization_barrier([*even, inverse_other])
    (reduced,) = call(
        coupled_kernel,
        shape_int,
        [load_int_half],
        [early],
        mv.gather_chips(face),
        even,
        odd,
        [above_own, above_other],
        [below_own, below_other],
    )
    mine, theirs = call(
        last_kernel,
        [(half, rows_int // 2)] * 2,
        mv.gather_chips(reduced),
        [inverse_own, inverse_other],
    )

    u_f = mv.from_half(face)
    u_i = mv.by_core(mine, mv.core(theirs), 0)
    new_a_i = u_i - d_i - 2.0 * v_i - a_i
    new_a_f = u_f - d_f - 2.0 * v_f - a_f
    new_v_i = v_i + a_i + new_a_i
    new_v_f = v_f + a_f + new_a_f
    return tuple(out.T[None] for out in (u_i, new_v_i, new_a_i, u_f, new_v_f, new_a_f))


def solution(mesh):
    whole, rows, cube = P(), P(("groups", "story"), ("rec", "blk")), P(("groups", "story"), ("rec", "blk"), None)
    in_specs = (P("groups"), whole) + (rows,) * 4 + (cube,) * 12
    return jax.shard_map(shards, mesh=mesh, in_specs=in_specs, out_specs=(cube,) * 6, check_vma=False)
```

```python
import functools

import jax
import jax.numpy as jnp
from jax import lax
from jax.experimental import pallas as pl
from jax.experimental.pallas import tpu as pltpu
from jax.sharding import PartitionSpec as P

AXES = ("story", "rec", "blk")
TILE = 256
VMEM = pl.BlockSpec(memory_space=pltpu.VMEM)


def split(value):
    high = value.astype(jnp.bfloat16)
    return high, (value - high.astype(jnp.float32)).astype(jnp.bfloat16)


def stacked(value):
    return jnp.concatenate(split(value), axis=0)


def matmul(left, right, over):
    rows = left.shape[0] // 2
    total = None
    for part in reversed(split(right)):
        both = lax.dot_general(
            left, part, (((1,), (over,)), ((), ())), preferred_element_type=jnp.float32
        )
        both = both[rows:] + both[:rows]
        total = both if total is None else total + both
    return total


def times_rows(left, *refs):
    left = stacked(left)
    count = refs[0].shape[0]
    ends = count * len(refs)
    columns = []
    for start in range(0, ends, TILE):
        stop = min(start + TILE, ends)
        blocks = []
        for i, ref in enumerate(refs):
            low, high = max(start - i * count, 0), min(stop - i * count, count)
            if low < high:
                blocks.append(ref[low:high, :])
        columns.append(matmul(left, jnp.concatenate(blocks, axis=0), 1))
    return jnp.concatenate(columns, axis=1)


def times(left, ref):
    left = stacked(left)
    width = ref.shape[1]
    columns = [matmul(left, ref[:, n : min(n + TILE, width)], 0) for n in range(0, width, TILE)]
    return jnp.concatenate(columns, axis=1)


def in_order(pieces, own):
    bit = 1
    while bit < len(pieces):
        swap = (own & bit) != 0
        pieces = [jnp.where(swap, pieces[j ^ bit], pieces[j]) for j in range(len(pieces))]
        bit *= 2
    return pieces


def joined(refs, axis="rec"):
    own = lax.axis_index(axis) if len(refs) > 1 else 0
    return jnp.concatenate(in_order([ref[...] for ref in refs], own), axis=1)


def store_rows(ref, value):
    half = value.shape[1] // 2
    swap = lax.axis_index("blk") == 1
    own, other = value[:, :half], value[:, half:]
    ref[...] = jnp.concatenate([jnp.where(swap, other, own), jnp.where(swap, own, other)], axis=1)


def call(kernel, shapes, *groups, cost=0):
    flat = [value for group in groups for value in group]

    def body(*refs):
        at, parts = 0, []
        for group in groups:
            parts.append(refs[at : at + len(group)])
            at += len(group)
        kernel(*parts, *refs[at:])

    out = [jax.ShapeDtypeStruct(shape, jnp.float32) for shape in shapes]
    return pl.pallas_call(
        body,
        in_specs=[VMEM] * len(flat),
        out_specs=[VMEM] * len(out),
        out_shape=out,
        compiler_params=pltpu.CompilerParams(vmem_limit_bytes=24 << 20),
        cost_estimate=pl.CostEstimate(flops=0, bytes_accessed=cost, transcendentals=0) if cost else None,
    )(*flat)


def staged(*matrices, after):
    held = lax.optimization_barrier([*matrices, *after])[: len(matrices)]
    held = [pltpu.with_memory_space_constraint(matrix, pltpu.HBM) for matrix in held]
    count = len(held)
    rows = held[0].shape[0]
    ends = [0]
    for matrix in held:
        ends.append(ends[-1] + matrix.shape[1])

    def body(*refs):
        out, sems = refs[count:]
        copies = []
        for i in range(count):
            for j in range(2):
                part = pl.ds(j * (rows // 2), rows // 2)
                copies.append(
                    pltpu.make_async_copy(
                        refs[i].at[part, :],
                        out.at[part, ends[i] : ends[i + 1]],
                        sems.at[2 * i + j],
                    )
                )
        for copy in copies:
            copy.start()
        for copy in copies:
            copy.wait()

    return pl.pallas_call(
        body,
        in_specs=[pl.BlockSpec(memory_space=pltpu.HBM)] * count,
        out_specs=VMEM,
        out_shape=pltpu.VMEM((rows, ends[-1]), jnp.float32),
        scratch_shapes=[pltpu.SemaphoreType.DMA((2 * count,))],
        compiler_params=pltpu.CompilerParams(vmem_limit_bytes=24 << 20),
    )(*held)


def forces_kernel(swap_chips, pieces, matrices, mine, theirs):
    (rows,) = matrices
    faces = mine.shape[2]
    inner = rows.shape[1] - 2 * faces
    inverse = rows.at[:, :inner]
    above = rows.at[:, inner : inner + faces]
    below = rows.at[:, inner + faces :]
    if swap_chips:
        chips = len(pieces) // 2
        core = lax.axis_index("blk")
        sets = [in_order([pieces[2 * j][...], pieces[2 * j + 1][...]], core) for j in range(chips)]
        sets = [jnp.concatenate(pair, axis=1) for pair in sets]
        full = jnp.concatenate(in_order(sets, lax.axis_index("rec")), axis=1)
    else:
        full = pieces[0][...]
    part = times_rows(full, inverse)
    half = part.shape[0] // 2
    second = lax.axis_index("blk") == 1
    for i, matrix in enumerate((above, below)):
        force = times(part, matrix)
        mine[i] = jnp.where(second, force[half:], force[:half])
        theirs[i] = jnp.where(second, force[:half], force[half:])


def records_kernel(whole, mine, theirs):
    value = whole[0][...]
    half = value.shape[0] // 2
    second = lax.axis_index("blk") == 1
    mine[...] = jnp.where(second, value[half:], value[:half])
    theirs[...] = jnp.where(second, value[:half], value[half:])


def by_core(own, other, axis):
    second = lax.axis_index("blk") == 1
    return jnp.concatenate([jnp.where(second, other, own), jnp.where(second, own, other)], axis=axis)


def condensed_kernel(load, forces, out):
    value = by_core(load[0][...], load[1][...], 1)
    for force in forces:
        value = value - force[...]
    out[...] = value


def halves_kernel(whole, mine, theirs):
    value = whole[0][...]
    half = value.shape[1] // 2
    second = lax.axis_index("blk") == 1
    mine[...] = jnp.where(second, value[:, half:], value[:, :half])
    theirs[...] = jnp.where(second, value[:, :half], value[:, half:])


def outputs_kernel(halves, before, new_disp, new_vel, new_acc):
    disp, vel, acc = before
    value = by_core(halves[0][...], halves[1][...], 0)
    change = value - disp[...] - 2.0 * vel[...] - acc[...]
    new_disp[...] = value
    new_vel[...] = vel[...] + acc[...] + change
    new_acc[...] = change


def chunks_kernel(inputs, *outs):
    mine, came = inputs
    chips = len(outs) // 2
    for i in range(2):
        total = mine[i] + came[i]
        width = total.shape[1] // chips
        pieces = [total[:, j * width : (j + 1) * width] for j in range(chips)]
        for j, piece in enumerate(in_order(pieces, lax.axis_index("rec"))):
            outs[i * chips + j][...] = piece


def step_kernel(story, pieces, rows, terms, out):
    first, latest = terms

    @pl.when(lax.axis_index("story") == story)
    def _():
        store_rows(out, times_rows(joined(pieces), *rows))
        out[...] = first[...] - out[...]

    @pl.when(lax.axis_index("story") != story)
    def _():
        out[...] = latest[...]


def rows_kernel(pieces, rows, out):
    store_rows(out, times_rows(joined(pieces), *rows))


def coupled_kernel(load, early, here, even, odd, above, below, out):
    story = lax.axis_index("story")

    @pl.when(story == 0)
    def _():
        store_rows(out, times_rows(joined(here), *above))
        out[...] = by_core(load[0][...], load[1][...], 1) - out[...]

    @pl.when(story > 0)
    def _():
        use = lax.rem(story, 2) == 1
        refs = [jnp.where(use, e[...], o[...]) for e, o in zip(even, odd)]
        own = lax.axis_index("rec") if len(refs) > 1 else 0
        value = jnp.concatenate(in_order(refs, own), axis=1)
        store_rows(out, times_rows(value, *below))
        out[...] = by_core(load[0][...], load[1][...], 1) - early[0][...] - out[...]


def last_kernel(pieces, rows, mine, theirs):
    value = times_rows(joined(pieces), *rows)
    half = value.shape[1] // 2
    mine[...] = value[:, :half]
    theirs[...] = value[:, half:]


class Moves:
    def __init__(self):
        self.stories = lax.axis_size("story")
        self.chips = lax.axis_size("rec")
        self.cores = lax.axis_size("blk")
        assert self.cores == 2 and self.chips & (self.chips - 1) == 0
        self.s = lax.axis_index("story")
        self.r = lax.axis_index("rec")
        self.b = lax.axis_index("blk")

    def permute(self, value, target):
        pairs = []
        for s in range(self.stories):
            for r in range(self.chips):
                for b in range(self.cores):
                    t, q, c = target(s, r, b)
                    pairs.append(
                        (
                            (s * self.chips + r) * self.cores + b,
                            (t * self.chips + q) * self.cores + c,
                        )
                    )
        return lax.ppermute(value, AXES, pairs)

    def core(self, value):
        return self.permute(value, lambda s, r, b: (s, r, 1 - b))

    def chip(self, value, j):
        return self.permute(value, lambda s, r, b: (s, r ^ j, b))

    def story(self, value, parity, j):
        def target(s, r, b):
            t = s ^ 1 if parity == 0 else ((s - 1) ^ 1) + 1
            if t < 0 or t >= self.stories:
                return (s, r ^ 1, b) if self.chips > 1 else (s, r, 1 - b)
            return t, r ^ j, b

        return self.permute(value, target)

    def by_core(self, own, other, axis):
        first = jnp.where(self.b == 0, own, other)
        second = jnp.where(self.b == 0, other, own)
        return jnp.concatenate([first, second], axis=axis)

    def by_chip(self, pieces, axis=1):
        bit = 1
        while bit < self.chips:
            swap = (self.r & bit) != 0
            pieces = [jnp.where(swap, pieces[j ^ bit], pieces[j]) for j in range(self.chips)]
            bit *= 2
        return jnp.concatenate(pieces, axis=axis)

    def pieces(self, pieces):
        return pieces if pieces[0].shape[1] % 128 == 0 else [self.by_chip(pieces)]

    def below(self, value, j):
        pairs = []
        for s in range(1, self.stories):
            for r in range(self.chips):
                for b in range(self.cores):
                    pairs.append(
                        (
                            (s * self.chips + r) * self.cores + b,
                            ((s - 1) * self.chips + (r ^ j)) * self.cores + b,
                        )
                    )
        return lax.ppermute(value, AXES, pairs)

    def gather_chips(self, value):
        return self.pieces([value] + [self.chip(value, j) for j in range(1, self.chips)])

    def gather_story(self, value, parity):
        return self.pieces([self.story(value, parity, j) for j in range(self.chips)])


def shards(
    record_ids,
    ground_table,
    mass_int,
    mass_face,
    pattern_int,
    pattern_face,
    disp_int,
    vel_int,
    acc_int,
    disp_face,
    vel_face,
    acc_face,
    interior_inverse,
    couple_below,
    couple_above,
    lower,
    pivot,
    upper,
):
    mv = Moves()
    library, records = ground_table.shape[0], record_ids.shape[0]
    half = records // 2
    cube_int = [value[0].T for value in (disp_int, vel_int, acc_int)]
    cube_face = [value[0].T for value in (disp_face, vel_face, acc_face)]
    own_int, own_face = cube_int[0].shape[1], cube_face[0].shape[1]
    picked = record_ids[:, None] == jnp.arange(library, dtype=jnp.int32)[None, :]
    ground = jnp.sum(jnp.where(picked, ground_table[None, :], 0.0), axis=1)[:, None]

    def newmark_load(mass, pattern, values):
        disp, vel, acc = values
        return mass * (disp + 2.0 * vel + acc - pattern * ground)

    load_int = newmark_load(mass_int, pattern_int, cube_int)
    load_face = newmark_load(mass_face, pattern_face, cube_face)
    rows_int, rows_face = 2 * own_int, 2 * own_face
    faces = couple_above.shape[2]

    def others(matrix, after):
        return mv.core(lax.optimization_barrier([matrix, *after])[0])

    lower_other = mv.core(lower[0])
    across = [mv.chip(load_int, j) for j in range(1, mv.chips)]
    phase_rows = staged(
        interior_inverse[0], couple_above[0], couple_below[0], after=[load_int, load_face]
    )
    phase_rows, *across = lax.optimization_barrier([phase_rows, *across])
    beside = [mv.core(piece) for piece in [load_int] + across]
    pieces = [piece for pair in zip([load_int] + across, beside) for piece in pair]
    aligned = load_int.shape[1] % 128 == 0
    if not aligned:
        pieces = [
            mv.by_chip([mv.by_core(pieces[2 * j], pieces[2 * j + 1], 1) for j in range(mv.chips)])
        ]
    mine, theirs = call(
        functools.partial(forces_kernel, aligned), [(2, half, faces)] * 2, pieces, [phase_rows]
    )
    mine_face, theirs_face = call(records_kernel, [(half, own_face)] * 2, [load_face])
    mine_int, theirs_int = call(records_kernel, [(half, own_int)] * 2, [load_int])
    load_face_half = [mine_face, mv.core(theirs_face)]
    load_int_half = [mine_int, mv.core(theirs_int)]
    chunks = call(
        chunks_kernel,
        [(half, faces // mv.chips)] * (2 * mv.chips),
        [mine, mv.core(theirs)],
    )
    pivot_other = others(pivot[0], [chunks[0]])
    forces = [mv.below(chunks[mv.chips], 0)]
    for j in range(1, mv.chips):
        forces += [mv.chip(chunks[j], j), mv.below(chunks[mv.chips + j], j)]
    shape = [(half, rows_face)]
    (condensed,) = call(condensed_kernel, shape, load_face_half, [chunks[0]] + forces)

    forward = condensed
    for k in range(1, mv.stories):
        came = mv.gather_story(forward, (k - 1) % 2)
        if k == min(2, mv.stories - 1):
            *came, pivot_other = lax.optimization_barrier([*came, pivot_other])
            upper_other = others(upper[0], [forward])
        if k == mv.stories - 1:
            *came, upper_other = lax.optimization_barrier([*came, upper_other])
            above_other = others(couple_above[0], [forward])
        (forward,) = call(
            functools.partial(step_kernel, k),
            shape,
            came,
            [lower[0], lower_other],
            [condensed, forward],
        )
    came = mv.gather_chips(forward)
    below_other = others(couple_below[0], [forward])
    *came, above_other = lax.optimization_barrier([*came, above_other])
    (pivoted,) = call(rows_kernel, shape, came, [pivot[0], pivot_other])

    shape_int = [(half, rows_int)]
    face = pivoted
    for k in range(mv.stories - 2, -1, -1):
        came = mv.gather_story(face, k % 2)
        if k == mv.stories - 2:
            inverse_other = others(interior_inverse[0], [face])
            *came, below_other = lax.optimization_barrier([*came, below_other])
        if k == 0:
            odd = mv.gather_story(face, 1)
            (early,) = call(
                rows_kernel,
                shape_int,
                mv.gather_chips(face),
                [couple_above[0], above_other],
                cost=8 << 20,
            )
            *came, early, inverse_other = lax.optimization_barrier([*came, early, inverse_other])
        (face,) = call(
            functools.partial(step_kernel, k),
            shape,
            came,
            [upper[0], upper_other],
            [pivoted, face],
        )

    even = mv.gather_story(face, 0)
    (reduced,) = call(
        coupled_kernel,
        shape_int,
        load_int_half,
        [early],
        mv.gather_chips(face),
        even,
        odd,
        [couple_above[0], above_other],
        [couple_below[0], below_other],
    )
    mine, theirs = call(
        last_kernel,
        [(half, rows_int // 2)] * 2,
        mv.gather_chips(reduced),
        [interior_inverse[0], inverse_other],
    )

    new_int = call(
        outputs_kernel, [(records, own_int)] * 3, [mine, mv.core(theirs)], cube_int
    )
    mine, theirs = call(halves_kernel, [(half, own_face)] * 2, [face])
    new_face = call(
        outputs_kernel, [(records, own_face)] * 3, [mine, mv.core(theirs)], cube_face
    )
    return tuple(out.T[None] for out in (*new_int, *new_face))


def solution(mesh):
    whole, rows, cube = P(), P(("groups", "story"), ("rec", "blk")), P(("groups", "story"), ("rec", "blk"), None)
    in_specs = (P("groups"), whole) + (rows,) * 4 + (cube,) * 12
    return jax.shard_map(shards, mesh=mesh, in_specs=in_specs, out_specs=(cube,) * 6, check_vma=False)
```

```python
import functools

import jax
import jax.numpy as jnp
from jax import lax
from jax.experimental import pallas as pl
from jax.experimental.pallas import tpu as pltpu
from jax.sharding import PartitionSpec as P

AXES = ("story", "rec", "blk")
TILE = 256
VMEM = pl.BlockSpec(memory_space=pltpu.VMEM)


def split(value):
    high = value.astype(jnp.bfloat16)
    return high, (value - high.astype(jnp.float32)).astype(jnp.bfloat16)


def stacked(value):
    return jnp.concatenate(split(value), axis=0)


def matmul(left, right, over):
    rows = left.shape[0] // 2
    total = None
    for part in reversed(split(right)):
        both = lax.dot_general(
            left, part, (((1,), (over,)), ((), ())), preferred_element_type=jnp.float32
        )
        both = both[rows:] + both[:rows]
        total = both if total is None else total + both
    return total


def times_rows(left, *refs):
    left = stacked(left)
    count = refs[0].shape[0]
    ends = count * len(refs)
    columns = []
    for start in range(0, ends, TILE):
        stop = min(start + TILE, ends)
        blocks = []
        for i, ref in enumerate(refs):
            low, high = max(start - i * count, 0), min(stop - i * count, count)
            if low < high:
                blocks.append(ref[low:high, :])
        columns.append(matmul(left, jnp.concatenate(blocks, axis=0), 1))
    return jnp.concatenate(columns, axis=1)


def times(left, ref):
    left = stacked(left)
    width = ref.shape[1]
    columns = [matmul(left, ref[:, n : min(n + TILE, width)], 0) for n in range(0, width, TILE)]
    return jnp.concatenate(columns, axis=1)


def in_order(pieces, own):
    bit = 1
    while bit < len(pieces):
        swap = (own & bit) != 0
        pieces = [jnp.where(swap, pieces[j ^ bit], pieces[j]) for j in range(len(pieces))]
        bit *= 2
    return pieces


def joined(refs, axis="rec"):
    own = lax.axis_index(axis) if len(refs) > 1 else 0
    return jnp.concatenate(in_order([ref[...] for ref in refs], own), axis=1)


def store_rows(ref, value):
    half = value.shape[1] // 2
    swap = lax.axis_index("blk") == 1
    own, other = value[:, :half], value[:, half:]
    ref[...] = jnp.concatenate([jnp.where(swap, other, own), jnp.where(swap, own, other)], axis=1)


def call(kernel, shapes, *groups, cost=0):
    flat = [value for group in groups for value in group]

    def body(*refs):
        at, parts = 0, []
        for group in groups:
            parts.append(refs[at : at + len(group)])
            at += len(group)
        kernel(*parts, *refs[at:])

    out = [jax.ShapeDtypeStruct(shape, jnp.float32) for shape in shapes]
    return pl.pallas_call(
        body,
        in_specs=[VMEM] * len(flat),
        out_specs=[VMEM] * len(out),
        out_shape=out,
        compiler_params=pltpu.CompilerParams(vmem_limit_bytes=24 << 20),
        cost_estimate=pl.CostEstimate(flops=0, bytes_accessed=cost, transcendentals=0) if cost else None,
    )(*flat)


def staged(*matrices, after):
    held = lax.optimization_barrier([*matrices, *after])[: len(matrices)]
    held = [pltpu.with_memory_space_constraint(matrix, pltpu.HBM) for matrix in held]
    count = len(held)
    rows = held[0].shape[0]
    ends = [0]
    for matrix in held:
        ends.append(ends[-1] + matrix.shape[1])

    def body(*refs):
        out, sems = refs[count:]
        copies = []
        for i in range(count):
            for j in range(2):
                part = pl.ds(j * (rows // 2), rows // 2)
                copies.append(
                    pltpu.make_async_copy(
                        refs[i].at[part, :],
                        out.at[part, ends[i] : ends[i + 1]],
                        sems.at[2 * i + j],
                    )
                )
        for copy in copies:
            copy.start()
        for copy in copies:
            copy.wait()

    return pl.pallas_call(
        body,
        in_specs=[pl.BlockSpec(memory_space=pltpu.HBM)] * count,
        out_specs=VMEM,
        out_shape=pltpu.VMEM((rows, ends[-1]), jnp.float32),
        scratch_shapes=[pltpu.SemaphoreType.DMA((2 * count,))],
        compiler_params=pltpu.CompilerParams(vmem_limit_bytes=24 << 20),
    )(*held)


def forces_kernel(swap_chips, pieces, matrices, mine, theirs):
    (rows,) = matrices
    faces = mine.shape[2]
    inner = rows.shape[1] - 2 * faces
    inverse = rows.at[:, :inner]
    above = rows.at[:, inner : inner + faces]
    below = rows.at[:, inner + faces :]
    if swap_chips:
        chips = len(pieces) // 2
        core = lax.axis_index("blk")
        sets = [in_order([pieces[2 * j][...], pieces[2 * j + 1][...]], core) for j in range(chips)]
        sets = [jnp.concatenate(pair, axis=1) for pair in sets]
        full = jnp.concatenate(in_order(sets, lax.axis_index("rec")), axis=1)
    else:
        full = pieces[0][...]
    part = times_rows(full, inverse)
    half = part.shape[0] // 2
    second = lax.axis_index("blk") == 1
    for i, matrix in enumerate((above, below)):
        force = times(part, matrix)
        mine[i] = jnp.where(second, force[half:], force[:half])
        theirs[i] = jnp.where(second, force[:half], force[half:])


def fetched(kernel, shapes, arrays, *held):
    count = len(arrays)
    arrays = [pltpu.with_memory_space_constraint(value, pltpu.HBM) for value in arrays]

    def body(*refs):
        sources, rest = refs[:count], refs[count:-1]
        buffers, sems = rest[len(held) + len(shapes) :], refs[-1]
        copies = [
            pltpu.make_async_copy(source, buffer, sems.at[i])
            for i, (source, buffer) in enumerate(zip(sources, buffers))
        ]
        for copy in copies:
            copy.start()
        for copy in copies:
            copy.wait()
        kernel(buffers, rest[: len(held)], *rest[len(held) : len(held) + len(shapes)])

    out = [jax.ShapeDtypeStruct(shape, jnp.float32) for shape in shapes]
    return pl.pallas_call(
        body,
        in_specs=[pl.BlockSpec(memory_space=pltpu.HBM)] * count + [VMEM] * len(held),
        out_specs=[VMEM] * len(out),
        out_shape=out,
        scratch_shapes=[pltpu.VMEM(value.shape, value.dtype) for value in arrays]
        + [pltpu.SemaphoreType.DMA((count,))],
        compiler_params=pltpu.CompilerParams(vmem_limit_bytes=24 << 20),
    )(*arrays, *held)


def newmark_load(mass, pattern, disp, vel, acc, ground):
    return mass[...] * (disp[...] + 2.0 * vel[...] + acc[...] - pattern[...] * ground)


def load_int_kernel(fetched_refs, held, load, ground_out):
    ids, table, *arrays = fetched_refs
    records, library = ids.shape[1], table.shape[1]
    shape = (records, records)
    diagonal = lax.broadcasted_iota(jnp.int32, shape, 0) == lax.broadcasted_iota(jnp.int32, shape, 1)
    row = jnp.broadcast_to(ids[...].astype(jnp.float32), shape)
    column = jnp.sum(jnp.where(diagonal, row, 0.0), axis=1, keepdims=True)
    index = lax.broadcasted_iota(jnp.int32, (records, library), 1).astype(jnp.float32)
    ground = jnp.sum(jnp.where(column == index, table[...], 0.0), axis=1, keepdims=True)
    ground_out[...] = jnp.broadcast_to(ground, ground_out.shape)
    load[...] = newmark_load(*arrays, ground)


def load_face_kernel(fetched_refs, held, mine, theirs):
    load = newmark_load(*fetched_refs, held[0][:, :1])
    half = load.shape[0] // 2
    second = lax.axis_index("blk") == 1
    mine[...] = jnp.where(second, load[half:], load[:half])
    theirs[...] = jnp.where(second, load[:half], load[half:])


def records_kernel(whole, mine, theirs):
    value = whole[0][...]
    half = value.shape[0] // 2
    second = lax.axis_index("blk") == 1
    mine[...] = jnp.where(second, value[half:], value[:half])
    theirs[...] = jnp.where(second, value[:half], value[half:])


def by_core(own, other, axis):
    second = lax.axis_index("blk") == 1
    return jnp.concatenate([jnp.where(second, other, own), jnp.where(second, own, other)], axis=axis)


def condensed_kernel(load, forces, out):
    value = by_core(load[0][...], load[1][...], 1)
    for force in forces:
        value = value - force[...]
    out[...] = value


def halves_kernel(whole, mine, theirs):
    value = whole[0][...]
    half = value.shape[1] // 2
    second = lax.axis_index("blk") == 1
    mine[...] = jnp.where(second, value[:, half:], value[:, :half])
    theirs[...] = jnp.where(second, value[:, :half], value[:, half:])


def outputs_kernel(halves, before, new_disp, new_vel, new_acc):
    disp, vel, acc = before
    value = by_core(halves[0][...], halves[1][...], 0)
    change = value - disp[...] - 2.0 * vel[...] - acc[...]
    new_disp[...] = value
    new_vel[...] = vel[...] + acc[...] + change
    new_acc[...] = change


def chunks_kernel(inputs, *outs):
    mine, came = inputs
    chips = len(outs) // 2
    for i in range(2):
        total = mine[i] + came[i]
        width = total.shape[1] // chips
        pieces = [total[:, j * width : (j + 1) * width] for j in range(chips)]
        for j, piece in enumerate(in_order(pieces, lax.axis_index("rec"))):
            outs[i * chips + j][...] = piece


def step_kernel(story, pieces, rows, terms, out):
    first, latest = terms

    @pl.when(lax.axis_index("story") == story)
    def _():
        store_rows(out, times_rows(joined(pieces), *rows))
        out[...] = first[...] - out[...]

    @pl.when(lax.axis_index("story") != story)
    def _():
        out[...] = latest[...]


def rows_kernel(pieces, rows, out):
    store_rows(out, times_rows(joined(pieces), *rows))


def coupled_kernel(load, early, here, even, odd, above, below, out):
    story = lax.axis_index("story")

    @pl.when(story == 0)
    def _():
        store_rows(out, times_rows(joined(here), *above))
        out[...] = by_core(load[0][...], load[1][...], 1) - out[...]

    @pl.when(story > 0)
    def _():
        use = lax.rem(story, 2) == 1
        refs = [jnp.where(use, e[...], o[...]) for e, o in zip(even, odd)]
        own = lax.axis_index("rec") if len(refs) > 1 else 0
        value = jnp.concatenate(in_order(refs, own), axis=1)
        store_rows(out, times_rows(value, *below))
        out[...] = by_core(load[0][...], load[1][...], 1) - early[0][...] - out[...]


def last_kernel(pieces, rows, mine, theirs):
    value = times_rows(joined(pieces), *rows)
    half = value.shape[1] // 2
    mine[...] = value[:, :half]
    theirs[...] = value[:, half:]


class Moves:
    def __init__(self):
        self.stories = lax.axis_size("story")
        self.chips = lax.axis_size("rec")
        self.cores = lax.axis_size("blk")
        assert self.cores == 2 and self.chips & (self.chips - 1) == 0
        self.s = lax.axis_index("story")
        self.r = lax.axis_index("rec")
        self.b = lax.axis_index("blk")

    def permute(self, value, target):
        pairs = []
        for s in range(self.stories):
            for r in range(self.chips):
                for b in range(self.cores):
                    t, q, c = target(s, r, b)
                    pairs.append(
                        (
                            (s * self.chips + r) * self.cores + b,
                            (t * self.chips + q) * self.cores + c,
                        )
                    )
        return lax.ppermute(value, AXES, pairs)

    def core(self, value):
        return self.permute(value, lambda s, r, b: (s, r, 1 - b))

    def chip(self, value, j):
        return self.permute(value, lambda s, r, b: (s, r ^ j, b))

    def story(self, value, parity, j):
        def target(s, r, b):
            t = s ^ 1 if parity == 0 else ((s - 1) ^ 1) + 1
            if t < 0 or t >= self.stories:
                return (s, r ^ 1, b) if self.chips > 1 else (s, r, 1 - b)
            return t, r ^ j, b

        return self.permute(value, target)

    def by_core(self, own, other, axis):
        first = jnp.where(self.b == 0, own, other)
        second = jnp.where(self.b == 0, other, own)
        return jnp.concatenate([first, second], axis=axis)

    def by_chip(self, pieces, axis=1):
        bit = 1
        while bit < self.chips:
            swap = (self.r & bit) != 0
            pieces = [jnp.where(swap, pieces[j ^ bit], pieces[j]) for j in range(self.chips)]
            bit *= 2
        return jnp.concatenate(pieces, axis=axis)

    def pieces(self, pieces):
        return pieces if pieces[0].shape[1] % 128 == 0 else [self.by_chip(pieces)]

    def below(self, value, j):
        pairs = []
        for s in range(1, self.stories):
            for r in range(self.chips):
                for b in range(self.cores):
                    pairs.append(
                        (
                            (s * self.chips + r) * self.cores + b,
                            ((s - 1) * self.chips + (r ^ j)) * self.cores + b,
                        )
                    )
        return lax.ppermute(value, AXES, pairs)

    def gather_chips(self, value):
        return self.pieces([value] + [self.chip(value, j) for j in range(1, self.chips)])

    def gather_story(self, value, parity):
        return self.pieces([self.story(value, parity, j) for j in range(self.chips)])


def shards(
    record_ids,
    ground_table,
    mass_int,
    mass_face,
    pattern_int,
    pattern_face,
    disp_int,
    vel_int,
    acc_int,
    disp_face,
    vel_face,
    acc_face,
    interior_inverse,
    couple_below,
    couple_above,
    lower,
    pivot,
    upper,
):
    mv = Moves()
    library, records = ground_table.shape[0], record_ids.shape[0]
    half = records // 2
    cube_int = [value[0].T for value in (disp_int, vel_int, acc_int)]
    cube_face = [value[0].T for value in (disp_face, vel_face, acc_face)]
    own_int, own_face = cube_int[0].shape[1], cube_face[0].shape[1]
    load_int, ground = fetched(
        load_int_kernel,
        [(records, own_int), (records, 128)],
        [record_ids.reshape(1, records), ground_table.reshape(1, library), mass_int, pattern_int]
        + cube_int,
    )
    mine_face, theirs_face = fetched(
        load_face_kernel, [(half, own_face)] * 2, [mass_face, pattern_face] + cube_face, ground
    )
    rows_int, rows_face = 2 * own_int, 2 * own_face
    faces = couple_above.shape[2]

    def others(matrix, after):
        return mv.core(lax.optimization_barrier([matrix, *after])[0])

    lower_other = mv.core(lower[0])
    across = [mv.chip(load_int, j) for j in range(1, mv.chips)]
    load_face_half = [mine_face, mv.core(theirs_face)]
    phase_rows = staged(
        interior_inverse[0], couple_above[0], couple_below[0], after=[theirs_face]
    )
    phase_rows, load_face_half[1], *across = lax.optimization_barrier(
        [phase_rows, load_face_half[1], *across]
    )
    beside = [mv.core(piece) for piece in [load_int] + across]
    pieces = [piece for pair in zip([load_int] + across, beside) for piece in pair]
    aligned = load_int.shape[1] % 128 == 0
    if not aligned:
        pieces = [
            mv.by_chip([mv.by_core(pieces[2 * j], pieces[2 * j + 1], 1) for j in range(mv.chips)])
        ]
    mine, theirs = call(
        functools.partial(forces_kernel, aligned), [(2, half, faces)] * 2, pieces, [phase_rows]
    )
    mine_int, theirs_int = call(records_kernel, [(half, own_int)] * 2, [load_int])
    load_int_half = [mine_int, mv.core(theirs_int)]
    chunks = call(
        chunks_kernel,
        [(half, faces // mv.chips)] * (2 * mv.chips),
        [mine, mv.core(theirs)],
    )
    forces = [mv.below(chunks[mv.chips], 0)]
    for j in range(1, mv.chips):
        forces += [mv.chip(chunks[j], j), mv.below(chunks[mv.chips + j], j)]
    shape = [(half, rows_face)]
    (condensed,) = call(condensed_kernel, shape, load_face_half, [chunks[0]] + forces)

    forward = condensed
    pivot_other = others(pivot[0], [condensed])
    for k in range(1, mv.stories):
        came = mv.gather_story(forward, (k - 1) % 2)
        if k == min(2, mv.stories - 1):
            *came, pivot_other = lax.optimization_barrier([*came, pivot_other])
            upper_other = others(upper[0], [forward])
        if k == mv.stories - 1:
            *came, upper_other = lax.optimization_barrier([*came, upper_other])
            above_other = others(couple_above[0], [upper_other])
        (forward,) = call(
            functools.partial(step_kernel, k),
            shape,
            came,
            [lower[0], lower_other],
            [condensed, forward],
        )
    (pivoted,) = call(rows_kernel, shape, mv.gather_chips(forward), [pivot[0], pivot_other])

    shape_int = [(half, rows_int)]
    face = pivoted
    for k in range(mv.stories - 2, -1, -1):
        came = mv.gather_story(face, k % 2)
        if k == mv.stories - 2:
            *came, above_other = lax.optimization_barrier([*came, above_other])
            below_other = others(couple_below[0], [above_other])
        if k == max(mv.stories - 3, 0):
            *came, below_other = lax.optimization_barrier([*came, below_other])
            inverse_other = others(interior_inverse[0], [below_other])
        if k == 0:
            odd = mv.gather_story(face, 1)
            (early,) = call(
                rows_kernel,
                shape_int,
                mv.gather_chips(face),
                [couple_above[0], above_other],
                cost=8 << 20,
            )
            *came, early = lax.optimization_barrier([*came, early])
        (face,) = call(
            functools.partial(step_kernel, k),
            shape,
            came,
            [upper[0], upper_other],
            [pivoted, face],
        )

    even = mv.gather_story(face, 0)
    *even, inverse_other = lax.optimization_barrier([*even, inverse_other])
    (reduced,) = call(
        coupled_kernel,
        shape_int,
        load_int_half,
        [early],
        mv.gather_chips(face),
        even,
        odd,
        [couple_above[0], above_other],
        [couple_below[0], below_other],
    )
    mine, theirs = call(halves_kernel, [(half, own_face)] * 2, [face])
    new_face = call(
        outputs_kernel, [(records, own_face)] * 3, [mine, mv.core(theirs)], cube_face
    )
    came = mv.gather_chips(reduced)
    *came, f0, f1, f2 = lax.optimization_barrier([*came, *new_face])
    mine, theirs = call(
        last_kernel, [(half, own_int)] * 2, came, [interior_inverse[0], inverse_other]
    )
    new_int = call(
        outputs_kernel, [(records, own_int)] * 3, [mine, mv.core(theirs)], cube_int
    )
    new_face = [f0, f1, f2]
    return tuple(out.T[None] for out in (*new_int, *new_face))


def solution(mesh):
    whole, rows, cube = P(), P(("groups", "story"), ("rec", "blk")), P(("groups", "story"), ("rec", "blk"), None)
    in_specs = (P("groups"), whole) + (rows,) * 4 + (cube,) * 12
    return jax.shard_map(shards, mesh=mesh, in_specs=in_specs, out_specs=(cube,) * 6, check_vma=False)
```

```python
import functools

import jax
import jax.numpy as jnp
from jax import lax
from jax.experimental import pallas as pl
from jax.experimental.pallas import tpu as pltpu
from jax.sharding import PartitionSpec as P

AXES = ("story", "rec", "blk")
TILE = 256
VMEM = pl.BlockSpec(memory_space=pltpu.VMEM)


def split(value):
    high = value.astype(jnp.bfloat16)
    return high, (value - high.astype(jnp.float32)).astype(jnp.bfloat16)


def stacked(value):
    return jnp.concatenate(split(value), axis=0)


def matmul(left, right, over):
    rows = left.shape[0] // 2
    total = None
    for part in reversed(split(right)):
        both = lax.dot_general(
            left, part, (((1,), (over,)), ((), ())), preferred_element_type=jnp.float32
        )
        both = both[rows:] + both[:rows]
        total = both if total is None else total + both
    return total


def times_rows(left, *refs, columns=slice(None)):
    left = stacked(left)
    count = refs[0].shape[0]
    ends = count * len(refs)
    results = []
    for start in range(0, ends, TILE):
        stop = min(start + TILE, ends)
        blocks = []
        for i, ref in enumerate(refs):
            low, high = max(start - i * count, 0), min(stop - i * count, count)
            if low < high:
                blocks.append(ref[low:high, columns])
        results.append(matmul(left, jnp.concatenate(blocks, axis=0), 1))
    return jnp.concatenate(results, axis=1)


def times(left, ref):
    left = stacked(left)
    width = ref.shape[1]
    columns = [matmul(left, ref[:, n : min(n + TILE, width)], 0) for n in range(0, width, TILE)]
    return jnp.concatenate(columns, axis=1)


def in_order(pieces, own):
    bit = 1
    while bit < len(pieces):
        swap = (own & bit) != 0
        pieces = [jnp.where(swap, pieces[j ^ bit], pieces[j]) for j in range(len(pieces))]
        bit *= 2
    return pieces


def joined(refs, axis="rec"):
    own = lax.axis_index(axis) if len(refs) > 1 else 0
    return jnp.concatenate(in_order([ref[...] for ref in refs], own), axis=1)


def store_rows(ref, value):
    half = value.shape[1] // 2
    swap = lax.axis_index("blk") == 1
    own, other = value[:, :half], value[:, half:]
    ref[...] = jnp.concatenate([jnp.where(swap, other, own), jnp.where(swap, own, other)], axis=1)


def call(kernel, shapes, *groups, cost=0):
    flat = [value for group in groups for value in group]

    def body(*refs):
        at, parts = 0, []
        for group in groups:
            parts.append(refs[at : at + len(group)])
            at += len(group)
        kernel(*parts, *refs[at:])

    out = [jax.ShapeDtypeStruct(shape, jnp.float32) for shape in shapes]
    return pl.pallas_call(
        body,
        in_specs=[VMEM] * len(flat),
        out_specs=[VMEM] * len(out),
        out_shape=out,
        compiler_params=pltpu.CompilerParams(vmem_limit_bytes=24 << 20),
        cost_estimate=pl.CostEstimate(flops=0, bytes_accessed=cost, transcendentals=0) if cost else None,
    )(*flat)


def staged(*matrices, after):
    held = lax.optimization_barrier([*matrices, *after])[: len(matrices)]
    held = [pltpu.with_memory_space_constraint(matrix, pltpu.HBM) for matrix in held]
    count = len(held)
    rows = held[0].shape[0]
    ends = [0]
    for matrix in held:
        ends.append(ends[-1] + matrix.shape[1])

    def body(*refs):
        out, sems = refs[count:]
        copies = []
        for i in range(count):
            for j in range(2):
                part = pl.ds(j * (rows // 2), rows // 2)
                copies.append(
                    pltpu.make_async_copy(
                        refs[i].at[part, :],
                        out.at[part, ends[i] : ends[i + 1]],
                        sems.at[2 * i + j],
                    )
                )
        for copy in copies:
            copy.start()
        for copy in copies:
            copy.wait()

    return pl.pallas_call(
        body,
        in_specs=[pl.BlockSpec(memory_space=pltpu.HBM)] * count,
        out_specs=VMEM,
        out_shape=pltpu.VMEM((rows, ends[-1]), jnp.float32),
        scratch_shapes=[pltpu.SemaphoreType.DMA((2 * count,))],
        compiler_params=pltpu.CompilerParams(vmem_limit_bytes=24 << 20),
    )(*held)


def forces_kernel(swap_chips, pieces, matrices, mine, theirs):
    (rows,) = matrices
    faces = mine.shape[2]
    inner = rows.shape[1] - 2 * faces
    inverse = rows.at[:, :inner]
    above = rows.at[:, inner : inner + faces]
    below = rows.at[:, inner + faces :]
    if swap_chips:
        chips = len(pieces) // 2
        core = lax.axis_index("blk")
        sets = [in_order([pieces[2 * j][...], pieces[2 * j + 1][...]], core) for j in range(chips)]
        sets = [jnp.concatenate(pair, axis=1) for pair in sets]
        full = jnp.concatenate(in_order(sets, lax.axis_index("rec")), axis=1)
    else:
        full = pieces[0][...]
    part = times_rows(full, inverse)
    half = part.shape[0] // 2
    second = lax.axis_index("blk") == 1
    for i, matrix in enumerate((above, below)):
        force = times(part, matrix)
        mine[i] = jnp.where(second, force[half:], force[:half])
        theirs[i] = jnp.where(second, force[:half], force[half:])


def fetched(kernel, shapes, arrays, *held):
    count = len(arrays)
    arrays = [pltpu.with_memory_space_constraint(value, pltpu.HBM) for value in arrays]

    def body(*refs):
        sources, rest = refs[:count], refs[count:-1]
        buffers, sems = rest[len(held) + len(shapes) :], refs[-1]
        copies = [
            pltpu.make_async_copy(source, buffer, sems.at[i])
            for i, (source, buffer) in enumerate(zip(sources, buffers))
        ]
        for copy in copies:
            copy.start()
        for copy in copies:
            copy.wait()
        kernel(buffers, rest[: len(held)], *rest[len(held) : len(held) + len(shapes)])

    out = [jax.ShapeDtypeStruct(shape, jnp.float32) for shape in shapes]
    return pl.pallas_call(
        body,
        in_specs=[pl.BlockSpec(memory_space=pltpu.HBM)] * count + [VMEM] * len(held),
        out_specs=[VMEM] * len(out),
        out_shape=out,
        scratch_shapes=[pltpu.VMEM(value.shape, value.dtype) for value in arrays]
        + [pltpu.SemaphoreType.DMA((count,))],
        compiler_params=pltpu.CompilerParams(vmem_limit_bytes=24 << 20),
    )(*arrays, *held)


def newmark_load(mass, pattern, disp, vel, acc, ground):
    return mass[...] * (disp[...] + 2.0 * vel[...] + acc[...] - pattern[...] * ground)


def load_int_kernel(fetched_refs, held, load, ground_out):
    ids, table, *arrays = fetched_refs
    records, library = ids.shape[1], table.shape[1]
    shape = (records, records)
    diagonal = lax.broadcasted_iota(jnp.int32, shape, 0) == lax.broadcasted_iota(jnp.int32, shape, 1)
    row = jnp.broadcast_to(ids[...].astype(jnp.float32), shape)
    column = jnp.sum(jnp.where(diagonal, row, 0.0), axis=1, keepdims=True)
    index = lax.broadcasted_iota(jnp.int32, (records, library), 1).astype(jnp.float32)
    ground = jnp.sum(jnp.where(column == index, table[...], 0.0), axis=1, keepdims=True)
    ground_out[...] = jnp.broadcast_to(ground, ground_out.shape)
    load[...] = newmark_load(*arrays, ground)


def load_face_kernel(fetched_refs, held, mine, theirs):
    load = newmark_load(*fetched_refs, held[0][:, :1])
    half = load.shape[0] // 2
    second = lax.axis_index("blk") == 1
    mine[...] = jnp.where(second, load[half:], load[:half])
    theirs[...] = jnp.where(second, load[:half], load[half:])


def records_kernel(whole, mine, theirs):
    value = whole[0][...]
    half = value.shape[0] // 2
    second = lax.axis_index("blk") == 1
    mine[...] = jnp.where(second, value[half:], value[:half])
    theirs[...] = jnp.where(second, value[:half], value[half:])


def by_core(own, other, axis):
    second = lax.axis_index("blk") == 1
    return jnp.concatenate([jnp.where(second, other, own), jnp.where(second, own, other)], axis=axis)


def condensed_kernel(load, forces, out):
    value = by_core(load[0][...], load[1][...], 1)
    for force in forces:
        value = value - force[...]
    out[...] = value


def halves_kernel(whole, mine, theirs):
    value = whole[0][...]
    half = value.shape[1] // 2
    second = lax.axis_index("blk") == 1
    mine[...] = jnp.where(second, value[:, half:], value[:, :half])
    theirs[...] = jnp.where(second, value[:, :half], value[:, half:])


def outputs_kernel(halves, before, new_disp, new_vel, new_acc):
    disp, vel, acc = before
    value = by_core(halves[0][...], halves[1][...], 0)
    change = value - disp[...] - 2.0 * vel[...] - acc[...]
    new_disp[...] = value
    new_vel[...] = vel[...] + acc[...] + change
    new_acc[...] = change


def chunks_kernel(inputs, *outs):
    mine, came = inputs
    chips = len(outs) // 2
    for i in range(2):
        total = mine[i] + came[i]
        width = total.shape[1] // chips
        pieces = [total[:, j * width : (j + 1) * width] for j in range(chips)]
        for j, piece in enumerate(in_order(pieces, lax.axis_index("rec"))):
            outs[i * chips + j][...] = piece


def from_chip(count, j):
    def columns(width):
        if count == 1:
            return slice(None)
        start = (lax.axis_index("rec") ^ j) * width
        return pl.ds(pl.multiple_of(start, 128), width)

    return columns


def plus(value, sofar):
    return value + sofar[0][...] if sofar else value


def part_kernel(columns, story, piece, rows, sofar, out):
    def product():
        value = piece[0][...]
        out[...] = plus(times_rows(value, *rows, columns=columns(value.shape[1])), sofar)

    if story is None:
        product()
    else:
        pl.when(lax.axis_index("story") == story)(product)


def step_kernel(columns, story, piece, rows, sofar, terms, out):
    first, latest = terms

    @pl.when(lax.axis_index("story") == story)
    def _():
        value = piece[0][...]
        value = plus(times_rows(value, *rows, columns=columns(value.shape[1])), sofar)
        store_rows(out, value)
        out[...] = first[...] - out[...]

    @pl.when(lax.axis_index("story") != story)
    def _():
        out[...] = latest[...]


def end_kernel(columns, piece, rows, sofar, out):
    value = piece[0][...]
    store_rows(out, plus(times_rows(value, *rows, columns=columns(value.shape[1])), sofar))


def rows_kernel(pieces, rows, out):
    store_rows(out, times_rows(joined(pieces), *rows))


def coupled_kernel(columns, final, load, early, pieces, sofar, above, below, out):
    here, lower = pieces
    story = lax.axis_index("story")
    width = here.shape[1]

    def finish(value, *terms):
        if not final:
            out[...] = value
            return
        store_rows(out, value)
        total = by_core(load[0][...], load[1][...], 1) - out[...]
        for term in terms:
            total = total - term[...]
        out[...] = total

    @pl.when(story == 0)
    def _():
        finish(plus(times_rows(here[...], *above, columns=columns(width)), sofar))

    @pl.when(story > 0)
    def _():
        finish(plus(times_rows(lower[...], *below, columns=columns(width)), sofar), *early)


def last_kernel(columns, piece, rows, sofar, mine, theirs):
    value = piece[0][...]
    value = plus(times_rows(value, *rows, columns=columns(value.shape[1])), sofar)
    half = value.shape[1] // 2
    mine[...] = value[:, :half]
    theirs[...] = value[:, half:]


def partial_sums(story, shape, pieces, rows):
    sofar = []
    for j, piece in enumerate(pieces[:-1]):
        kernel = functools.partial(part_kernel, from_chip(len(pieces), j), story)
        sofar = call(kernel, shape, [piece], rows, sofar, cost=4 << 20)
    return [pieces[-1]], rows, sofar


class Moves:
    def __init__(self):
        self.stories = lax.axis_size("story")
        self.chips = lax.axis_size("rec")
        self.cores = lax.axis_size("blk")
        assert self.cores == 2 and self.chips & (self.chips - 1) == 0
        self.s = lax.axis_index("story")
        self.r = lax.axis_index("rec")
        self.b = lax.axis_index("blk")

    def permute(self, value, target):
        pairs = []
        for s in range(self.stories):
            for r in range(self.chips):
                for b in range(self.cores):
                    t, q, c = target(s, r, b)
                    pairs.append(
                        (
                            (s * self.chips + r) * self.cores + b,
                            (t * self.chips + q) * self.cores + c,
                        )
                    )
        return lax.ppermute(value, AXES, pairs)

    def core(self, value):
        return self.permute(value, lambda s, r, b: (s, r, 1 - b))

    def chip(self, value, j):
        return self.permute(value, lambda s, r, b: (s, r ^ j, b))

    def story(self, value, parity, j):
        def target(s, r, b):
            t = s ^ 1 if parity == 0 else ((s - 1) ^ 1) + 1
            if t < 0 or t >= self.stories:
                return (s, r ^ 1, b) if self.chips > 1 else (s, r, 1 - b)
            return t, r ^ j, b

        return self.permute(value, target)

    def by_core(self, own, other, axis):
        first = jnp.where(self.b == 0, own, other)
        second = jnp.where(self.b == 0, other, own)
        return jnp.concatenate([first, second], axis=axis)

    def by_chip(self, pieces, axis=1):
        bit = 1
        while bit < self.chips:
            swap = (self.r & bit) != 0
            pieces = [jnp.where(swap, pieces[j ^ bit], pieces[j]) for j in range(self.chips)]
            bit *= 2
        return jnp.concatenate(pieces, axis=axis)

    def pieces(self, pieces):
        return pieces if pieces[0].shape[1] % 128 == 0 else [self.by_chip(pieces)]

    def shift(self, value, step, j):
        pairs = []
        for s in range(self.stories):
            if not 0 <= s + step < self.stories:
                continue
            for r in range(self.chips):
                for b in range(self.cores):
                    pairs.append(
                        (
                            (s * self.chips + r) * self.cores + b,
                            ((s + step) * self.chips + (r ^ j)) * self.cores + b,
                        )
                    )
        return lax.ppermute(value, AXES, pairs)

    def gather_chips(self, value):
        return self.pieces([value] + [self.chip(value, j) for j in range(1, self.chips)])

    def gather_story(self, value, parity):
        return self.pieces([self.story(value, parity, j) for j in range(self.chips)])


def shards(
    record_ids,
    ground_table,
    mass_int,
    mass_face,
    pattern_int,
    pattern_face,
    disp_int,
    vel_int,
    acc_int,
    disp_face,
    vel_face,
    acc_face,
    interior_inverse,
    couple_below,
    couple_above,
    lower,
    pivot,
    upper,
):
    mv = Moves()
    library, records = ground_table.shape[0], record_ids.shape[0]
    half = records // 2
    cube_int = [value[0].T for value in (disp_int, vel_int, acc_int)]
    cube_face = [value[0].T for value in (disp_face, vel_face, acc_face)]
    own_int, own_face = cube_int[0].shape[1], cube_face[0].shape[1]
    load_int, ground = fetched(
        load_int_kernel,
        [(records, own_int), (records, 128)],
        [record_ids.reshape(1, records), ground_table.reshape(1, library), mass_int, pattern_int]
        + cube_int,
    )
    rows_int, rows_face = 2 * own_int, 2 * own_face
    faces = couple_above.shape[2]

    def others(matrix, after):
        return mv.core(lax.optimization_barrier([matrix, *after])[0])

    lower_other = mv.core(lower[0])
    across = [mv.chip(load_int, j) for j in range(1, mv.chips)]
    phase_rows = staged(
        interior_inverse[0], couple_above[0], couple_below[0], after=[load_int]
    )
    phase_rows, *across = lax.optimization_barrier([phase_rows, *across])
    beside = [mv.core(piece) for piece in [load_int] + across]
    pieces = [piece for pair in zip([load_int] + across, beside) for piece in pair]
    aligned = load_int.shape[1] % 128 == 0
    if not aligned:
        pieces = [
            mv.by_chip([mv.by_core(pieces[2 * j], pieces[2 * j + 1], 1) for j in range(mv.chips)])
        ]
    mine, theirs = call(
        functools.partial(forces_kernel, aligned), [(2, half, faces)] * 2, pieces, [phase_rows]
    )
    chunks = call(
        chunks_kernel,
        [(half, faces // mv.chips)] * (2 * mv.chips),
        [mine, mv.core(theirs)],
    )
    ground, _ = lax.optimization_barrier([ground, chunks[0]])
    mine_face, theirs_face = fetched(
        load_face_kernel, [(half, own_face)] * 2, [mass_face, pattern_face] + cube_face, ground
    )
    load_late, _ = lax.optimization_barrier([load_int, chunks[0]])
    mine_int, theirs_int = call(records_kernel, [(half, own_int)] * 2, [load_late])
    halves = lax.optimization_barrier([mv.core(theirs_face), mv.core(theirs_int)])
    load_face_half, load_int_half = [mine_face, halves[0]], [mine_int, halves[1]]
    forces = [mv.shift(chunks[mv.chips], -1, 0)]
    for j in range(1, mv.chips):
        forces += [mv.chip(chunks[j], j), mv.shift(chunks[mv.chips + j], -1, j)]
    shape = [(half, rows_face)]
    (condensed,) = call(condensed_kernel, shape, load_face_half, [chunks[0]] + forces)

    forward = condensed
    pivot_other = others(pivot[0], [condensed])
    for k in range(1, mv.stories):
        came = mv.gather_story(forward, (k - 1) % 2)
        if k == min(2, mv.stories - 1):
            upper_other = others(upper[0], [pivot_other, forward])
            came[-1], pivot_other = lax.optimization_barrier([came[-1], pivot_other])
        if k == mv.stories - 1:
            above_other = others(couple_above[0], [upper_other, forward])
            came[-1], upper_other = lax.optimization_barrier([came[-1], upper_other])
        (forward,) = call(
            functools.partial(step_kernel, from_chip(len(came), len(came) - 1), k),
            shape,
            *partial_sums(k, shape, came, [lower[0], lower_other]),
            [condensed, forward],
        )
    came = mv.gather_chips(forward)
    (pivoted,) = call(
        functools.partial(end_kernel, from_chip(len(came), len(came) - 1)),
        shape,
        *partial_sums(None, shape, came, [pivot[0], pivot_other]),
    )

    shape_int = [(half, rows_int)]
    face = pivoted
    for k in range(mv.stories - 2, -1, -1):
        came = mv.gather_story(face, k % 2)
        if k == mv.stories - 2:
            below_other = others(couple_below[0], [above_other, face])
            came[-1], above_other = lax.optimization_barrier([came[-1], above_other])
        if k == max(mv.stories - 3, 0):
            inverse_other = others(interior_inverse[0], [below_other, face])
            came[-1], below_other = lax.optimization_barrier([came[-1], below_other])
        if k == 0:
            (early,) = call(
                rows_kernel,
                shape_int,
                mv.gather_chips(face),
                [couple_above[0], above_other],
                cost=8 << 20,
            )
            came[-1], early = lax.optimization_barrier([came[-1], early])
        (face,) = call(
            functools.partial(step_kernel, from_chip(len(came), len(came) - 1), k),
            shape,
            *partial_sums(k, shape, came, [upper[0], upper_other]),
            [pivoted, face],
        )

    came = mv.pieces([mv.shift(face, 1, j) for j in range(mv.chips)])
    came[-1], inverse_other = lax.optimization_barrier([came[-1], inverse_other])
    pairs = list(zip(mv.gather_chips(face), came))
    sofar = []
    for j, pair in enumerate(pairs):
        final = j == len(pairs) - 1
        sofar = call(
            functools.partial(coupled_kernel, from_chip(len(pairs), j), final),
            shape_int,
            load_int_half if final else [],
            [early] if final else [],
            list(pair),
            sofar,
            [couple_above[0], above_other],
            [couple_below[0], below_other],
            cost=4 << 20,
        )
    (reduced,) = sofar

    mine, theirs = call(halves_kernel, [(half, own_face)] * 2, [face])
    new_face = call(
        outputs_kernel, [(records, own_face)] * 3, [mine, mv.core(theirs)], cube_face
    )
    came = mv.gather_chips(reduced)
    came[-1], f0, f1, f2 = lax.optimization_barrier([came[-1], *new_face])
    mine, theirs = call(
        functools.partial(last_kernel, from_chip(len(came), len(came) - 1)),
        [(half, own_int)] * 2,
        *partial_sums(None, shape_int, came, [interior_inverse[0], inverse_other]),
    )
    new_int = call(
        outputs_kernel, [(records, own_int)] * 3, [mine, mv.core(theirs)], cube_int
    )
    new_face = [f0, f1, f2]
    return tuple(out.T[None] for out in (*new_int, *new_face))


def solution(mesh):
    whole, rows, cube = P(), P(("groups", "story"), ("rec", "blk")), P(("groups", "story"), ("rec", "blk"), None)
    in_specs = (P("groups"), whole) + (rows,) * 4 + (cube,) * 12
    return jax.shard_map(shards, mesh=mesh, in_specs=in_specs, out_specs=(cube,) * 6, check_vma=False)
```

```python
import functools

import jax
import jax.numpy as jnp
from jax import lax
from jax.experimental import pallas as pl
from jax.experimental.pallas import tpu as pltpu
from jax.sharding import PartitionSpec as P

AXES = ("story", "rec", "blk")
TILE = 256
VMEM = pl.BlockSpec(memory_space=pltpu.VMEM)


def split(value):
    high = value.astype(jnp.bfloat16)
    return high, (value - high.astype(jnp.float32)).astype(jnp.bfloat16)


def stacked(value):
    return jnp.concatenate(split(value), axis=0)


def matmul(left, right, over):
    rows = left.shape[0] // 2
    total = None
    for part in reversed(split(right)):
        both = lax.dot_general(
            left, part, (((1,), (over,)), ((), ())), preferred_element_type=jnp.float32
        )
        both = both[rows:] + both[:rows]
        total = both if total is None else total + both
    return total


def times_rows(left, *refs, columns=slice(None)):
    left = stacked(left)
    count = refs[0].shape[0]
    ends = count * len(refs)
    results = []
    for start in range(0, ends, TILE):
        stop = min(start + TILE, ends)
        blocks = []
        for i, ref in enumerate(refs):
            low, high = max(start - i * count, 0), min(stop - i * count, count)
            if low < high:
                blocks.append(ref[low:high, columns])
        results.append(matmul(left, jnp.concatenate(blocks, axis=0), 1))
    return jnp.concatenate(results, axis=1)


def times(left, ref):
    left = stacked(left)
    width = ref.shape[1]
    columns = [matmul(left, ref[:, n : min(n + TILE, width)], 0) for n in range(0, width, TILE)]
    return jnp.concatenate(columns, axis=1)


def in_order(pieces, own):
    bit = 1
    while bit < len(pieces):
        swap = (own & bit) != 0
        pieces = [jnp.where(swap, pieces[j ^ bit], pieces[j]) for j in range(len(pieces))]
        bit *= 2
    return pieces


def joined(refs, axis="rec"):
    own = lax.axis_index(axis) if len(refs) > 1 else 0
    return jnp.concatenate(in_order([ref[...] for ref in refs], own), axis=1)


def store_rows(ref, value):
    half = value.shape[1] // 2
    swap = lax.axis_index("blk") == 1
    own, other = value[:, :half], value[:, half:]
    ref[...] = jnp.concatenate([jnp.where(swap, other, own), jnp.where(swap, own, other)], axis=1)


def call(kernel, shapes, *groups, cost=0):
    flat = [value for group in groups for value in group]

    def body(*refs):
        at, parts = 0, []
        for group in groups:
            parts.append(refs[at : at + len(group)])
            at += len(group)
        kernel(*parts, *refs[at:])

    out = [jax.ShapeDtypeStruct(shape, jnp.float32) for shape in shapes]
    return pl.pallas_call(
        body,
        in_specs=[VMEM] * len(flat),
        out_specs=[VMEM] * len(out),
        out_shape=out,
        compiler_params=pltpu.CompilerParams(vmem_limit_bytes=24 << 20),
        cost_estimate=pl.CostEstimate(flops=0, bytes_accessed=cost, transcendentals=0) if cost else None,
    )(*flat)


def staged(*matrices, after):
    held = lax.optimization_barrier([*matrices, *after])[: len(matrices)]
    held = [pltpu.with_memory_space_constraint(matrix, pltpu.HBM) for matrix in held]
    count = len(held)
    rows = held[0].shape[0]
    ends = [0]
    for matrix in held:
        ends.append(ends[-1] + matrix.shape[1])

    def body(*refs):
        out, sems = refs[count:]
        copies = []
        for i in range(count):
            for j in range(2):
                part = pl.ds(j * (rows // 2), rows // 2)
                copies.append(
                    pltpu.make_async_copy(
                        refs[i].at[part, :],
                        out.at[part, ends[i] : ends[i + 1]],
                        sems.at[2 * i + j],
                    )
                )
        for copy in copies:
            copy.start()
        for copy in copies:
            copy.wait()

    return pl.pallas_call(
        body,
        in_specs=[pl.BlockSpec(memory_space=pltpu.HBM)] * count,
        out_specs=VMEM,
        out_shape=pltpu.VMEM((rows, ends[-1]), jnp.float32),
        scratch_shapes=[pltpu.SemaphoreType.DMA((2 * count,))],
        compiler_params=pltpu.CompilerParams(vmem_limit_bytes=24 << 20),
    )(*held)


def forces_kernel(swap_chips, pieces, matrices, mine, theirs):
    (rows,) = matrices
    faces = mine.shape[2]
    inner = rows.shape[1] - 2 * faces
    inverse = rows.at[:, :inner]
    above = rows.at[:, inner : inner + faces]
    below = rows.at[:, inner + faces :]
    if swap_chips:
        chips = len(pieces) // 2
        core = lax.axis_index("blk")
        sets = [in_order([pieces[2 * j][...], pieces[2 * j + 1][...]], core) for j in range(chips)]
        sets = [jnp.concatenate(pair, axis=1) for pair in sets]
        full = jnp.concatenate(in_order(sets, lax.axis_index("rec")), axis=1)
    else:
        full = pieces[0][...]
    part = times_rows(full, inverse)
    half = part.shape[0] // 2
    second = lax.axis_index("blk") == 1
    for i, matrix in enumerate((above, below)):
        force = times(part, matrix)
        mine[i] = jnp.where(second, force[half:], force[:half])
        theirs[i] = jnp.where(second, force[:half], force[half:])


def fetched(kernel, shapes, arrays, *held):
    count = len(arrays)
    arrays = [pltpu.with_memory_space_constraint(value, pltpu.HBM) for value in arrays]

    def body(*refs):
        sources, rest = refs[:count], refs[count:-1]
        buffers, sems = rest[len(held) + len(shapes) :], refs[-1]
        copies = [
            pltpu.make_async_copy(source, buffer, sems.at[i])
            for i, (source, buffer) in enumerate(zip(sources, buffers))
        ]
        for copy in copies:
            copy.start()
        for copy in copies:
            copy.wait()
        kernel(buffers, rest[: len(held)], *rest[len(held) : len(held) + len(shapes)])

    out = [jax.ShapeDtypeStruct(shape, jnp.float32) for shape in shapes]
    return pl.pallas_call(
        body,
        in_specs=[pl.BlockSpec(memory_space=pltpu.HBM)] * count + [VMEM] * len(held),
        out_specs=[VMEM] * len(out),
        out_shape=out,
        scratch_shapes=[pltpu.VMEM(value.shape, value.dtype) for value in arrays]
        + [pltpu.SemaphoreType.DMA((count,))],
        compiler_params=pltpu.CompilerParams(vmem_limit_bytes=24 << 20),
    )(*arrays, *held)


def newmark_load(mass, pattern, disp, vel, acc, ground):
    return mass[...] * (disp[...] + 2.0 * vel[...] + acc[...] - pattern[...] * ground)


def load_int_kernel(fetched_refs, held, load, ground_out):
    ids, table, *arrays = fetched_refs
    records, library = ids.shape[1], table.shape[1]
    shape = (records, records)
    diagonal = lax.broadcasted_iota(jnp.int32, shape, 0) == lax.broadcasted_iota(jnp.int32, shape, 1)
    row = jnp.broadcast_to(ids[...].astype(jnp.float32), shape)
    column = jnp.sum(jnp.where(diagonal, row, 0.0), axis=1, keepdims=True)
    index = lax.broadcasted_iota(jnp.int32, (records, library), 1).astype(jnp.float32)
    ground = jnp.sum(jnp.where(column == index, table[...], 0.0), axis=1, keepdims=True)
    ground_out[...] = jnp.broadcast_to(ground, ground_out.shape)
    load[...] = newmark_load(*arrays, ground)


def load_face_kernel(fetched_refs, held, mine, theirs):
    load = newmark_load(*fetched_refs, held[0][:, :1])
    half = load.shape[0] // 2
    second = lax.axis_index("blk") == 1
    mine[...] = jnp.where(second, load[half:], load[:half])
    theirs[...] = jnp.where(second, load[:half], load[half:])


def records_kernel(whole, mine, theirs):
    value = whole[0][...]
    half = value.shape[0] // 2
    second = lax.axis_index("blk") == 1
    mine[...] = jnp.where(second, value[half:], value[:half])
    theirs[...] = jnp.where(second, value[:half], value[half:])


def by_core(own, other, axis):
    second = lax.axis_index("blk") == 1
    return jnp.concatenate([jnp.where(second, other, own), jnp.where(second, own, other)], axis=axis)


def condensed_kernel(load, forces, out):
    value = by_core(load[0][...], load[1][...], 1)
    for force in forces:
        value = value - force[...]
    out[...] = value


def halves_kernel(whole, mine, theirs):
    value = whole[0][...]
    half = value.shape[1] // 2
    second = lax.axis_index("blk") == 1
    mine[...] = jnp.where(second, value[:, half:], value[:, :half])
    theirs[...] = jnp.where(second, value[:, :half], value[:, half:])


def outputs_kernel(halves, before, new_disp, new_vel, new_acc):
    disp, vel, acc = before
    value = by_core(halves[0][...], halves[1][...], 0)
    change = value - disp[...] - 2.0 * vel[...] - acc[...]
    new_disp[...] = value
    new_vel[...] = vel[...] + acc[...] + change
    new_acc[...] = change


def chunks_kernel(inputs, *outs):
    mine, came = inputs
    chips = len(outs) // 2
    for i in range(2):
        total = mine[i] + came[i]
        width = total.shape[1] // chips
        pieces = [total[:, j * width : (j + 1) * width] for j in range(chips)]
        for j, piece in enumerate(in_order(pieces, lax.axis_index("rec"))):
            outs[i * chips + j][...] = piece


def from_chip(count, j):
    def columns(width):
        if count == 1:
            return slice(None)
        start = (lax.axis_index("rec") ^ j) * width
        return pl.ds(pl.multiple_of(start, 128), width)

    return columns


def plus(value, sofar):
    return value + sofar[0][...] if sofar else value


def part_kernel(columns, story, piece, rows, sofar, out):
    def product():
        value = piece[0][...]
        out[...] = plus(times_rows(value, *rows, columns=columns(value.shape[1])), sofar)

    if story is None:
        product()
    else:
        pl.when(lax.axis_index("story") == story)(product)


def step_kernel(columns, story, piece, rows, sofar, terms, out):
    first, latest = terms

    @pl.when(lax.axis_index("story") == story)
    def _():
        value = piece[0][...]
        value = plus(times_rows(value, *rows, columns=columns(value.shape[1])), sofar)
        store_rows(out, value)
        out[...] = first[...] - out[...]

    @pl.when(lax.axis_index("story") != story)
    def _():
        out[...] = latest[...]


def end_kernel(columns, piece, rows, sofar, out):
    value = piece[0][...]
    store_rows(out, plus(times_rows(value, *rows, columns=columns(value.shape[1])), sofar))


def coupled_kernel(columns, final, load, piece, rows, sofar, out):
    story = lax.axis_index("story")

    def finish(value):
        if final:
            store_rows(out, value)
            out[...] = by_core(load[0][...], load[1][...], 1) - out[...]
        else:
            out[...] = value

    @pl.when(story == 0)
    def _():
        finish(sofar[0][...])

    @pl.when(story > 0)
    def _():
        value = piece[0][...]
        finish(plus(times_rows(value, *rows, columns=columns(value.shape[1])), sofar))


def last_kernel(columns, piece, rows, sofar, mine, theirs):
    value = piece[0][...]
    value = plus(times_rows(value, *rows, columns=columns(value.shape[1])), sofar)
    half = value.shape[1] // 2
    mine[...] = value[:, :half]
    theirs[...] = value[:, half:]


def partial_sums(story, shape, pieces, rows):
    sofar = []
    for j, piece in enumerate(pieces[:-1]):
        kernel = functools.partial(part_kernel, from_chip(len(pieces), j), story)
        sofar = call(kernel, shape, [piece], rows, sofar, cost=4 << 20)
    return [pieces[-1]], rows, sofar


class Moves:
    def __init__(self):
        self.stories = lax.axis_size("story")
        self.chips = lax.axis_size("rec")
        self.cores = lax.axis_size("blk")
        assert self.cores == 2 and self.chips & (self.chips - 1) == 0
        self.s = lax.axis_index("story")
        self.r = lax.axis_index("rec")
        self.b = lax.axis_index("blk")

    def permute(self, value, target):
        pairs = []
        for s in range(self.stories):
            for r in range(self.chips):
                for b in range(self.cores):
                    t, q, c = target(s, r, b)
                    pairs.append(
                        (
                            (s * self.chips + r) * self.cores + b,
                            (t * self.chips + q) * self.cores + c,
                        )
                    )
        return lax.ppermute(value, AXES, pairs)

    def core(self, value):
        return self.permute(value, lambda s, r, b: (s, r, 1 - b))

    def chip(self, value, j):
        return self.permute(value, lambda s, r, b: (s, r ^ j, b))

    def story(self, value, parity, j):
        def target(s, r, b):
            t = s ^ 1 if parity == 0 else ((s - 1) ^ 1) + 1
            if t < 0 or t >= self.stories:
                return (s, r ^ 1, b) if self.chips > 1 else (s, r, 1 - b)
            return t, r ^ j, b

        return self.permute(value, target)

    def by_core(self, own, other, axis):
        first = jnp.where(self.b == 0, own, other)
        second = jnp.where(self.b == 0, other, own)
        return jnp.concatenate([first, second], axis=axis)

    def by_chip(self, pieces, axis=1):
        bit = 1
        while bit < self.chips:
            swap = (self.r & bit) != 0
            pieces = [jnp.where(swap, pieces[j ^ bit], pieces[j]) for j in range(self.chips)]
            bit *= 2
        return jnp.concatenate(pieces, axis=axis)

    def pieces(self, pieces):
        return pieces if pieces[0].shape[1] % 128 == 0 else [self.by_chip(pieces)]

    def shift(self, value, step, j):
        pairs = []
        for s in range(self.stories):
            if not 0 <= s + step < self.stories:
                continue
            for r in range(self.chips):
                for b in range(self.cores):
                    pairs.append(
                        (
                            (s * self.chips + r) * self.cores + b,
                            ((s + step) * self.chips + (r ^ j)) * self.cores + b,
                        )
                    )
        return lax.ppermute(value, AXES, pairs)

    def gather_chips(self, value):
        return self.pieces([value] + [self.chip(value, j) for j in range(1, self.chips)])

    def gather_story(self, value, parity):
        return self.pieces([self.story(value, parity, j) for j in range(self.chips)])


def shards(
    record_ids,
    ground_table,
    mass_int,
    mass_face,
    pattern_int,
    pattern_face,
    disp_int,
    vel_int,
    acc_int,
    disp_face,
    vel_face,
    acc_face,
    interior_inverse,
    couple_below,
    couple_above,
    lower,
    pivot,
    upper,
):
    mv = Moves()
    library, records = ground_table.shape[0], record_ids.shape[0]
    half = records // 2
    cube_int = [value[0].T for value in (disp_int, vel_int, acc_int)]
    cube_face = [value[0].T for value in (disp_face, vel_face, acc_face)]
    own_int, own_face = cube_int[0].shape[1], cube_face[0].shape[1]
    load_int, ground = fetched(
        load_int_kernel,
        [(records, own_int), (records, 128)],
        [record_ids.reshape(1, records), ground_table.reshape(1, library), mass_int, pattern_int]
        + cube_int,
    )
    rows_int, rows_face = 2 * own_int, 2 * own_face
    faces = couple_above.shape[2]

    def others(matrix, after):
        return mv.core(lax.optimization_barrier([matrix, *after])[0])

    lower_other = mv.core(lower[0])
    across = [mv.chip(load_int, j) for j in range(1, mv.chips)]
    phase_rows = staged(
        interior_inverse[0], couple_above[0], couple_below[0], after=[load_int]
    )
    phase_rows, *across = lax.optimization_barrier([phase_rows, *across])
    beside = [mv.core(piece) for piece in [load_int] + across]
    pieces = [piece for pair in zip([load_int] + across, beside) for piece in pair]
    aligned = load_int.shape[1] % 128 == 0
    if not aligned:
        pieces = [
            mv.by_chip([mv.by_core(pieces[2 * j], pieces[2 * j + 1], 1) for j in range(mv.chips)])
        ]
    mine, theirs = call(
        functools.partial(forces_kernel, aligned), [(2, half, faces)] * 2, pieces, [phase_rows]
    )
    chunks = call(
        chunks_kernel,
        [(half, faces // mv.chips)] * (2 * mv.chips),
        [mine, mv.core(theirs)],
    )
    ground, _ = lax.optimization_barrier([ground, chunks[0]])
    mine_face, theirs_face = fetched(
        load_face_kernel, [(half, own_face)] * 2, [mass_face, pattern_face] + cube_face, ground
    )
    load_late, _ = lax.optimization_barrier([load_int, chunks[0]])
    mine_int, theirs_int = call(records_kernel, [(half, own_int)] * 2, [load_late])
    halves = lax.optimization_barrier([mv.core(theirs_face), mv.core(theirs_int)])
    load_face_half, load_int_half = [mine_face, halves[0]], [mine_int, halves[1]]
    forces = [mv.shift(chunks[mv.chips], -1, 0)]
    for j in range(1, mv.chips):
        forces += [mv.chip(chunks[j], j), mv.shift(chunks[mv.chips + j], -1, j)]
    shape = [(half, rows_face)]
    (condensed,) = call(condensed_kernel, shape, load_face_half, [chunks[0]] + forces)

    forward = condensed
    pivot_other = others(pivot[0], [condensed])
    for k in range(1, mv.stories):
        came = mv.gather_story(forward, (k - 1) % 2)
        if k == min(2, mv.stories - 1):
            upper_other = others(upper[0], [pivot_other, forward])
            came[-1], pivot_other = lax.optimization_barrier([came[-1], pivot_other])
        if k == mv.stories - 1:
            above_other = others(couple_above[0], [upper_other, forward])
            came[-1], upper_other = lax.optimization_barrier([came[-1], upper_other])
        (forward,) = call(
            functools.partial(step_kernel, from_chip(len(came), len(came) - 1), k),
            shape,
            *partial_sums(k, shape, came, [lower[0], lower_other]),
            [condensed, forward],
        )
    came = mv.gather_chips(forward)
    (pivoted,) = call(
        functools.partial(end_kernel, from_chip(len(came), len(came) - 1)),
        shape,
        *partial_sums(None, shape, came, [pivot[0], pivot_other]),
    )

    shape_int = [(half, rows_int)]
    face = pivoted
    for k in range(mv.stories - 2, -1, -1):
        came = mv.gather_story(face, k % 2)
        if k == mv.stories - 2:
            below_other = others(couple_below[0], [above_other, face])
            came[-1], above_other = lax.optimization_barrier([came[-1], above_other])
        if k == max(mv.stories - 3, 0):
            inverse_other = others(interior_inverse[0], [below_other, face])
            came[-1], below_other = lax.optimization_barrier([came[-1], below_other])
        (face,) = call(
            functools.partial(step_kernel, from_chip(len(came), len(came) - 1), k),
            shape,
            *partial_sums(k, shape, came, [upper[0], upper_other]),
            [pivoted, face],
        )

    here = mv.gather_chips(face)
    came = mv.pieces([mv.shift(face, 1, j) for j in range(mv.chips)])
    came[-1], inverse_other = lax.optimization_barrier([came[-1], inverse_other])
    rows = [couple_above[0], above_other]
    sofar = []
    for j, piece in enumerate(here):
        kernel = functools.partial(part_kernel, from_chip(len(here), j), None)
        sofar = call(kernel, shape_int, [piece], rows, sofar, cost=4 << 20)
    rows = [couple_below[0], below_other]
    for j, piece in enumerate(came):
        final = j == len(came) - 1
        sofar = call(
            functools.partial(coupled_kernel, from_chip(len(came), j), final),
            shape_int,
            load_int_half if final else [],
            [piece],
            rows,
            sofar,
            cost=4 << 20,
        )
    (reduced,) = sofar

    mine, theirs = call(halves_kernel, [(half, own_face)] * 2, [face])
    new_face = call(
        outputs_kernel, [(records, own_face)] * 3, [mine, mv.core(theirs)], cube_face
    )
    came = mv.gather_chips(reduced)
    came[-1], f0, f1, f2 = lax.optimization_barrier([came[-1], *new_face])
    mine, theirs = call(
        functools.partial(last_kernel, from_chip(len(came), len(came) - 1)),
        [(half, own_int)] * 2,
        *partial_sums(None, shape_int, came, [interior_inverse[0], inverse_other]),
    )
    new_int = call(
        outputs_kernel, [(records, own_int)] * 3, [mine, mv.core(theirs)], cube_int
    )
    new_face = [f0, f1, f2]
    return tuple(out.T[None] for out in (*new_int, *new_face))


def solution(mesh):
    whole, rows, cube = P(), P(("groups", "story"), ("rec", "blk")), P(("groups", "story"), ("rec", "blk"), None)
    in_specs = (P("groups"), whole) + (rows,) * 4 + (cube,) * 12
    return jax.shard_map(shards, mesh=mesh, in_specs=in_specs, out_specs=(cube,) * 6, check_vma=False)
```

```python
import functools

import jax
import jax.numpy as jnp
from jax import lax
from jax.experimental import pallas as pl
from jax.experimental.pallas import tpu as pltpu
from jax.sharding import PartitionSpec as P

AXES = ("story", "rec", "blk")
TILE = 256
VMEM = pl.BlockSpec(memory_space=pltpu.VMEM)


def split(value):
    high = value.astype(jnp.bfloat16)
    return high, (value - high.astype(jnp.float32)).astype(jnp.bfloat16)


def stacked(value):
    return jnp.concatenate(split(value), axis=0)


def matmul(left, right, over):
    rows = left.shape[0] // 2
    total = None
    for part in reversed(split(right)):
        both = lax.dot_general(
            left, part, (((1,), (over,)), ((), ())), preferred_element_type=jnp.float32
        )
        both = both[rows:] + both[:rows]
        total = both if total is None else total + both
    return total


def times_rows(left, *refs, columns=slice(None)):
    left = stacked(left)
    count = refs[0].shape[0]
    ends = count * len(refs)
    results = []
    for start in range(0, ends, TILE):
        stop = min(start + TILE, ends)
        blocks = []
        for i, ref in enumerate(refs):
            low, high = max(start - i * count, 0), min(stop - i * count, count)
            if low < high:
                blocks.append(ref[low:high, columns])
        results.append(matmul(left, jnp.concatenate(blocks, axis=0), 1))
    return jnp.concatenate(results, axis=1)


def times(left, ref):
    left = stacked(left)
    width = ref.shape[1]
    columns = [matmul(left, ref[:, n : min(n + TILE, width)], 0) for n in range(0, width, TILE)]
    return jnp.concatenate(columns, axis=1)


def in_order(pieces, own):
    bit = 1
    while bit < len(pieces):
        swap = (own & bit) != 0
        pieces = [jnp.where(swap, pieces[j ^ bit], pieces[j]) for j in range(len(pieces))]
        bit *= 2
    return pieces


def joined(refs, axis="rec"):
    own = lax.axis_index(axis) if len(refs) > 1 else 0
    return jnp.concatenate(in_order([ref[...] for ref in refs], own), axis=1)


def store_rows(ref, value):
    half = value.shape[1] // 2
    swap = lax.axis_index("blk") == 1
    own, other = value[:, :half], value[:, half:]
    ref[...] = jnp.concatenate([jnp.where(swap, other, own), jnp.where(swap, own, other)], axis=1)


def call(kernel, shapes, *groups, cost=0):
    flat = [value for group in groups for value in group]

    def body(*refs):
        at, parts = 0, []
        for group in groups:
            parts.append(refs[at : at + len(group)])
            at += len(group)
        kernel(*parts, *refs[at:])

    out = [jax.ShapeDtypeStruct(shape, jnp.float32) for shape in shapes]
    return pl.pallas_call(
        body,
        in_specs=[VMEM] * len(flat),
        out_specs=[VMEM] * len(out),
        out_shape=out,
        compiler_params=pltpu.CompilerParams(vmem_limit_bytes=24 << 20),
        cost_estimate=pl.CostEstimate(flops=0, bytes_accessed=cost, transcendentals=0) if cost else None,
    )(*flat)


def staged(*matrices, after):
    held = lax.optimization_barrier([*matrices, *after])[: len(matrices)]
    held = [pltpu.with_memory_space_constraint(matrix, pltpu.HBM) for matrix in held]
    count = len(held)
    rows = held[0].shape[0]
    ends = [0]
    for matrix in held:
        ends.append(ends[-1] + matrix.shape[1])

    def body(*refs):
        out, sems = refs[count:]
        copies = []
        for i in range(count):
            for j in range(2):
                part = pl.ds(j * (rows // 2), rows // 2)
                copies.append(
                    pltpu.make_async_copy(
                        refs[i].at[part, :],
                        out.at[part, ends[i] : ends[i + 1]],
                        sems.at[2 * i + j],
                    )
                )
        for copy in copies:
            copy.start()
        for copy in copies:
            copy.wait()

    return pl.pallas_call(
        body,
        in_specs=[pl.BlockSpec(memory_space=pltpu.HBM)] * count,
        out_specs=VMEM,
        out_shape=pltpu.VMEM((rows, ends[-1]), jnp.float32),
        scratch_shapes=[pltpu.SemaphoreType.DMA((2 * count,))],
        compiler_params=pltpu.CompilerParams(vmem_limit_bytes=24 << 20),
    )(*held)


def forces_kernel(swap_chips, pieces, matrices, mine, theirs):
    (rows,) = matrices
    faces = mine.shape[2]
    inner = rows.shape[1] - 2 * faces
    inverse = rows.at[:, :inner]
    above = rows.at[:, inner : inner + faces]
    below = rows.at[:, inner + faces :]
    if swap_chips:
        chips = len(pieces) // 2
        core = lax.axis_index("blk")
        sets = [in_order([pieces[2 * j][...], pieces[2 * j + 1][...]], core) for j in range(chips)]
        sets = [jnp.concatenate(pair, axis=1) for pair in sets]
        full = jnp.concatenate(in_order(sets, lax.axis_index("rec")), axis=1)
    else:
        full = pieces[0][...]
    part = times_rows(full, inverse)
    half = part.shape[0] // 2
    second = lax.axis_index("blk") == 1
    for i, matrix in enumerate((above, below)):
        force = times(part, matrix)
        mine[i] = jnp.where(second, force[half:], force[:half])
        theirs[i] = jnp.where(second, force[:half], force[half:])


def fetched(kernel, shapes, arrays, *held):
    count = len(arrays)
    arrays = [pltpu.with_memory_space_constraint(value, pltpu.HBM) for value in arrays]

    def body(*refs):
        sources, rest = refs[:count], refs[count:-1]
        buffers, sems = rest[len(held) + len(shapes) :], refs[-1]
        copies = [
            pltpu.make_async_copy(source, buffer, sems.at[i])
            for i, (source, buffer) in enumerate(zip(sources, buffers))
        ]
        for copy in copies:
            copy.start()
        for copy in copies:
            copy.wait()
        kernel(buffers, rest[: len(held)], *rest[len(held) : len(held) + len(shapes)])

    out = [jax.ShapeDtypeStruct(shape, jnp.float32) for shape in shapes]
    return pl.pallas_call(
        body,
        in_specs=[pl.BlockSpec(memory_space=pltpu.HBM)] * count + [VMEM] * len(held),
        out_specs=[VMEM] * len(out),
        out_shape=out,
        scratch_shapes=[pltpu.VMEM(value.shape, value.dtype) for value in arrays]
        + [pltpu.SemaphoreType.DMA((count,))],
        compiler_params=pltpu.CompilerParams(vmem_limit_bytes=24 << 20),
    )(*arrays, *held)


def newmark_load(mass, pattern, disp, vel, acc, ground):
    return mass[...] * (disp[...] + 2.0 * vel[...] + acc[...] - pattern[...] * ground)


def load_int_kernel(fetched_refs, held, load, ground_out):
    ids, table, *arrays = fetched_refs
    records, library = ids.shape[1], table.shape[1]
    shape = (records, records)
    diagonal = lax.broadcasted_iota(jnp.int32, shape, 0) == lax.broadcasted_iota(jnp.int32, shape, 1)
    row = jnp.broadcast_to(ids[...].astype(jnp.float32), shape)
    column = jnp.sum(jnp.where(diagonal, row, 0.0), axis=1, keepdims=True)
    index = lax.broadcasted_iota(jnp.int32, (records, library), 1).astype(jnp.float32)
    ground = jnp.sum(jnp.where(column == index, table[...], 0.0), axis=1, keepdims=True)
    ground_out[...] = jnp.broadcast_to(ground, ground_out.shape)
    load[...] = newmark_load(*arrays, ground)


def load_face_kernel(fetched_refs, held, mine, theirs):
    load = newmark_load(*fetched_refs, held[0][:, :1])
    half = load.shape[0] // 2
    second = lax.axis_index("blk") == 1
    mine[...] = jnp.where(second, load[half:], load[:half])
    theirs[...] = jnp.where(second, load[:half], load[half:])


def records_kernel(whole, mine, theirs):
    value = whole[0][...]
    half = value.shape[0] // 2
    second = lax.axis_index("blk") == 1
    mine[...] = jnp.where(second, value[half:], value[:half])
    theirs[...] = jnp.where(second, value[:half], value[half:])


def by_core(own, other, axis):
    second = lax.axis_index("blk") == 1
    return jnp.concatenate([jnp.where(second, other, own), jnp.where(second, own, other)], axis=axis)


def condensed_kernel(load, forces, out):
    value = by_core(load[0][...], load[1][...], 1)
    for force in forces:
        value = value - force[...]
    out[...] = value


def halves_kernel(whole, mine, theirs):
    value = whole[0][...]
    half = value.shape[1] // 2
    second = lax.axis_index("blk") == 1
    mine[...] = jnp.where(second, value[:, half:], value[:, :half])
    theirs[...] = jnp.where(second, value[:, :half], value[:, half:])


def outputs_kernel(halves, before, new_disp, new_vel, new_acc):
    disp, vel, acc = before
    value = by_core(halves[0][...], halves[1][...], 0)
    change = value - disp[...] - 2.0 * vel[...] - acc[...]
    new_disp[...] = value
    new_vel[...] = vel[...] + acc[...] + change
    new_acc[...] = change


def chunks_kernel(inputs, *outs):
    mine, came = inputs
    chips = len(outs) // 2
    for i in range(2):
        total = mine[i] + came[i]
        width = total.shape[1] // chips
        pieces = [total[:, j * width : (j + 1) * width] for j in range(chips)]
        for j, piece in enumerate(in_order(pieces, lax.axis_index("rec"))):
            outs[i * chips + j][...] = piece


def from_chip(count, j):
    def columns(width):
        if count == 1:
            return slice(None)
        start = (lax.axis_index("rec") ^ j) * width
        return pl.ds(pl.multiple_of(start, 128), width)

    return columns


def plus(value, sofar):
    return value + sofar[0][...] if sofar else value


def part_kernel(columns, story, piece, rows, sofar, out):
    def product():
        value = piece[0][...]
        out[...] = plus(times_rows(value, *rows, columns=columns(value.shape[1])), sofar)

    if story is None:
        product()
    else:
        pl.when(lax.axis_index("story") == story)(product)


def step_kernel(columns, story, piece, rows, sofar, terms, out):
    first, latest = terms

    @pl.when(lax.axis_index("story") == story)
    def _():
        value = piece[0][...]
        value = plus(times_rows(value, *rows, columns=columns(value.shape[1])), sofar)
        store_rows(out, value)
        out[...] = first[...] - out[...]

    @pl.when(lax.axis_index("story") != story)
    def _():
        out[...] = latest[...]


def end_kernel(columns, piece, rows, sofar, out):
    value = piece[0][...]
    store_rows(out, plus(times_rows(value, *rows, columns=columns(value.shape[1])), sofar))


def coupled_kernel(columns, final, load, pair, rows, sofar, out):
    even, odd = pair
    story = lax.axis_index("story")

    def finish(value):
        if final:
            store_rows(out, value)
            out[...] = by_core(load[0][...], load[1][...], 1) - out[...]
        else:
            out[...] = value

    @pl.when(story == 0)
    def _():
        finish(sofar[0][...])

    @pl.when(story > 0)
    def _():
        value = jnp.where(lax.rem(story, 2) == 1, even[...], odd[...])
        finish(plus(times_rows(value, *rows, columns=columns(value.shape[1])), sofar))


def last_kernel(columns, piece, rows, sofar, mine, theirs):
    value = piece[0][...]
    value = plus(times_rows(value, *rows, columns=columns(value.shape[1])), sofar)
    half = value.shape[1] // 2
    mine[...] = value[:, :half]
    theirs[...] = value[:, half:]


def partial_sums(story, shape, pieces, rows):
    sofar = []
    for j, piece in enumerate(pieces[:-1]):
        kernel = functools.partial(part_kernel, from_chip(len(pieces), j), story)
        sofar = call(kernel, shape, [piece], rows, sofar, cost=4 << 20)
    return [pieces[-1]], rows, sofar


class Moves:
    def __init__(self):
        self.stories = lax.axis_size("story")
        self.chips = lax.axis_size("rec")
        self.cores = lax.axis_size("blk")
        assert self.cores == 2 and self.chips & (self.chips - 1) == 0
        self.s = lax.axis_index("story")
        self.r = lax.axis_index("rec")
        self.b = lax.axis_index("blk")

    def permute(self, value, target):
        pairs = []
        for s in range(self.stories):
            for r in range(self.chips):
                for b in range(self.cores):
                    t, q, c = target(s, r, b)
                    pairs.append(
                        (
                            (s * self.chips + r) * self.cores + b,
                            (t * self.chips + q) * self.cores + c,
                        )
                    )
        return lax.ppermute(value, AXES, pairs)

    def core(self, value):
        return self.permute(value, lambda s, r, b: (s, r, 1 - b))

    def chip(self, value, j):
        return self.permute(value, lambda s, r, b: (s, r ^ j, b))

    def story(self, value, parity, j):
        def target(s, r, b):
            t = s ^ 1 if parity == 0 else ((s - 1) ^ 1) + 1
            if t < 0 or t >= self.stories:
                return (s, r ^ 1, b) if self.chips > 1 else (s, r, 1 - b)
            return t, r ^ j, b

        return self.permute(value, target)

    def by_core(self, own, other, axis):
        first = jnp.where(self.b == 0, own, other)
        second = jnp.where(self.b == 0, other, own)
        return jnp.concatenate([first, second], axis=axis)

    def by_chip(self, pieces, axis=1):
        bit = 1
        while bit < self.chips:
            swap = (self.r & bit) != 0
            pieces = [jnp.where(swap, pieces[j ^ bit], pieces[j]) for j in range(self.chips)]
            bit *= 2
        return jnp.concatenate(pieces, axis=axis)

    def pieces(self, pieces):
        return pieces if pieces[0].shape[1] % 128 == 0 else [self.by_chip(pieces)]

    def shift(self, value, step, j):
        pairs = []
        for s in range(self.stories):
            if not 0 <= s + step < self.stories:
                continue
            for r in range(self.chips):
                for b in range(self.cores):
                    pairs.append(
                        (
                            (s * self.chips + r) * self.cores + b,
                            ((s + step) * self.chips + (r ^ j)) * self.cores + b,
                        )
                    )
        return lax.ppermute(value, AXES, pairs)

    def gather_chips(self, value):
        return self.pieces([value] + [self.chip(value, j) for j in range(1, self.chips)])

    def gather_story(self, value, parity):
        return self.pieces([self.story(value, parity, j) for j in range(self.chips)])


def shards(
    record_ids,
    ground_table,
    mass_int,
    mass_face,
    pattern_int,
    pattern_face,
    disp_int,
    vel_int,
    acc_int,
    disp_face,
    vel_face,
    acc_face,
    interior_inverse,
    couple_below,
    couple_above,
    lower,
    pivot,
    upper,
):
    mv = Moves()
    library, records = ground_table.shape[0], record_ids.shape[0]
    half = records // 2
    cube_int = [value[0].T for value in (disp_int, vel_int, acc_int)]
    cube_face = [value[0].T for value in (disp_face, vel_face, acc_face)]
    own_int, own_face = cube_int[0].shape[1], cube_face[0].shape[1]
    load_int, ground = fetched(
        load_int_kernel,
        [(records, own_int), (records, 128)],
        [record_ids.reshape(1, records), ground_table.reshape(1, library), mass_int, pattern_int]
        + cube_int,
    )
    rows_int, rows_face = 2 * own_int, 2 * own_face
    faces = couple_above.shape[2]

    def others(matrix, after):
        return mv.core(lax.optimization_barrier([matrix, *after])[0])

    lower_other = mv.core(lower[0])
    across = [mv.chip(load_int, j) for j in range(1, mv.chips)]
    phase_rows = staged(
        interior_inverse[0], couple_above[0], couple_below[0], after=[load_int]
    )
    phase_rows, *across = lax.optimization_barrier([phase_rows, *across])
    beside = [mv.core(piece) for piece in [load_int] + across]
    pieces = [piece for pair in zip([load_int] + across, beside) for piece in pair]
    aligned = load_int.shape[1] % 128 == 0
    if not aligned:
        pieces = [
            mv.by_chip([mv.by_core(pieces[2 * j], pieces[2 * j + 1], 1) for j in range(mv.chips)])
        ]
    mine, theirs = call(
        functools.partial(forces_kernel, aligned), [(2, half, faces)] * 2, pieces, [phase_rows]
    )
    chunks = call(
        chunks_kernel,
        [(half, faces // mv.chips)] * (2 * mv.chips),
        [mine, mv.core(theirs)],
    )
    ground, _ = lax.optimization_barrier([ground, chunks[0]])
    mine_face, theirs_face = fetched(
        load_face_kernel, [(half, own_face)] * 2, [mass_face, pattern_face] + cube_face, ground
    )
    load_late, _ = lax.optimization_barrier([load_int, chunks[0]])
    mine_int, theirs_int = call(records_kernel, [(half, own_int)] * 2, [load_late])
    halves = lax.optimization_barrier([mv.core(theirs_face), mv.core(theirs_int)])
    load_face_half, load_int_half = [mine_face, halves[0]], [mine_int, halves[1]]
    forces = [mv.shift(chunks[mv.chips], -1, 0)]
    for j in range(1, mv.chips):
        forces += [mv.chip(chunks[j], j), mv.shift(chunks[mv.chips + j], -1, j)]
    shape = [(half, rows_face)]
    (condensed,) = call(condensed_kernel, shape, load_face_half, [chunks[0]] + forces)

    forward = condensed
    pivot_other = others(pivot[0], [condensed])
    for k in range(1, mv.stories):
        came = mv.gather_story(forward, (k - 1) % 2)
        if k == min(2, mv.stories - 1):
            upper_other = others(upper[0], [pivot_other, forward])
            came[-1], pivot_other = lax.optimization_barrier([came[-1], pivot_other])
        if k == mv.stories - 1:
            above_other = others(couple_above[0], [upper_other, forward])
            came[-1], upper_other = lax.optimization_barrier([came[-1], upper_other])
        (forward,) = call(
            functools.partial(step_kernel, from_chip(len(came), len(came) - 1), k),
            shape,
            *partial_sums(k, shape, came, [lower[0], lower_other]),
            [condensed, forward],
        )
    came = mv.gather_chips(forward)
    (pivoted,) = call(
        functools.partial(end_kernel, from_chip(len(came), len(came) - 1)),
        shape,
        *partial_sums(None, shape, came, [pivot[0], pivot_other]),
    )

    shape_int = [(half, rows_int)]
    face = pivoted
    for k in range(mv.stories - 2, -1, -1):
        came = mv.gather_story(face, k % 2)
        if k == mv.stories - 2:
            below_other = others(couple_below[0], [above_other, face])
            came[-1], above_other = lax.optimization_barrier([came[-1], above_other])
        if k == max(mv.stories - 3, 0):
            inverse_other = others(interior_inverse[0], [below_other, face])
            came[-1], below_other = lax.optimization_barrier([came[-1], below_other])
        if k == 0:
            late, came[0] = lax.optimization_barrier([face, came[0]])
            odd = mv.gather_story(late, 1)
        (face,) = call(
            functools.partial(step_kernel, from_chip(len(came), len(came) - 1), k),
            shape,
            *partial_sums(k, shape, came, [upper[0], upper_other]),
            [pivoted, face],
        )

    here = mv.gather_chips(face)
    face, *odd = lax.optimization_barrier([face, *odd])
    even = mv.gather_story(face, 0)
    even[-1], inverse_other = lax.optimization_barrier([even[-1], inverse_other])
    rows = [couple_above[0], above_other]
    sofar = []
    for j, piece in enumerate(here):
        kernel = functools.partial(part_kernel, from_chip(len(here), j), None)
        sofar = call(kernel, shape_int, [piece], rows, sofar, cost=4 << 20)
    rows = [couple_below[0], below_other]
    for j, pair in enumerate(zip(even, odd)):
        final = j == len(even) - 1
        sofar = call(
            functools.partial(coupled_kernel, from_chip(len(even), j), final),
            shape_int,
            load_int_half if final else [],
            list(pair),
            rows,
            sofar,
            cost=4 << 20,
        )
    (reduced,) = sofar

    mine, theirs = call(halves_kernel, [(half, own_face)] * 2, [face])
    new_face = call(
        outputs_kernel, [(records, own_face)] * 3, [mine, mv.core(theirs)], cube_face
    )
    came = mv.gather_chips(reduced)
    came[-1], f0, f1, f2 = lax.optimization_barrier([came[-1], *new_face])
    mine, theirs = call(
        functools.partial(last_kernel, from_chip(len(came), len(came) - 1)),
        [(half, own_int)] * 2,
        *partial_sums(None, shape_int, came, [interior_inverse[0], inverse_other]),
    )
    new_int = call(
        outputs_kernel, [(records, own_int)] * 3, [mine, mv.core(theirs)], cube_int
    )
    new_face = [f0, f1, f2]
    return tuple(out.T[None] for out in (*new_int, *new_face))


def solution(mesh):
    whole, rows, cube = P(), P(("groups", "story"), ("rec", "blk")), P(("groups", "story"), ("rec", "blk"), None)
    in_specs = (P("groups"), whole) + (rows,) * 4 + (cube,) * 12
    return jax.shard_map(shards, mesh=mesh, in_specs=in_specs, out_specs=(cube,) * 6, check_vma=False)
```

```python
import functools

import jax
import jax.numpy as jnp
from jax import lax
from jax.experimental import pallas as pl
from jax.experimental.pallas import tpu as pltpu
from jax.sharding import PartitionSpec as P

AXES = ("story", "rec", "blk")
TILE = 256
VMEM = pl.BlockSpec(memory_space=pltpu.VMEM)


def split(value):
    high = value.astype(jnp.bfloat16)
    return high, (value - high.astype(jnp.float32)).astype(jnp.bfloat16)


def stacked(value):
    return jnp.concatenate(split(value), axis=0)


def matmul(left, right, over):
    rows = left.shape[0] // 2
    total = None
    for part in reversed(split(right)):
        both = lax.dot_general(
            left, part, (((1,), (over,)), ((), ())), preferred_element_type=jnp.float32
        )
        both = both[rows:] + both[:rows]
        total = both if total is None else total + both
    return total


def times_rows(left, *refs, columns=slice(None)):
    left = stacked(left)
    count = refs[0].shape[0]
    ends = count * len(refs)
    results = []
    for start in range(0, ends, TILE):
        stop = min(start + TILE, ends)
        blocks = []
        for i, ref in enumerate(refs):
            low, high = max(start - i * count, 0), min(stop - i * count, count)
            if low < high:
                blocks.append(ref[low:high, columns])
        results.append(matmul(left, jnp.concatenate(blocks, axis=0), 1))
    return jnp.concatenate(results, axis=1)


def times(left, ref):
    left = stacked(left)
    width = ref.shape[1]
    columns = [matmul(left, ref[:, n : min(n + TILE, width)], 0) for n in range(0, width, TILE)]
    return jnp.concatenate(columns, axis=1)


def in_order(pieces, own):
    bit = 1
    while bit < len(pieces):
        swap = (own & bit) != 0
        pieces = [jnp.where(swap, pieces[j ^ bit], pieces[j]) for j in range(len(pieces))]
        bit *= 2
    return pieces


def joined(refs, axis="rec"):
    own = lax.axis_index(axis) if len(refs) > 1 else 0
    return jnp.concatenate(in_order([ref[...] for ref in refs], own), axis=1)


def store_rows(ref, value):
    half = value.shape[1] // 2
    swap = lax.axis_index("blk") == 1
    own, other = value[:, :half], value[:, half:]
    ref[...] = jnp.concatenate([jnp.where(swap, other, own), jnp.where(swap, own, other)], axis=1)


def call(kernel, shapes, *groups, cost=0, late=None):
    flat = [value for group in groups for value in group]

    def body(*refs):
        at, parts = 0, []
        for group in groups:
            parts.append(refs[at : at + len(group)])
            at += len(group)
        if late is None:
            kernel(*parts, *refs[at:])
            return
        buffer, sem = refs[-2:]
        copy = pltpu.make_async_copy(refs[at], buffer, sem)
        copy.start()
        kernel(*parts, *refs[at + 1 : -2], copy, buffer)

    out = [jax.ShapeDtypeStruct(shape, jnp.float32) for shape in shapes]
    last = [] if late is None else [pltpu.with_memory_space_constraint(late, pltpu.HBM)]
    return pl.pallas_call(
        body,
        in_specs=[VMEM] * len(flat) + [pl.BlockSpec(memory_space=pltpu.HBM)] * len(last),
        out_specs=[VMEM] * len(out),
        out_shape=out,
        compiler_params=pltpu.CompilerParams(vmem_limit_bytes=24 << 20),
        cost_estimate=pl.CostEstimate(flops=0, bytes_accessed=cost, transcendentals=0) if cost else None,
        scratch_shapes=[*(pltpu.VMEM(x.shape, x.dtype) for x in last), *[pltpu.SemaphoreType.DMA] * len(last)],
    )(*flat, *last)


def staged(*matrices, after):
    held = lax.optimization_barrier([*matrices, *after])[: len(matrices)]
    held = [pltpu.with_memory_space_constraint(matrix, pltpu.HBM) for matrix in held]
    count = len(held)
    rows = held[0].shape[0]
    ends = [0]
    for matrix in held:
        ends.append(ends[-1] + matrix.shape[1])

    def body(*refs):
        out, sems = refs[count:]
        copies = []
        for i in range(count):
            for j in range(2):
                part = pl.ds(j * (rows // 2), rows // 2)
                copies.append(
                    pltpu.make_async_copy(
                        refs[i].at[part, :],
                        out.at[part, ends[i] : ends[i + 1]],
                        sems.at[2 * i + j],
                    )
                )
        for copy in copies:
            copy.start()
        for copy in copies:
            copy.wait()

    return pl.pallas_call(
        body,
        in_specs=[pl.BlockSpec(memory_space=pltpu.HBM)] * count,
        out_specs=VMEM,
        out_shape=pltpu.VMEM((rows, ends[-1]), jnp.float32),
        scratch_shapes=[pltpu.SemaphoreType.DMA((2 * count,))],
        compiler_params=pltpu.CompilerParams(vmem_limit_bytes=24 << 20),
    )(*held)


def forces_kernel(swap_chips, pieces, matrices, mine, theirs, copy, below):
    (rows,) = matrices
    faces = mine.shape[2]
    inner = rows.shape[1] - faces
    inverse = rows.at[:, :inner]
    above = rows.at[:, inner:]
    if swap_chips:
        chips = len(pieces) // 2
        core = lax.axis_index("blk")
        sets = [in_order([pieces[2 * j][...], pieces[2 * j + 1][...]], core) for j in range(chips)]
        sets = [jnp.concatenate(pair, axis=1) for pair in sets]
        full = jnp.concatenate(in_order(sets, lax.axis_index("rec")), axis=1)
    else:
        full = pieces[0][...]
    part = times_rows(full, inverse)
    half = part.shape[0] // 2
    second = lax.axis_index("blk") == 1
    for i, matrix in enumerate((above, below)):
        if i == 1:
            copy.wait()
        force = times(part, matrix)
        mine[i] = jnp.where(second, force[half:], force[:half])
        theirs[i] = jnp.where(second, force[:half], force[half:])


def fetched(kernel, shapes, arrays, *held):
    count = len(arrays)
    arrays = [pltpu.with_memory_space_constraint(value, pltpu.HBM) for value in arrays]

    def body(*refs):
        sources, rest = refs[:count], refs[count:-1]
        buffers, sems = rest[len(held) + len(shapes) :], refs[-1]
        copies = [
            pltpu.make_async_copy(source, buffer, sems.at[i])
            for i, (source, buffer) in enumerate(zip(sources, buffers))
        ]
        for copy in copies:
            copy.start()
        for copy in copies:
            copy.wait()
        kernel(buffers, rest[: len(held)], *rest[len(held) : len(held) + len(shapes)])

    out = [jax.ShapeDtypeStruct(shape, jnp.float32) for shape in shapes]
    return pl.pallas_call(
        body,
        in_specs=[pl.BlockSpec(memory_space=pltpu.HBM)] * count + [VMEM] * len(held),
        out_specs=[VMEM] * len(out),
        out_shape=out,
        scratch_shapes=[pltpu.VMEM(value.shape, value.dtype) for value in arrays]
        + [pltpu.SemaphoreType.DMA((count,))],
        compiler_params=pltpu.CompilerParams(vmem_limit_bytes=24 << 20),
    )(*arrays, *held)


def newmark_load(mass, pattern, disp, vel, acc, ground):
    return mass[...] * (disp[...] + 2.0 * vel[...] + acc[...] - pattern[...] * ground)


def load_int_kernel(fetched_refs, held, load, ground_out):
    ids, table, *arrays = fetched_refs
    records, library = ids.shape[1], table.shape[1]
    shape = (records, records)
    diagonal = lax.broadcasted_iota(jnp.int32, shape, 0) == lax.broadcasted_iota(jnp.int32, shape, 1)
    row = jnp.broadcast_to(ids[...].astype(jnp.float32), shape)
    column = jnp.sum(jnp.where(diagonal, row, 0.0), axis=1, keepdims=True)
    index = lax.broadcasted_iota(jnp.int32, (records, library), 1).astype(jnp.float32)
    ground = jnp.sum(jnp.where(column == index, table[...], 0.0), axis=1, keepdims=True)
    ground_out[...] = jnp.broadcast_to(ground, ground_out.shape)
    load[...] = newmark_load(*arrays, ground)


def load_face_kernel(fetched_refs, held, mine, theirs):
    load = newmark_load(*fetched_refs, held[0][:, :1])
    half = load.shape[0] // 2
    second = lax.axis_index("blk") == 1
    mine[...] = jnp.where(second, load[half:], load[:half])
    theirs[...] = jnp.where(second, load[:half], load[half:])


def records_kernel(whole, mine, theirs):
    value = whole[0][...]
    half = value.shape[0] // 2
    second = lax.axis_index("blk") == 1
    mine[...] = jnp.where(second, value[half:], value[:half])
    theirs[...] = jnp.where(second, value[:half], value[half:])


def by_core(own, other, axis):
    second = lax.axis_index("blk") == 1
    return jnp.concatenate([jnp.where(second, other, own), jnp.where(second, own, other)], axis=axis)


def less_in(stories_of, value, forces):
    story, count = lax.axis_index("story"), lax.axis_size("story")
    there = (lax.rem(story, 2) == stories_of) & (story + 1 < count)
    for force in forces:
        value = jnp.where(there, value - force[...], value)
    return value


def condensed_kernel(load, forces, even, out):
    value = by_core(load[0][...], load[1][...], 1)
    for force in forces:
        value = value - force[...]
    out[...] = less_in(0, value, even)


def odd_kernel(value, odd, out):
    out[...] = less_in(1, value[0][...], odd)


def halves_kernel(whole, mine, theirs):
    value = whole[0][...]
    half = value.shape[1] // 2
    second = lax.axis_index("blk") == 1
    mine[...] = jnp.where(second, value[:, half:], value[:, :half])
    theirs[...] = jnp.where(second, value[:, :half], value[:, half:])


def outputs_kernel(halves, before, new_disp, new_vel, new_acc):
    disp, vel, acc = before
    value = by_core(halves[0][...], halves[1][...], 0)
    change = value - disp[...] - 2.0 * vel[...] - acc[...]
    new_disp[...] = value
    new_vel[...] = vel[...] + acc[...] + change
    new_acc[...] = change


def chunks_kernel(inputs, *outs):
    mine, came = inputs
    chips = len(outs) // 2
    for i in range(2):
        total = mine[i] + came[i]
        width = total.shape[1] // chips
        pieces = [total[:, j * width : (j + 1) * width] for j in range(chips)]
        for j, piece in enumerate(in_order(pieces, lax.axis_index("rec"))):
            outs[i * chips + j][...] = piece


def from_chip(count, j):
    def columns(width):
        if count == 1:
            return slice(None)
        start = (lax.axis_index("rec") ^ j) * width
        return pl.ds(pl.multiple_of(start, 128), width)

    return columns


def plus(value, sofar):
    return value + sofar[0][...] if sofar else value


def part_kernel(columns, story, piece, rows, sofar, out):
    def product():
        value = piece[0][...]
        out[...] = plus(times_rows(value, *rows, columns=columns(value.shape[1])), sofar)

    if story is None:
        product()
    else:
        pl.when(lax.axis_index("story") == story)(product)


def step_kernel(columns, story, piece, rows, sofar, terms, out):
    first, latest = terms

    @pl.when(lax.axis_index("story") == story)
    def _():
        value = piece[0][...]
        value = plus(times_rows(value, *rows, columns=columns(value.shape[1])), sofar)
        store_rows(out, value)
        out[...] = first[...] - out[...]

    @pl.when(lax.axis_index("story") != story)
    def _():
        out[...] = latest[...]


def end_kernel(columns, piece, rows, sofar, out):
    value = piece[0][...]
    store_rows(out, plus(times_rows(value, *rows, columns=columns(value.shape[1])), sofar))


def coupled_kernel(columns, final, load, pair, rows, sofar, out):
    even, odd = pair
    story = lax.axis_index("story")

    def finish(value):
        if final:
            store_rows(out, value)
            out[...] = by_core(load[0][...], load[1][...], 1) - out[...]
        else:
            out[...] = value

    @pl.when(story == 0)
    def _():
        finish(sofar[0][...])

    @pl.when(story > 0)
    def _():
        value = jnp.where(lax.rem(story, 2) == 1, even[...], odd[...])
        finish(plus(times_rows(value, *rows, columns=columns(value.shape[1])), sofar))


def last_kernel(columns, piece, rows, sofar, mine, theirs):
    value = piece[0][...]
    value = plus(times_rows(value, *rows, columns=columns(value.shape[1])), sofar)
    half = value.shape[1] // 2
    mine[...] = value[:, :half]
    theirs[...] = value[:, half:]


def partial_sums(story, shape, pieces, rows):
    sofar = []
    for j, piece in enumerate(pieces[:-1]):
        kernel = functools.partial(part_kernel, from_chip(len(pieces), j), story)
        sofar = call(kernel, shape, [piece], rows, sofar, cost=4 << 20)
    return [pieces[-1]], rows, sofar


class Moves:
    def __init__(self):
        self.stories = lax.axis_size("story")
        self.chips = lax.axis_size("rec")
        self.cores = lax.axis_size("blk")
        assert self.cores == 2 and self.chips & (self.chips - 1) == 0
        self.s = lax.axis_index("story")
        self.r = lax.axis_index("rec")
        self.b = lax.axis_index("blk")

    def permute(self, value, target):
        pairs = []
        for s in range(self.stories):
            for r in range(self.chips):
                for b in range(self.cores):
                    t, q, c = target(s, r, b)
                    pairs.append(
                        (
                            (s * self.chips + r) * self.cores + b,
                            (t * self.chips + q) * self.cores + c,
                        )
                    )
        return lax.ppermute(value, AXES, pairs)

    def core(self, value):
        return self.permute(value, lambda s, r, b: (s, r, 1 - b))

    def chip(self, value, j):
        return self.permute(value, lambda s, r, b: (s, r ^ j, b))

    def story(self, value, parity, j):
        def target(s, r, b):
            t = s ^ 1 if parity == 0 else ((s - 1) ^ 1) + 1
            if t < 0 or t >= self.stories:
                return (s, r ^ 1, b) if self.chips > 1 else (s, r, 1 - b)
            return t, r ^ j, b

        return self.permute(value, target)

    def by_core(self, own, other, axis):
        first = jnp.where(self.b == 0, own, other)
        second = jnp.where(self.b == 0, other, own)
        return jnp.concatenate([first, second], axis=axis)

    def by_chip(self, pieces, axis=1):
        bit = 1
        while bit < self.chips:
            swap = (self.r & bit) != 0
            pieces = [jnp.where(swap, pieces[j ^ bit], pieces[j]) for j in range(self.chips)]
            bit *= 2
        return jnp.concatenate(pieces, axis=axis)

    def pieces(self, pieces):
        return pieces if pieces[0].shape[1] % 128 == 0 else [self.by_chip(pieces)]

    def shift(self, value, step, j):
        pairs = []
        for s in range(self.stories):
            if not 0 <= s + step < self.stories:
                continue
            for r in range(self.chips):
                for b in range(self.cores):
                    pairs.append(
                        (
                            (s * self.chips + r) * self.cores + b,
                            ((s + step) * self.chips + (r ^ j)) * self.cores + b,
                        )
                    )
        return lax.ppermute(value, AXES, pairs)

    def gather_chips(self, value):
        return self.pieces([value] + [self.chip(value, j) for j in range(1, self.chips)])

    def gather_story(self, value, parity):
        return self.pieces([self.story(value, parity, j) for j in range(self.chips)])


def shards(
    record_ids,
    ground_table,
    mass_int,
    mass_face,
    pattern_int,
    pattern_face,
    disp_int,
    vel_int,
    acc_int,
    disp_face,
    vel_face,
    acc_face,
    interior_inverse,
    couple_below,
    couple_above,
    lower,
    pivot,
    upper,
):
    mv = Moves()
    library, records = ground_table.shape[0], record_ids.shape[0]
    half = records // 2
    cube_int = [value[0].T for value in (disp_int, vel_int, acc_int)]
    cube_face = [value[0].T for value in (disp_face, vel_face, acc_face)]
    own_int, own_face = cube_int[0].shape[1], cube_face[0].shape[1]
    load_int, ground = fetched(
        load_int_kernel,
        [(records, own_int), (records, 128)],
        [record_ids.reshape(1, records), ground_table.reshape(1, library), mass_int, pattern_int]
        + cube_int,
    )
    rows_int, rows_face = 2 * own_int, 2 * own_face
    faces = couple_above.shape[2]

    def others(matrix, after):
        return mv.core(lax.optimization_barrier([matrix, *after])[0])

    lower_other = mv.core(lower[0])
    across = [mv.chip(load_int, j) for j in range(1, mv.chips)]
    phase_rows = staged(interior_inverse[0], couple_above[0], after=[load_int])
    phase_rows, *across = lax.optimization_barrier([phase_rows, *across])
    beside = [mv.core(piece) for piece in [load_int] + across]
    pieces = [piece for pair in zip([load_int] + across, beside) for piece in pair]
    aligned = load_int.shape[1] % 128 == 0
    if not aligned:
        pieces = [
            mv.by_chip([mv.by_core(pieces[2 * j], pieces[2 * j + 1], 1) for j in range(mv.chips)])
        ]
    mine, theirs = call(
        functools.partial(forces_kernel, aligned),
        [(2, half, faces)] * 2,
        pieces,
        [phase_rows],
        late=couple_below[0],
    )
    chunks = call(
        chunks_kernel,
        [(half, faces // mv.chips)] * (2 * mv.chips),
        [mine, mv.core(theirs)],
    )
    ground, _ = lax.optimization_barrier([ground, chunks[0]])
    mine_face, theirs_face = fetched(
        load_face_kernel, [(half, own_face)] * 2, [mass_face, pattern_face] + cube_face, ground
    )
    load_late, _ = lax.optimization_barrier([load_int, chunks[0]])
    mine_int, theirs_int = call(records_kernel, [(half, own_int)] * 2, [load_late])
    halves = lax.optimization_barrier([mv.core(theirs_face), mv.core(theirs_int)])
    load_face_half, load_int_half = [mine_face, halves[0]], [mine_int, halves[1]]
    below_parts = chunks[mv.chips :]
    even = [mv.story(below_parts[j], 0, j) for j in range(mv.chips)]
    forces = [chunks[0]] + [mv.chip(chunks[j], j) for j in range(1, mv.chips)]
    shape = [(half, rows_face)]
    (condensed,) = call(condensed_kernel, shape, load_face_half, forces, even)
    odd = [mv.story(below_parts[j], 1, j) for j in range(mv.chips)]

    forward = condensed
    pivot_other = others(pivot[0], [condensed])
    for k in range(1, mv.stories):
        came = mv.gather_story(forward, (k - 1) % 2)
        if k == 1:
            (condensed,) = call(odd_kernel, shape, [condensed], odd)
        if k == min(2, mv.stories - 1):
            upper_other = others(upper[0], [pivot_other, forward])
            came[-1], pivot_other = lax.optimization_barrier([came[-1], pivot_other])
        if k == mv.stories - 1:
            above_other = others(couple_above[0], [upper_other, forward])
            came[-1], upper_other = lax.optimization_barrier([came[-1], upper_other])
        (forward,) = call(
            functools.partial(step_kernel, from_chip(len(came), len(came) - 1), k),
            shape,
            *partial_sums(k, shape, came, [lower[0], lower_other]),
            [condensed, forward],
        )
    came = mv.gather_chips(forward)
    (pivoted,) = call(
        functools.partial(end_kernel, from_chip(len(came), len(came) - 1)),
        shape,
        *partial_sums(None, shape, came, [pivot[0], pivot_other]),
    )

    shape_int = [(half, rows_int)]
    face = pivoted
    for k in range(mv.stories - 2, -1, -1):
        came = mv.gather_story(face, k % 2)
        if k == mv.stories - 2:
            below_other = others(couple_below[0], [above_other, face])
            came[-1], above_other = lax.optimization_barrier([came[-1], above_other])
        if k == max(mv.stories - 3, 0):
            inverse_other = others(interior_inverse[0], [below_other, face])
            came[-1], below_other = lax.optimization_barrier([came[-1], below_other])
        (face,) = call(
            functools.partial(step_kernel, from_chip(len(came), len(came) - 1), k),
            shape,
            *partial_sums(k, shape, came, [upper[0], upper_other]),
            [pivoted, face],
        )

    here = mv.gather_chips(face)
    even = mv.gather_story(face, 0)
    odd = mv.gather_story(face, 1)
    even[-1], inverse_other = lax.optimization_barrier([even[-1], inverse_other])
    rows = [couple_above[0], above_other]
    sofar = []
    for j, piece in enumerate(here):
        kernel = functools.partial(part_kernel, from_chip(len(here), j), None)
        sofar = call(kernel, shape_int, [piece], rows, sofar, cost=4 << 20)
    rows = [couple_below[0], below_other]
    for j, pair in enumerate(zip(even, odd)):
        final = j == len(even) - 1
        sofar = call(
            functools.partial(coupled_kernel, from_chip(len(even), j), final),
            shape_int,
            load_int_half if final else [],
            list(pair),
            rows,
            sofar,
            cost=4 << 20,
        )
    (reduced,) = sofar

    mine, theirs = call(halves_kernel, [(half, own_face)] * 2, [face])
    new_face = call(
        outputs_kernel, [(records, own_face)] * 3, [mine, mv.core(theirs)], cube_face
    )
    came = mv.gather_chips(reduced)
    came[-1], f0, f1, f2 = lax.optimization_barrier([came[-1], *new_face])
    mine, theirs = call(
        functools.partial(last_kernel, from_chip(len(came), len(came) - 1)),
        [(half, own_int)] * 2,
        *partial_sums(None, shape_int, came, [interior_inverse[0], inverse_other]),
    )
    new_int = call(
        outputs_kernel, [(records, own_int)] * 3, [mine, mv.core(theirs)], cube_int
    )
    new_face = [f0, f1, f2]
    return tuple(out.T[None] for out in (*new_int, *new_face))


def solution(mesh):
    whole, rows, cube = P(), P(("groups", "story"), ("rec", "blk")), P(("groups", "story"), ("rec", "blk"), None)
    in_specs = (P("groups"), whole) + (rows,) * 4 + (cube,) * 12
    return jax.shard_map(shards, mesh=mesh, in_specs=in_specs, out_specs=(cube,) * 6, check_vma=False)
```

```python
import functools

import jax
import jax.numpy as jnp
from jax import lax
from jax.experimental import pallas as pl
from jax.experimental.pallas import tpu as pltpu
from jax.sharding import PartitionSpec as P

AXES = ("story", "rec", "blk")
TILE = 256
VMEM = pl.BlockSpec(memory_space=pltpu.VMEM)


def split(value):
    high = value.astype(jnp.bfloat16)
    return high, (value - high.astype(jnp.float32)).astype(jnp.bfloat16)


def stacked(value):
    return jnp.concatenate(split(value), axis=0)


def matmul(left, right, over):
    rows = left.shape[0] // 2
    total = None
    for part in reversed(split(right)):
        both = lax.dot_general(
            left, part, (((1,), (over,)), ((), ())), preferred_element_type=jnp.float32
        )
        both = both[rows:] + both[:rows]
        total = both if total is None else total + both
    return total


def times_rows(left, *refs, columns=slice(None)):
    left = stacked(left)
    count = refs[0].shape[0]
    ends = count * len(refs)
    results = []
    for start in range(0, ends, TILE):
        stop = min(start + TILE, ends)
        blocks = []
        for i, ref in enumerate(refs):
            low, high = max(start - i * count, 0), min(stop - i * count, count)
            if low < high:
                blocks.append(ref[low:high, columns])
        results.append(matmul(left, jnp.concatenate(blocks, axis=0), 1))
    return jnp.concatenate(results, axis=1)


def times(left, ref):
    left = stacked(left)
    width = ref.shape[1]
    columns = [matmul(left, ref[:, n : min(n + TILE, width)], 0) for n in range(0, width, TILE)]
    return jnp.concatenate(columns, axis=1)


def in_order(pieces, own):
    bit = 1
    while bit < len(pieces):
        swap = (own & bit) != 0
        pieces = [jnp.where(swap, pieces[j ^ bit], pieces[j]) for j in range(len(pieces))]
        bit *= 2
    return pieces


def joined(refs, axis="rec"):
    own = lax.axis_index(axis) if len(refs) > 1 else 0
    return jnp.concatenate(in_order([ref[...] for ref in refs], own), axis=1)


def store_rows(ref, value):
    half = value.shape[1] // 2
    swap = lax.axis_index("blk") == 1
    own, other = value[:, :half], value[:, half:]
    ref[...] = jnp.concatenate([jnp.where(swap, other, own), jnp.where(swap, own, other)], axis=1)


def call(kernel, shapes, *groups, cost=0, late=None):
    flat = [value for group in groups for value in group]

    def body(*refs):
        at, parts = 0, []
        for group in groups:
            parts.append(refs[at : at + len(group)])
            at += len(group)
        if late is None:
            kernel(*parts, *refs[at:])
            return
        buffer, sem = refs[-2:]
        copy = pltpu.make_async_copy(refs[at], buffer, sem)
        copy.start()
        kernel(*parts, *refs[at + 1 : -2], copy, buffer)

    out = [jax.ShapeDtypeStruct(shape, jnp.float32) for shape in shapes]
    last = [] if late is None else [pltpu.with_memory_space_constraint(late, pltpu.HBM)]
    return pl.pallas_call(
        body,
        in_specs=[VMEM] * len(flat) + [pl.BlockSpec(memory_space=pltpu.HBM)] * len(last),
        out_specs=[VMEM] * len(out),
        out_shape=out,
        compiler_params=pltpu.CompilerParams(vmem_limit_bytes=24 << 20),
        cost_estimate=pl.CostEstimate(flops=0, bytes_accessed=cost, transcendentals=0) if cost else None,
        scratch_shapes=[*(pltpu.VMEM(x.shape, x.dtype) for x in last), *[pltpu.SemaphoreType.DMA] * len(last)],
    )(*flat, *last)


def staged(*matrices, after):
    held = lax.optimization_barrier([*matrices, *after])[: len(matrices)]
    held = [pltpu.with_memory_space_constraint(matrix, pltpu.HBM) for matrix in held]
    count = len(held)
    rows = held[0].shape[0]
    ends = [0]
    for matrix in held:
        ends.append(ends[-1] + matrix.shape[1])

    def body(*refs):
        out, sems = refs[count:]
        copies = []
        for i in range(count):
            for j in range(2):
                part = pl.ds(j * (rows // 2), rows // 2)
                copies.append(
                    pltpu.make_async_copy(
                        refs[i].at[part, :],
                        out.at[part, ends[i] : ends[i + 1]],
                        sems.at[2 * i + j],
                    )
                )
        for copy in copies:
            copy.start()
        for copy in copies:
            copy.wait()

    return pl.pallas_call(
        body,
        in_specs=[pl.BlockSpec(memory_space=pltpu.HBM)] * count,
        out_specs=VMEM,
        out_shape=pltpu.VMEM((rows, ends[-1]), jnp.float32),
        scratch_shapes=[pltpu.SemaphoreType.DMA((2 * count,))],
        compiler_params=pltpu.CompilerParams(vmem_limit_bytes=24 << 20),
    )(*held)


def forces_kernel(swap_chips, pieces, matrices, mine, theirs, copy, below):
    (rows,) = matrices
    faces = mine.shape[2]
    inner = rows.shape[1] - faces
    inverse = rows.at[:, :inner]
    above = rows.at[:, inner:]
    if swap_chips:
        chips = len(pieces) // 2
        core = lax.axis_index("blk")
        sets = [in_order([pieces[2 * j][...], pieces[2 * j + 1][...]], core) for j in range(chips)]
        sets = [jnp.concatenate(pair, axis=1) for pair in sets]
        full = jnp.concatenate(in_order(sets, lax.axis_index("rec")), axis=1)
    else:
        full = pieces[0][...]
    part = times_rows(full, inverse)
    half = part.shape[0] // 2
    second = lax.axis_index("blk") == 1
    for i, matrix in enumerate((above, below)):
        if i == 1:
            copy.wait()
        force = times(part, matrix)
        mine[i] = jnp.where(second, force[half:], force[:half])
        theirs[i] = jnp.where(second, force[:half], force[half:])


def fetched(kernel, shapes, arrays, *held):
    count = len(arrays)
    arrays = [pltpu.with_memory_space_constraint(value, pltpu.HBM) for value in arrays]

    def body(*refs):
        sources, rest = refs[:count], refs[count:-1]
        buffers, sems = rest[len(held) + len(shapes) :], refs[-1]
        copies = [
            pltpu.make_async_copy(source, buffer, sems.at[i])
            for i, (source, buffer) in enumerate(zip(sources, buffers))
        ]
        for copy in copies:
            copy.start()
        for copy in copies:
            copy.wait()
        kernel(buffers, rest[: len(held)], *rest[len(held) : len(held) + len(shapes)])

    out = [jax.ShapeDtypeStruct(shape, jnp.float32) for shape in shapes]
    return pl.pallas_call(
        body,
        in_specs=[pl.BlockSpec(memory_space=pltpu.HBM)] * count + [VMEM] * len(held),
        out_specs=[VMEM] * len(out),
        out_shape=out,
        scratch_shapes=[pltpu.VMEM(value.shape, value.dtype) for value in arrays]
        + [pltpu.SemaphoreType.DMA((count,))],
        compiler_params=pltpu.CompilerParams(vmem_limit_bytes=24 << 20),
    )(*arrays, *held)


def newmark_load(mass, pattern, disp, vel, acc, ground):
    return mass[...] * (disp[...] + 2.0 * vel[...] + acc[...] - pattern[...] * ground)


def load_int_kernel(fetched_refs, held, load, ground_out):
    ids, table, *arrays = fetched_refs
    records, library = ids.shape[1], table.shape[1]
    shape = (records, records)
    diagonal = lax.broadcasted_iota(jnp.int32, shape, 0) == lax.broadcasted_iota(jnp.int32, shape, 1)
    row = jnp.broadcast_to(ids[...].astype(jnp.float32), shape)
    column = jnp.sum(jnp.where(diagonal, row, 0.0), axis=1, keepdims=True)
    index = lax.broadcasted_iota(jnp.int32, (records, library), 1).astype(jnp.float32)
    ground = jnp.sum(jnp.where(column == index, table[...], 0.0), axis=1, keepdims=True)
    ground_out[...] = jnp.broadcast_to(ground, ground_out.shape)
    load[...] = newmark_load(*arrays, ground)


def load_face_kernel(fetched_refs, held, mine, theirs):
    load = newmark_load(*fetched_refs, held[0][:, :1])
    half = load.shape[0] // 2
    second = lax.axis_index("blk") == 1
    mine[...] = jnp.where(second, load[half:], load[:half])
    theirs[...] = jnp.where(second, load[:half], load[half:])


def records_kernel(whole, mine, theirs):
    value = whole[0][...]
    half = value.shape[0] // 2
    second = lax.axis_index("blk") == 1
    mine[...] = jnp.where(second, value[half:], value[:half])
    theirs[...] = jnp.where(second, value[:half], value[half:])


def by_core(own, other, axis):
    second = lax.axis_index("blk") == 1
    return jnp.concatenate([jnp.where(second, other, own), jnp.where(second, own, other)], axis=axis)


def condensed_kernel(load, forces, out):
    value = by_core(load[0][...], load[1][...], 1)
    for force in forces:
        value = value - force[...]
    out[...] = value


def halves_kernel(whole, mine, theirs):
    value = whole[0][...]
    half = value.shape[1] // 2
    second = lax.axis_index("blk") == 1
    mine[...] = jnp.where(second, value[:, half:], value[:, :half])
    theirs[...] = jnp.where(second, value[:, :half], value[:, half:])


def outputs_kernel(halves, before, new_disp, new_vel, new_acc):
    disp, vel, acc = before
    value = by_core(halves[0][...], halves[1][...], 0)
    change = value - disp[...] - 2.0 * vel[...] - acc[...]
    new_disp[...] = value
    new_vel[...] = vel[...] + acc[...] + change
    new_acc[...] = change


def chunks_kernel(inputs, *outs):
    mine, came = inputs
    chips = len(outs) // 2
    for i in range(2):
        total = mine[i] + came[i]
        width = total.shape[1] // chips
        pieces = [total[:, j * width : (j + 1) * width] for j in range(chips)]
        for j, piece in enumerate(in_order(pieces, lax.axis_index("rec"))):
            outs[i * chips + j][...] = piece


def from_chip(count, j):
    def columns(width):
        if count == 1:
            return slice(None)
        start = (lax.axis_index("rec") ^ j) * width
        return pl.ds(pl.multiple_of(start, 128), width)

    return columns


def plus(value, sofar):
    return value + sofar[0][...] if sofar else value


def part_kernel(columns, story, piece, rows, sofar, out):
    def product():
        value = piece[0][...]
        out[...] = plus(times_rows(value, *rows, columns=columns(value.shape[1])), sofar)

    if story is None:
        product()
    else:
        pl.when(lax.axis_index("story") == story)(product)


def step_kernel(columns, story, piece, rows, sofar, terms, out):
    first, latest = terms

    @pl.when(lax.axis_index("story") == story)
    def _():
        value = piece[0][...]
        value = plus(times_rows(value, *rows, columns=columns(value.shape[1])), sofar)
        store_rows(out, value)
        out[...] = first[...] - out[...]

    @pl.when(lax.axis_index("story") != story)
    def _():
        out[...] = latest[...]


def end_kernel(columns, piece, rows, sofar, out):
    value = piece[0][...]
    store_rows(out, plus(times_rows(value, *rows, columns=columns(value.shape[1])), sofar))


def coupled_kernel(columns, final, load, pair, rows, sofar, out):
    even, odd = pair
    story = lax.axis_index("story")

    def finish(value):
        if final:
            store_rows(out, value)
            out[...] = by_core(load[0][...], load[1][...], 1) - out[...]
        else:
            out[...] = value

    @pl.when(story == 0)
    def _():
        finish(sofar[0][...])

    @pl.when(story > 0)
    def _():
        value = jnp.where(lax.rem(story, 2) == 1, even[...], odd[...])
        finish(plus(times_rows(value, *rows, columns=columns(value.shape[1])), sofar))


def last_kernel(columns, piece, rows, sofar, mine, theirs):
    value = piece[0][...]
    value = plus(times_rows(value, *rows, columns=columns(value.shape[1])), sofar)
    half = value.shape[1] // 2
    mine[...] = value[:, :half]
    theirs[...] = value[:, half:]


def partial_sums(story, shape, pieces, rows):
    sofar = []
    for j, piece in enumerate(pieces[:-1]):
        kernel = functools.partial(part_kernel, from_chip(len(pieces), j), story)
        sofar = call(kernel, shape, [piece], rows, sofar, cost=4 << 20)
    return [pieces[-1]], rows, sofar


class Moves:
    def __init__(self):
        self.stories = lax.axis_size("story")
        self.chips = lax.axis_size("rec")
        self.cores = lax.axis_size("blk")
        assert self.cores == 2 and self.chips & (self.chips - 1) == 0
        self.s = lax.axis_index("story")
        self.r = lax.axis_index("rec")
        self.b = lax.axis_index("blk")

    def permute(self, value, target):
        pairs = []
        for s in range(self.stories):
            for r in range(self.chips):
                for b in range(self.cores):
                    t, q, c = target(s, r, b)
                    pairs.append(
                        (
                            (s * self.chips + r) * self.cores + b,
                            (t * self.chips + q) * self.cores + c,
                        )
                    )
        return lax.ppermute(value, AXES, pairs)

    def core(self, value):
        return self.permute(value, lambda s, r, b: (s, r, 1 - b))

    def chip(self, value, j):
        return self.permute(value, lambda s, r, b: (s, r ^ j, b))

    def story(self, value, parity, j):
        def target(s, r, b):
            t = s ^ 1 if parity == 0 else ((s - 1) ^ 1) + 1
            if t < 0 or t >= self.stories:
                return (s, r ^ 1, b) if self.chips > 1 else (s, r, 1 - b)
            return t, r ^ j, b

        return self.permute(value, target)

    def by_core(self, own, other, axis):
        first = jnp.where(self.b == 0, own, other)
        second = jnp.where(self.b == 0, other, own)
        return jnp.concatenate([first, second], axis=axis)

    def by_chip(self, pieces, axis=1):
        bit = 1
        while bit < self.chips:
            swap = (self.r & bit) != 0
            pieces = [jnp.where(swap, pieces[j ^ bit], pieces[j]) for j in range(self.chips)]
            bit *= 2
        return jnp.concatenate(pieces, axis=axis)

    def pieces(self, pieces):
        return pieces if pieces[0].shape[1] % 128 == 0 else [self.by_chip(pieces)]

    def shift(self, value, step, j):
        pairs = []
        for s in range(self.stories):
            if not 0 <= s + step < self.stories:
                continue
            for r in range(self.chips):
                for b in range(self.cores):
                    pairs.append(
                        (
                            (s * self.chips + r) * self.cores + b,
                            ((s + step) * self.chips + (r ^ j)) * self.cores + b,
                        )
                    )
        return lax.ppermute(value, AXES, pairs)

    def gather_chips(self, value):
        return self.pieces([value] + [self.chip(value, j) for j in range(1, self.chips)])

    def gather_story(self, value, parity):
        return self.pieces([self.story(value, parity, j) for j in range(self.chips)])


def shards(
    record_ids,
    ground_table,
    mass_int,
    mass_face,
    pattern_int,
    pattern_face,
    disp_int,
    vel_int,
    acc_int,
    disp_face,
    vel_face,
    acc_face,
    interior_inverse,
    couple_below,
    couple_above,
    lower,
    pivot,
    upper,
):
    mv = Moves()
    library, records = ground_table.shape[0], record_ids.shape[0]
    half = records // 2
    cube_int = [value[0].T for value in (disp_int, vel_int, acc_int)]
    cube_face = [value[0].T for value in (disp_face, vel_face, acc_face)]
    own_int, own_face = cube_int[0].shape[1], cube_face[0].shape[1]
    load_int, ground = fetched(
        load_int_kernel,
        [(records, own_int), (records, 128)],
        [record_ids.reshape(1, records), ground_table.reshape(1, library), mass_int, pattern_int]
        + cube_int,
    )
    rows_int, rows_face = 2 * own_int, 2 * own_face
    faces = couple_above.shape[2]

    def others(matrix, after):
        return mv.core(lax.optimization_barrier([matrix, *after])[0])

    lower_other = mv.core(lower[0])
    across = [mv.chip(load_int, j) for j in range(1, mv.chips)]
    phase_rows = staged(interior_inverse[0], couple_above[0], after=[load_int])
    phase_rows, *across = lax.optimization_barrier([phase_rows, *across])
    beside = [mv.core(piece) for piece in [load_int] + across]
    pieces = [piece for pair in zip([load_int] + across, beside) for piece in pair]
    aligned = load_int.shape[1] % 128 == 0
    if not aligned:
        pieces = [
            mv.by_chip([mv.by_core(pieces[2 * j], pieces[2 * j + 1], 1) for j in range(mv.chips)])
        ]
    mine, theirs = call(
        functools.partial(forces_kernel, aligned),
        [(2, half, faces)] * 2,
        pieces,
        [phase_rows],
        late=couple_below[0],
    )
    chunks = call(
        chunks_kernel,
        [(half, faces // mv.chips)] * (2 * mv.chips),
        [mine, mv.core(theirs)],
    )
    ground, _ = lax.optimization_barrier([ground, chunks[0]])
    mine_face, theirs_face = fetched(
        load_face_kernel, [(half, own_face)] * 2, [mass_face, pattern_face] + cube_face, ground
    )
    load_late, _ = lax.optimization_barrier([load_int, chunks[0]])
    mine_int, theirs_int = call(records_kernel, [(half, own_int)] * 2, [load_late])
    halves = lax.optimization_barrier([mv.core(theirs_face), mv.core(theirs_int)])
    load_face_half, load_int_half = [mine_face, halves[0]], [mine_int, halves[1]]
    forces = [mv.shift(chunks[mv.chips], -1, 0)]
    for j in range(1, mv.chips):
        forces += [mv.chip(chunks[j], j), mv.shift(chunks[mv.chips + j], -1, j)]
    shape = [(half, rows_face)]
    (condensed,) = call(condensed_kernel, shape, load_face_half, [chunks[0]] + forces)

    forward = condensed
    pivot_other = others(pivot[0], [condensed])
    for k in range(1, mv.stories):
        came = mv.gather_story(forward, (k - 1) % 2)
        if k == min(2, mv.stories - 1):
            upper_other = others(upper[0], [pivot_other, forward])
            came[-1], pivot_other = lax.optimization_barrier([came[-1], pivot_other])
        if k == mv.stories - 1:
            above_other = others(couple_above[0], [upper_other, forward])
            came[-1], upper_other = lax.optimization_barrier([came[-1], upper_other])
        (forward,) = call(
            functools.partial(step_kernel, from_chip(len(came), len(came) - 1), k),
            shape,
            *partial_sums(k, shape, came, [lower[0], lower_other]),
            [condensed, forward],
        )
    came = mv.gather_chips(forward)
    (pivoted,) = call(
        functools.partial(end_kernel, from_chip(len(came), len(came) - 1)),
        shape,
        *partial_sums(None, shape, came, [pivot[0], pivot_other]),
    )

    shape_int = [(half, rows_int)]
    face = pivoted
    for k in range(mv.stories - 2, -1, -1):
        came = mv.gather_story(face, k % 2)
        if k == mv.stories - 2:
            below_other = others(couple_below[0], [above_other, face])
            came[-1], above_other = lax.optimization_barrier([came[-1], above_other])
        if k == max(mv.stories - 3, 0):
            inverse_other = others(interior_inverse[0], [below_other, face])
            came[-1], below_other = lax.optimization_barrier([came[-1], below_other])
        if k == 0:
            late, came[0] = lax.optimization_barrier([face, came[0]])
            odd = mv.gather_story(late, 1)
        (face,) = call(
            functools.partial(step_kernel, from_chip(len(came), len(came) - 1), k),
            shape,
            *partial_sums(k, shape, came, [upper[0], upper_other]),
            [pivoted, face],
        )

    here = mv.gather_chips(face)
    here[0], *odd = lax.optimization_barrier([here[0], *odd])
    even = mv.gather_story(face, 0)
    even[-1], inverse_other = lax.optimization_barrier([even[-1], inverse_other])
    rows = [couple_above[0], above_other]
    sofar = []
    for j, piece in enumerate(here):
        kernel = functools.partial(part_kernel, from_chip(len(here), j), None)
        sofar = call(kernel, shape_int, [piece], rows, sofar, cost=4 << 20)
    rows = [couple_below[0], below_other]
    for j, pair in enumerate(zip(even, odd)):
        final = j == len(even) - 1
        sofar = call(
            functools.partial(coupled_kernel, from_chip(len(even), j), final),
            shape_int,
            load_int_half if final else [],
            list(pair),
            rows,
            sofar,
            cost=4 << 20,
        )
    (reduced,) = sofar

    mine, theirs = call(halves_kernel, [(half, own_face)] * 2, [face])
    new_face = call(
        outputs_kernel, [(records, own_face)] * 3, [mine, mv.core(theirs)], cube_face
    )
    came = mv.gather_chips(reduced)
    came[-1], f0, f1, f2 = lax.optimization_barrier([came[-1], *new_face])
    mine, theirs = call(
        functools.partial(last_kernel, from_chip(len(came), len(came) - 1)),
        [(half, own_int)] * 2,
        *partial_sums(None, shape_int, came, [interior_inverse[0], inverse_other]),
    )
    new_int = call(
        outputs_kernel, [(records, own_int)] * 3, [mine, mv.core(theirs)], cube_int
    )
    new_face = [f0, f1, f2]
    return tuple(out.T[None] for out in (*new_int, *new_face))


def solution(mesh):
    whole, rows, cube = P(), P(("groups", "story"), ("rec", "blk")), P(("groups", "story"), ("rec", "blk"), None)
    in_specs = (P("groups"), whole) + (rows,) * 4 + (cube,) * 12
    return jax.shard_map(shards, mesh=mesh, in_specs=in_specs, out_specs=(cube,) * 6, check_vma=False)
```

```python
import functools

import jax
import jax.numpy as jnp
from jax import lax
from jax.experimental import pallas as pl
from jax.experimental.pallas import tpu as pltpu
from jax.sharding import PartitionSpec as P

AXES = ("story", "rec", "blk")
TILE = 256
VMEM = pl.BlockSpec(memory_space=pltpu.VMEM)


def split(value):
    high = value.astype(jnp.bfloat16)
    return high, (value - high.astype(jnp.float32)).astype(jnp.bfloat16)


def stacked(value):
    return jnp.concatenate(split(value), axis=0)


def matmul(left, right, over):
    rows = left.shape[0] // 2
    total = None
    for part in reversed(split(right)):
        both = lax.dot_general(
            left, part, (((1,), (over,)), ((), ())), preferred_element_type=jnp.float32
        )
        both = both[rows:] + both[:rows]
        total = both if total is None else total + both
    return total


def times_rows(left, *refs, columns=slice(None)):
    left = stacked(left)
    count = refs[0].shape[0]
    ends = count * len(refs)
    results = []
    for start in range(0, ends, TILE):
        stop = min(start + TILE, ends)
        blocks = []
        for i, ref in enumerate(refs):
            low, high = max(start - i * count, 0), min(stop - i * count, count)
            if low < high:
                blocks.append(ref[low:high, columns])
        results.append(matmul(left, jnp.concatenate(blocks, axis=0), 1))
    return jnp.concatenate(results, axis=1)


def times(left, ref):
    left = stacked(left)
    width = ref.shape[1]
    columns = [matmul(left, ref[:, n : min(n + TILE, width)], 0) for n in range(0, width, TILE)]
    return jnp.concatenate(columns, axis=1)


def in_order(pieces, own):
    bit = 1
    while bit < len(pieces):
        swap = (own & bit) != 0
        pieces = [jnp.where(swap, pieces[j ^ bit], pieces[j]) for j in range(len(pieces))]
        bit *= 2
    return pieces


def joined(refs, axis="rec"):
    own = lax.axis_index(axis) if len(refs) > 1 else 0
    return jnp.concatenate(in_order([ref[...] for ref in refs], own), axis=1)


def store_rows(ref, value):
    half = value.shape[1] // 2
    swap = lax.axis_index("blk") == 1
    own, other = value[:, :half], value[:, half:]
    ref[...] = jnp.concatenate([jnp.where(swap, other, own), jnp.where(swap, own, other)], axis=1)


def call(kernel, shapes, *groups, cost=0, late=None):
    flat = [value for group in groups for value in group]

    def body(*refs):
        at, parts = 0, []
        for group in groups:
            parts.append(refs[at : at + len(group)])
            at += len(group)
        if late is None:
            kernel(*parts, *refs[at:])
            return
        buffer, sem = refs[-2:]
        copy = pltpu.make_async_copy(refs[at], buffer, sem)
        copy.start()
        kernel(*parts, *refs[at + 1 : -2], copy, buffer)

    out = [jax.ShapeDtypeStruct(shape, jnp.float32) for shape in shapes]
    last = [] if late is None else [pltpu.with_memory_space_constraint(late, pltpu.HBM)]
    return pl.pallas_call(
        body,
        in_specs=[VMEM] * len(flat) + [pl.BlockSpec(memory_space=pltpu.HBM)] * len(last),
        out_specs=[VMEM] * len(out),
        out_shape=out,
        compiler_params=pltpu.CompilerParams(vmem_limit_bytes=24 << 20),
        cost_estimate=pl.CostEstimate(flops=0, bytes_accessed=cost, transcendentals=0) if cost else None,
        scratch_shapes=[*(pltpu.VMEM(x.shape, x.dtype) for x in last), *[pltpu.SemaphoreType.DMA] * len(last)],
    )(*flat, *last)


def staged(*matrices, after):
    held = lax.optimization_barrier([*matrices, *after])[: len(matrices)]
    held = [pltpu.with_memory_space_constraint(matrix, pltpu.HBM) for matrix in held]
    count = len(held)
    rows = held[0].shape[0]
    ends = [0]
    for matrix in held:
        ends.append(ends[-1] + matrix.shape[1])

    def body(*refs):
        out, sems = refs[count:]
        copies = []
        for i in range(count):
            for j in range(2):
                part = pl.ds(j * (rows // 2), rows // 2)
                copies.append(
                    pltpu.make_async_copy(
                        refs[i].at[part, :],
                        out.at[part, ends[i] : ends[i + 1]],
                        sems.at[2 * i + j],
                    )
                )
        for copy in copies:
            copy.start()
        for copy in copies:
            copy.wait()

    return pl.pallas_call(
        body,
        in_specs=[pl.BlockSpec(memory_space=pltpu.HBM)] * count,
        out_specs=VMEM,
        out_shape=pltpu.VMEM((rows, ends[-1]), jnp.float32),
        scratch_shapes=[pltpu.SemaphoreType.DMA((2 * count,))],
        compiler_params=pltpu.CompilerParams(vmem_limit_bytes=24 << 20),
    )(*held)


def forces_kernel(swap_chips, pieces, matrices, mine, theirs, copy, below):
    (rows,) = matrices
    faces = mine.shape[2]
    inner = rows.shape[1] - faces
    inverse = rows.at[:, :inner]
    above = rows.at[:, inner:]
    if swap_chips:
        chips = len(pieces) // 2
        core = lax.axis_index("blk")
        sets = [in_order([pieces[2 * j][...], pieces[2 * j + 1][...]], core) for j in range(chips)]
        sets = [jnp.concatenate(pair, axis=1) for pair in sets]
        full = jnp.concatenate(in_order(sets, lax.axis_index("rec")), axis=1)
    else:
        full = pieces[0][...]
    part = times_rows(full, inverse)
    half = part.shape[0] // 2
    second = lax.axis_index("blk") == 1
    for i, matrix in enumerate((above, below)):
        if i == 1:
            copy.wait()
        force = times(part, matrix)
        mine[i] = jnp.where(second, force[half:], force[:half])
        theirs[i] = jnp.where(second, force[:half], force[half:])


def fetched(kernel, shapes, arrays, *held):
    count = len(arrays)
    arrays = [pltpu.with_memory_space_constraint(value, pltpu.HBM) for value in arrays]

    def body(*refs):
        sources, rest = refs[:count], refs[count:-1]
        buffers, sems = rest[len(held) + len(shapes) :], refs[-1]
        copies = [
            pltpu.make_async_copy(source, buffer, sems.at[i])
            for i, (source, buffer) in enumerate(zip(sources, buffers))
        ]
        for copy in copies:
            copy.start()
        for copy in copies:
            copy.wait()
        kernel(buffers, rest[: len(held)], *rest[len(held) : len(held) + len(shapes)])

    out = [jax.ShapeDtypeStruct(shape, jnp.float32) for shape in shapes]
    return pl.pallas_call(
        body,
        in_specs=[pl.BlockSpec(memory_space=pltpu.HBM)] * count + [VMEM] * len(held),
        out_specs=[VMEM] * len(out),
        out_shape=out,
        scratch_shapes=[pltpu.VMEM(value.shape, value.dtype) for value in arrays]
        + [pltpu.SemaphoreType.DMA((count,))],
        compiler_params=pltpu.CompilerParams(vmem_limit_bytes=24 << 20),
    )(*arrays, *held)


def newmark_load(mass, pattern, disp, vel, acc, ground):
    return mass[...] * (disp[...] + 2.0 * vel[...] + acc[...] - pattern[...] * ground)


def load_int_kernel(fetched_refs, held, load, ground_out):
    ids, table, *arrays = fetched_refs
    records, library = ids.shape[1], table.shape[1]
    shape = (records, records)
    diagonal = lax.broadcasted_iota(jnp.int32, shape, 0) == lax.broadcasted_iota(jnp.int32, shape, 1)
    row = jnp.broadcast_to(ids[...].astype(jnp.float32), shape)
    column = jnp.sum(jnp.where(diagonal, row, 0.0), axis=1, keepdims=True)
    index = lax.broadcasted_iota(jnp.int32, (records, library), 1).astype(jnp.float32)
    ground = jnp.sum(jnp.where(column == index, table[...], 0.0), axis=1, keepdims=True)
    ground_out[...] = jnp.broadcast_to(ground, ground_out.shape)
    load[...] = newmark_load(*arrays, ground)


def load_face_kernel(fetched_refs, held, mine, theirs):
    load = newmark_load(*fetched_refs, held[0][:, :1])
    half = load.shape[0] // 2
    second = lax.axis_index("blk") == 1
    mine[...] = jnp.where(second, load[half:], load[:half])
    theirs[...] = jnp.where(second, load[:half], load[half:])


def records_kernel(whole, mine, theirs):
    value = whole[0][...]
    half = value.shape[0] // 2
    second = lax.axis_index("blk") == 1
    mine[...] = jnp.where(second, value[half:], value[:half])
    theirs[...] = jnp.where(second, value[:half], value[half:])


def by_core(own, other, axis):
    second = lax.axis_index("blk") == 1
    return jnp.concatenate([jnp.where(second, other, own), jnp.where(second, own, other)], axis=axis)


def condensed_kernel(load, forces, out):
    value = by_core(load[0][...], load[1][...], 1)
    for force in forces:
        value = value - force[...]
    out[...] = value


def halves_kernel(whole, mine, theirs):
    value = whole[0][...]
    half = value.shape[1] // 2
    second = lax.axis_index("blk") == 1
    mine[...] = jnp.where(second, value[:, half:], value[:, :half])
    theirs[...] = jnp.where(second, value[:, :half], value[:, half:])


def outputs_kernel(halves, before, new_disp, new_vel, new_acc):
    disp, vel, acc = before
    value = by_core(halves[0][...], halves[1][...], 0)
    change = value - disp[...] - 2.0 * vel[...] - acc[...]
    new_disp[...] = value
    new_vel[...] = vel[...] + acc[...] + change
    new_acc[...] = change


def chunks_kernel(inputs, *outs):
    mine, came = inputs
    chips = len(outs) // 2
    for i in range(2):
        total = mine[i] + came[i]
        width = total.shape[1] // chips
        pieces = [total[:, j * width : (j + 1) * width] for j in range(chips)]
        for j, piece in enumerate(in_order(pieces, lax.axis_index("rec"))):
            outs[i * chips + j][...] = piece


def from_chip(count, j):
    def columns(width):
        if count == 1:
            return slice(None)
        start = (lax.axis_index("rec") ^ j) * width
        return pl.ds(pl.multiple_of(start, 128), width)

    return columns


def plus(value, sofar):
    return value + sofar[0][...] if sofar else value


def part_kernel(columns, story, piece, rows, sofar, out):
    def product():
        value = piece[0][...]
        out[...] = plus(times_rows(value, *rows, columns=columns(value.shape[1])), sofar)

    if story is None:
        product()
    else:
        pl.when(lax.axis_index("story") == story)(product)


def step_kernel(columns, story, piece, rows, sofar, terms, out):
    first, latest = terms

    @pl.when(lax.axis_index("story") == story)
    def _():
        value = piece[0][...]
        value = plus(times_rows(value, *rows, columns=columns(value.shape[1])), sofar)
        store_rows(out, value)
        out[...] = first[...] - out[...]

    @pl.when(lax.axis_index("story") != story)
    def _():
        out[...] = latest[...]


def end_kernel(columns, piece, rows, sofar, out):
    value = piece[0][...]
    store_rows(out, plus(times_rows(value, *rows, columns=columns(value.shape[1])), sofar))


def first_kernel(columns, piece, rows, early, out):
    @pl.when(lax.axis_index("story") == 0)
    def _():
        value = piece[0][...]
        out[...] = times_rows(value, *rows, columns=columns(value.shape[1]))

    @pl.when(lax.axis_index("story") > 0)
    def _():
        out[...] = early[0][...]


def coupled_kernel(columns, final, load, pair, rows, sofar, out):
    even, odd = pair
    story = lax.axis_index("story")

    def finish(value):
        if final:
            store_rows(out, value)
            out[...] = by_core(load[0][...], load[1][...], 1) - out[...]
        else:
            out[...] = value

    @pl.when(story == 0)
    def _():
        finish(sofar[0][...])

    @pl.when(story > 0)
    def _():
        value = jnp.where(lax.rem(story, 2) == 1, even[...], odd[...])
        finish(plus(times_rows(value, *rows, columns=columns(value.shape[1])), sofar))


def last_kernel(columns, piece, rows, sofar, mine, theirs):
    value = piece[0][...]
    value = plus(times_rows(value, *rows, columns=columns(value.shape[1])), sofar)
    half = value.shape[1] // 2
    mine[...] = value[:, :half]
    theirs[...] = value[:, half:]


def partial_sums(story, shape, pieces, rows):
    sofar = []
    for j, piece in enumerate(pieces[:-1]):
        kernel = functools.partial(part_kernel, from_chip(len(pieces), j), story)
        sofar = call(kernel, shape, [piece], rows, sofar, cost=4 << 20)
    return [pieces[-1]], rows, sofar


class Moves:
    def __init__(self):
        self.stories = lax.axis_size("story")
        self.chips = lax.axis_size("rec")
        self.cores = lax.axis_size("blk")
        assert self.cores == 2 and self.chips & (self.chips - 1) == 0
        self.s = lax.axis_index("story")
        self.r = lax.axis_index("rec")
        self.b = lax.axis_index("blk")

    def permute(self, value, target):
        pairs = []
        for s in range(self.stories):
            for r in range(self.chips):
                for b in range(self.cores):
                    t, q, c = target(s, r, b)
                    pairs.append(
                        (
                            (s * self.chips + r) * self.cores + b,
                            (t * self.chips + q) * self.cores + c,
                        )
                    )
        return lax.ppermute(value, AXES, pairs)

    def core(self, value):
        return self.permute(value, lambda s, r, b: (s, r, 1 - b))

    def chip(self, value, j):
        return self.permute(value, lambda s, r, b: (s, r ^ j, b))

    def story(self, value, parity, j):
        def target(s, r, b):
            t = s ^ 1 if parity == 0 else ((s - 1) ^ 1) + 1
            if t < 0 or t >= self.stories:
                return (s, r ^ 1, b) if self.chips > 1 else (s, r, 1 - b)
            return t, r ^ j, b

        return self.permute(value, target)

    def by_core(self, own, other, axis):
        first = jnp.where(self.b == 0, own, other)
        second = jnp.where(self.b == 0, other, own)
        return jnp.concatenate([first, second], axis=axis)

    def by_chip(self, pieces, axis=1):
        bit = 1
        while bit < self.chips:
            swap = (self.r & bit) != 0
            pieces = [jnp.where(swap, pieces[j ^ bit], pieces[j]) for j in range(self.chips)]
            bit *= 2
        return jnp.concatenate(pieces, axis=axis)

    def pieces(self, pieces):
        return pieces if pieces[0].shape[1] % 128 == 0 else [self.by_chip(pieces)]

    def shift(self, value, step, j):
        pairs = []
        for s in range(self.stories):
            if not 0 <= s + step < self.stories:
                continue
            for r in range(self.chips):
                for b in range(self.cores):
                    pairs.append(
                        (
                            (s * self.chips + r) * self.cores + b,
                            ((s + step) * self.chips + (r ^ j)) * self.cores + b,
                        )
                    )
        return lax.ppermute(value, AXES, pairs)

    def gather_chips(self, value):
        return self.pieces([value] + [self.chip(value, j) for j in range(1, self.chips)])

    def gather_story(self, value, parity):
        return self.pieces([self.story(value, parity, j) for j in range(self.chips)])


def shards(
    record_ids,
    ground_table,
    mass_int,
    mass_face,
    pattern_int,
    pattern_face,
    disp_int,
    vel_int,
    acc_int,
    disp_face,
    vel_face,
    acc_face,
    interior_inverse,
    couple_below,
    couple_above,
    lower,
    pivot,
    upper,
):
    mv = Moves()
    library, records = ground_table.shape[0], record_ids.shape[0]
    half = records // 2
    cube_int = [value[0].T for value in (disp_int, vel_int, acc_int)]
    cube_face = [value[0].T for value in (disp_face, vel_face, acc_face)]
    own_int, own_face = cube_int[0].shape[1], cube_face[0].shape[1]
    load_int, ground = fetched(
        load_int_kernel,
        [(records, own_int), (records, 128)],
        [record_ids.reshape(1, records), ground_table.reshape(1, library), mass_int, pattern_int]
        + cube_int,
    )
    rows_int, rows_face = 2 * own_int, 2 * own_face
    faces = couple_above.shape[2]

    def others(matrix, after):
        return mv.core(lax.optimization_barrier([matrix, *after])[0])

    lower_other = mv.core(lower[0])
    across = [mv.chip(load_int, j) for j in range(1, mv.chips)]
    phase_rows = staged(interior_inverse[0], couple_above[0], after=[load_int])
    phase_rows, *across = lax.optimization_barrier([phase_rows, *across])
    beside = [mv.core(piece) for piece in [load_int] + across]
    pieces = [piece for pair in zip([load_int] + across, beside) for piece in pair]
    aligned = load_int.shape[1] % 128 == 0
    if not aligned:
        pieces = [
            mv.by_chip([mv.by_core(pieces[2 * j], pieces[2 * j + 1], 1) for j in range(mv.chips)])
        ]
    mine, theirs = call(
        functools.partial(forces_kernel, aligned),
        [(2, half, faces)] * 2,
        pieces,
        [phase_rows],
        late=couple_below[0],
    )
    chunks = call(
        chunks_kernel,
        [(half, faces // mv.chips)] * (2 * mv.chips),
        [mine, mv.core(theirs)],
    )
    ground, _ = lax.optimization_barrier([ground, chunks[0]])
    mine_face, theirs_face = fetched(
        load_face_kernel, [(half, own_face)] * 2, [mass_face, pattern_face] + cube_face, ground
    )
    load_late, _ = lax.optimization_barrier([load_int, chunks[0]])
    mine_int, theirs_int = call(records_kernel, [(half, own_int)] * 2, [load_late])
    halves = lax.optimization_barrier([mv.core(theirs_face), mv.core(theirs_int)])
    load_face_half, load_int_half = [mine_face, halves[0]], [mine_int, halves[1]]
    forces = [mv.shift(chunks[mv.chips], -1, 0)]
    for j in range(1, mv.chips):
        forces += [mv.chip(chunks[j], j), mv.shift(chunks[mv.chips + j], -1, j)]
    shape = [(half, rows_face)]
    (condensed,) = call(condensed_kernel, shape, load_face_half, [chunks[0]] + forces)

    forward = condensed
    pivot_other = others(pivot[0], [condensed])
    for k in range(1, mv.stories):
        came = mv.gather_story(forward, (k - 1) % 2)
        if k == min(2, mv.stories - 1):
            upper_other = others(upper[0], [pivot_other, forward])
            came[-1], pivot_other = lax.optimization_barrier([came[-1], pivot_other])
        if k == mv.stories - 1:
            above_other = others(couple_above[0], [upper_other, forward])
            came[-1], upper_other = lax.optimization_barrier([came[-1], upper_other])
        (forward,) = call(
            functools.partial(step_kernel, from_chip(len(came), len(came) - 1), k),
            shape,
            *partial_sums(k, shape, came, [lower[0], lower_other]),
            [condensed, forward],
        )
    came = mv.gather_chips(forward)
    (pivoted,) = call(
        functools.partial(end_kernel, from_chip(len(came), len(came) - 1)),
        shape,
        *partial_sums(None, shape, came, [pivot[0], pivot_other]),
    )

    shape_int = [(half, rows_int)]
    face = pivoted
    for k in range(mv.stories - 2, -1, -1):
        came = mv.gather_story(face, k % 2)
        if k == mv.stories - 2:
            below_other = others(couple_below[0], [above_other, face])
            came[-1], above_other = lax.optimization_barrier([came[-1], above_other])
        if k == max(mv.stories - 3, 0):
            inverse_other = others(interior_inverse[0], [below_other, face])
            came[-1], below_other = lax.optimization_barrier([came[-1], below_other])
        if k == 0:
            early = []
            if face.shape[1] % 128 == 0:
                kernel = functools.partial(part_kernel, from_chip(mv.chips, 0), None)
                rows = [couple_above[0], above_other]
                early = call(kernel, shape_int, [face], rows, [], cost=4 << 20)
            late, came[0], *early = lax.optimization_barrier([face, came[0], *early])
            odd = mv.gather_story(late, 1)
        (face,) = call(
            functools.partial(step_kernel, from_chip(len(came), len(came) - 1), k),
            shape,
            *partial_sums(k, shape, came, [upper[0], upper_other]),
            [pivoted, face],
        )

    here = mv.gather_chips(face)
    here[0], *odd = lax.optimization_barrier([here[0], *odd])
    even = mv.gather_story(face, 0)
    even[-1], inverse_other = lax.optimization_barrier([even[-1], inverse_other])
    rows = [couple_above[0], above_other]
    sofar = []
    for j, piece in enumerate(here):
        kernel = functools.partial(part_kernel, from_chip(len(here), j), None)
        if j == 0 and early:
            kernel, sofar = functools.partial(first_kernel, from_chip(len(here), j)), early
        sofar = call(kernel, shape_int, [piece], rows, sofar, cost=4 << 20)
    rows = [couple_below[0], below_other]
    for j, pair in enumerate(zip(even, odd)):
        final = j == len(even) - 1
        sofar = call(
            functools.partial(coupled_kernel, from_chip(len(even), j), final),
            shape_int,
            load_int_half if final else [],
            list(pair),
            rows,
            sofar,
            cost=4 << 20,
        )
    (reduced,) = sofar

    mine, theirs = call(halves_kernel, [(half, own_face)] * 2, [face])
    new_face = call(
        outputs_kernel, [(records, own_face)] * 3, [mine, mv.core(theirs)], cube_face
    )
    came = mv.gather_chips(reduced)
    came[-1], f0, f1, f2 = lax.optimization_barrier([came[-1], *new_face])
    mine, theirs = call(
        functools.partial(last_kernel, from_chip(len(came), len(came) - 1)),
        [(half, own_int)] * 2,
        *partial_sums(None, shape_int, came, [interior_inverse[0], inverse_other]),
    )
    new_int = call(
        outputs_kernel, [(records, own_int)] * 3, [mine, mv.core(theirs)], cube_int
    )
    new_face = [f0, f1, f2]
    return tuple(out.T[None] for out in (*new_int, *new_face))


def solution(mesh):
    whole, rows, cube = P(), P(("groups", "story"), ("rec", "blk")), P(("groups", "story"), ("rec", "blk"), None)
    in_specs = (P("groups"), whole) + (rows,) * 4 + (cube,) * 12
    return jax.shard_map(shards, mesh=mesh, in_specs=in_specs, out_specs=(cube,) * 6, check_vma=False)
```

```python
import functools

import jax
import jax.numpy as jnp
from jax import lax
from jax.experimental import pallas as pl
from jax.experimental.pallas import tpu as pltpu
from jax.sharding import PartitionSpec as P

AXES = ("story", "rec", "blk")
TILE = 256
VMEM = pl.BlockSpec(memory_space=pltpu.VMEM)


def split(value):
    high = value.astype(jnp.bfloat16)
    return high, (value - high.astype(jnp.float32)).astype(jnp.bfloat16)


def stacked(value):
    return jnp.concatenate(split(value), axis=0)


def matmul(left, right, over):
    rows = left.shape[0] // 2
    total = None
    for part in reversed(split(right)):
        both = lax.dot_general(
            left, part, (((1,), (over,)), ((), ())), preferred_element_type=jnp.float32
        )
        both = both[rows:] + both[:rows]
        total = both if total is None else total + both
    return total


def times_rows(left, *refs, columns=slice(None)):
    left = stacked(left)
    count = refs[0].shape[0]
    ends = count * len(refs)
    results = []
    for start in range(0, ends, TILE):
        stop = min(start + TILE, ends)
        blocks = []
        for i, ref in enumerate(refs):
            low, high = max(start - i * count, 0), min(stop - i * count, count)
            if low < high:
                blocks.append(ref[low:high, columns])
        results.append(matmul(left, jnp.concatenate(blocks, axis=0), 1))
    return jnp.concatenate(results, axis=1)


def times(left, ref):
    left = stacked(left)
    width = ref.shape[1]
    columns = [matmul(left, ref[:, n : min(n + TILE, width)], 0) for n in range(0, width, TILE)]
    return jnp.concatenate(columns, axis=1)


def in_order(pieces, own):
    bit = 1
    while bit < len(pieces):
        swap = (own & bit) != 0
        pieces = [jnp.where(swap, pieces[j ^ bit], pieces[j]) for j in range(len(pieces))]
        bit *= 2
    return pieces


def joined(refs, axis="rec"):
    own = lax.axis_index(axis) if len(refs) > 1 else 0
    return jnp.concatenate(in_order([ref[...] for ref in refs], own), axis=1)


def store_rows(ref, value):
    half = value.shape[1] // 2
    swap = lax.axis_index("blk") == 1
    own, other = value[:, :half], value[:, half:]
    ref[...] = jnp.concatenate([jnp.where(swap, other, own), jnp.where(swap, own, other)], axis=1)


def call(kernel, shapes, *groups, cost=0, late=None):
    flat = [value for group in groups for value in group]

    def body(*refs):
        at, parts = 0, []
        for group in groups:
            parts.append(refs[at : at + len(group)])
            at += len(group)
        if late is None:
            kernel(*parts, *refs[at:])
            return
        buffer, sem = refs[-2:]
        copy = pltpu.make_async_copy(refs[at], buffer, sem)
        copy.start()
        kernel(*parts, *refs[at + 1 : -2], copy, buffer)

    out = [jax.ShapeDtypeStruct(shape, jnp.float32) for shape in shapes]
    last = [] if late is None else [pltpu.with_memory_space_constraint(late, pltpu.HBM)]
    return pl.pallas_call(
        body,
        in_specs=[VMEM] * len(flat) + [pl.BlockSpec(memory_space=pltpu.HBM)] * len(last),
        out_specs=[VMEM] * len(out),
        out_shape=out,
        compiler_params=pltpu.CompilerParams(vmem_limit_bytes=24 << 20),
        cost_estimate=pl.CostEstimate(flops=0, bytes_accessed=cost, transcendentals=0) if cost else None,
        scratch_shapes=[*(pltpu.VMEM(x.shape, x.dtype) for x in last), *[pltpu.SemaphoreType.DMA] * len(last)],
    )(*flat, *last)


def staged(*matrices, after):
    held = lax.optimization_barrier([*matrices, *after])[: len(matrices)]
    held = [pltpu.with_memory_space_constraint(matrix, pltpu.HBM) for matrix in held]
    count = len(held)
    rows = held[0].shape[0]
    ends = [0]
    for matrix in held:
        ends.append(ends[-1] + matrix.shape[1])

    def body(*refs):
        out, sems = refs[count:]
        copies = []
        for i in range(count):
            for j in range(2):
                part = pl.ds(j * (rows // 2), rows // 2)
                copies.append(
                    pltpu.make_async_copy(
                        refs[i].at[part, :],
                        out.at[part, ends[i] : ends[i + 1]],
                        sems.at[2 * i + j],
                    )
                )
        for copy in copies:
            copy.start()
        for copy in copies:
            copy.wait()

    return pl.pallas_call(
        body,
        in_specs=[pl.BlockSpec(memory_space=pltpu.HBM)] * count,
        out_specs=VMEM,
        out_shape=pltpu.VMEM((rows, ends[-1]), jnp.float32),
        scratch_shapes=[pltpu.SemaphoreType.DMA((2 * count,))],
        compiler_params=pltpu.CompilerParams(vmem_limit_bytes=24 << 20),
    )(*held)


def load_columns(chip, core, width):
    place = (lax.axis_index("rec") ^ chip) * 2 + (lax.axis_index("blk") ^ core)
    return pl.ds(pl.multiple_of(place * width, 128), width)


def loads_kernel(places, pieces, matrices, out):
    total = None
    for (chip, core), piece in zip(places, pieces):
        value = piece[...]
        part = times_rows(value, matrices[0], columns=load_columns(chip, core, value.shape[1]))
        total = part if total is None else total + part
    out[...] = total


def forces_kernel(place, pieces, matrices, sofar, mine, theirs, copy, below):
    (rows,) = matrices
    faces = mine.shape[2]
    inner = rows.shape[1] - faces
    above = rows.at[:, inner:]
    value = pieces[0][...]
    columns = slice(0, inner) if place is None else load_columns(*place, value.shape[1])
    part = plus(times_rows(value, rows, columns=columns), sofar)
    half = part.shape[0] // 2
    second = lax.axis_index("blk") == 1
    for i, matrix in enumerate((above, below)):
        if i == 1:
            copy.wait()
        force = times(part, matrix)
        mine[i] = jnp.where(second, force[half:], force[:half])
        theirs[i] = jnp.where(second, force[:half], force[half:])


def fetched(kernel, shapes, arrays, *held):
    count = len(arrays)
    arrays = [pltpu.with_memory_space_constraint(value, pltpu.HBM) for value in arrays]

    def body(*refs):
        sources, rest = refs[:count], refs[count:-1]
        buffers, sems = rest[len(held) + len(shapes) :], refs[-1]
        copies = [
            pltpu.make_async_copy(source, buffer, sems.at[i])
            for i, (source, buffer) in enumerate(zip(sources, buffers))
        ]
        for copy in copies:
            copy.start()
        for copy in copies:
            copy.wait()
        kernel(buffers, rest[: len(held)], *rest[len(held) : len(held) + len(shapes)])

    out = [jax.ShapeDtypeStruct(shape, jnp.float32) for shape in shapes]
    return pl.pallas_call(
        body,
        in_specs=[pl.BlockSpec(memory_space=pltpu.HBM)] * count + [VMEM] * len(held),
        out_specs=[VMEM] * len(out),
        out_shape=out,
        scratch_shapes=[pltpu.VMEM(value.shape, value.dtype) for value in arrays]
        + [pltpu.SemaphoreType.DMA((count,))],
        compiler_params=pltpu.CompilerParams(vmem_limit_bytes=24 << 20),
    )(*arrays, *held)


def newmark_load(mass, pattern, disp, vel, acc, ground):
    return mass[...] * (disp[...] + 2.0 * vel[...] + acc[...] - pattern[...] * ground)


def load_int_kernel(fetched_refs, held, load, ground_out):
    ids, table, *arrays = fetched_refs
    records, library = ids.shape[1], table.shape[1]
    shape = (records, records)
    diagonal = lax.broadcasted_iota(jnp.int32, shape, 0) == lax.broadcasted_iota(jnp.int32, shape, 1)
    row = jnp.broadcast_to(ids[...].astype(jnp.float32), shape)
    column = jnp.sum(jnp.where(diagonal, row, 0.0), axis=1, keepdims=True)
    index = lax.broadcasted_iota(jnp.int32, (records, library), 1).astype(jnp.float32)
    ground = jnp.sum(jnp.where(column == index, table[...], 0.0), axis=1, keepdims=True)
    ground_out[...] = jnp.broadcast_to(ground, ground_out.shape)
    load[...] = newmark_load(*arrays, ground)


def load_face_kernel(fetched_refs, held, mine, theirs):
    load = newmark_load(*fetched_refs, held[0][:, :1])
    half = load.shape[0] // 2
    second = lax.axis_index("blk") == 1
    mine[...] = jnp.where(second, load[half:], load[:half])
    theirs[...] = jnp.where(second, load[:half], load[half:])


def records_kernel(whole, mine, theirs):
    value = whole[0][...]
    half = value.shape[0] // 2
    second = lax.axis_index("blk") == 1
    mine[...] = jnp.where(second, value[half:], value[:half])
    theirs[...] = jnp.where(second, value[:half], value[half:])


def by_core(own, other, axis):
    second = lax.axis_index("blk") == 1
    return jnp.concatenate([jnp.where(second, other, own), jnp.where(second, own, other)], axis=axis)


def condensed_kernel(load, forces, out):
    value = by_core(load[0][...], load[1][...], 1)
    for force in forces:
        value = value - force[...]
    out[...] = value


def halves_kernel(whole, mine, theirs):
    value = whole[0][...]
    half = value.shape[1] // 2
    second = lax.axis_index("blk") == 1
    mine[...] = jnp.where(second, value[:, half:], value[:, :half])
    theirs[...] = jnp.where(second, value[:, :half], value[:, half:])


def outputs_kernel(halves, before, new_disp, new_vel, new_acc):
    disp, vel, acc = before
    value = by_core(halves[0][...], halves[1][...], 0)
    change = value - disp[...] - 2.0 * vel[...] - acc[...]
    new_disp[...] = value
    new_vel[...] = vel[...] + acc[...] + change
    new_acc[...] = change


def chunks_kernel(inputs, *outs):
    mine, came = inputs
    chips = len(outs) // 2
    for i in range(2):
        total = mine[i] + came[i]
        width = total.shape[1] // chips
        pieces = [total[:, j * width : (j + 1) * width] for j in range(chips)]
        for j, piece in enumerate(in_order(pieces, lax.axis_index("rec"))):
            outs[i * chips + j][...] = piece


def from_chip(count, j):
    def columns(width):
        if count == 1:
            return slice(None)
        start = (lax.axis_index("rec") ^ j) * width
        return pl.ds(pl.multiple_of(start, 128), width)

    return columns


def plus(value, sofar):
    return value + sofar[0][...] if sofar else value


def part_kernel(columns, story, piece, rows, sofar, out):
    def product():
        value = piece[0][...]
        out[...] = plus(times_rows(value, *rows, columns=columns(value.shape[1])), sofar)

    if story is None:
        product()
    else:
        pl.when(lax.axis_index("story") == story)(product)


def step_kernel(columns, story, piece, rows, sofar, terms, out):
    first, latest = terms

    @pl.when(lax.axis_index("story") == story)
    def _():
        value = piece[0][...]
        value = plus(times_rows(value, *rows, columns=columns(value.shape[1])), sofar)
        store_rows(out, value)
        out[...] = first[...] - out[...]

    @pl.when(lax.axis_index("story") != story)
    def _():
        out[...] = latest[...]


def end_kernel(columns, piece, rows, sofar, out):
    value = piece[0][...]
    store_rows(out, plus(times_rows(value, *rows, columns=columns(value.shape[1])), sofar))


def first_kernel(columns, piece, rows, early, out):
    @pl.when(lax.axis_index("story") == 0)
    def _():
        value = piece[0][...]
        out[...] = times_rows(value, *rows, columns=columns(value.shape[1]))

    @pl.when(lax.axis_index("story") > 0)
    def _():
        out[...] = early[0][...]


def coupled_kernel(columns, final, load, pair, rows, sofar, out):
    even, odd = pair
    story = lax.axis_index("story")

    def finish(value):
        if final:
            store_rows(out, value)
            out[...] = by_core(load[0][...], load[1][...], 1) - out[...]
        else:
            out[...] = value

    @pl.when(story == 0)
    def _():
        finish(sofar[0][...])

    @pl.when(story > 0)
    def _():
        value = jnp.where(lax.rem(story, 2) == 1, even[...], odd[...])
        finish(plus(times_rows(value, *rows, columns=columns(value.shape[1])), sofar))


def last_kernel(columns, piece, rows, sofar, mine, theirs):
    value = piece[0][...]
    value = plus(times_rows(value, *rows, columns=columns(value.shape[1])), sofar)
    half = value.shape[1] // 2
    mine[...] = value[:, :half]
    theirs[...] = value[:, half:]


def partial_sums(story, shape, pieces, rows):
    sofar = []
    for j, piece in enumerate(pieces[:-1]):
        kernel = functools.partial(part_kernel, from_chip(len(pieces), j), story)
        sofar = call(kernel, shape, [piece], rows, sofar, cost=4 << 20)
    return [pieces[-1]], rows, sofar


class Moves:
    def __init__(self):
        self.stories = lax.axis_size("story")
        self.chips = lax.axis_size("rec")
        self.cores = lax.axis_size("blk")
        assert self.cores == 2 and self.chips & (self.chips - 1) == 0
        self.s = lax.axis_index("story")
        self.r = lax.axis_index("rec")
        self.b = lax.axis_index("blk")

    def permute(self, value, target):
        pairs = []
        for s in range(self.stories):
            for r in range(self.chips):
                for b in range(self.cores):
                    t, q, c = target(s, r, b)
                    pairs.append(
                        (
                            (s * self.chips + r) * self.cores + b,
                            (t * self.chips + q) * self.cores + c,
                        )
                    )
        return lax.ppermute(value, AXES, pairs)

    def core(self, value):
        return self.permute(value, lambda s, r, b: (s, r, 1 - b))

    def chip(self, value, j):
        return self.permute(value, lambda s, r, b: (s, r ^ j, b))

    def story(self, value, parity, j):
        def target(s, r, b):
            t = s ^ 1 if parity == 0 else ((s - 1) ^ 1) + 1
            if t < 0 or t >= self.stories:
                return (s, r ^ 1, b) if self.chips > 1 else (s, r, 1 - b)
            return t, r ^ j, b

        return self.permute(value, target)

    def by_core(self, own, other, axis):
        first = jnp.where(self.b == 0, own, other)
        second = jnp.where(self.b == 0, other, own)
        return jnp.concatenate([first, second], axis=axis)

    def by_chip(self, pieces, axis=1):
        bit = 1
        while bit < self.chips:
            swap = (self.r & bit) != 0
            pieces = [jnp.where(swap, pieces[j ^ bit], pieces[j]) for j in range(self.chips)]
            bit *= 2
        return jnp.concatenate(pieces, axis=axis)

    def pieces(self, pieces):
        return pieces if pieces[0].shape[1] % 128 == 0 else [self.by_chip(pieces)]

    def shift(self, value, step, j):
        pairs = []
        for s in range(self.stories):
            if not 0 <= s + step < self.stories:
                continue
            for r in range(self.chips):
                for b in range(self.cores):
                    pairs.append(
                        (
                            (s * self.chips + r) * self.cores + b,
                            ((s + step) * self.chips + (r ^ j)) * self.cores + b,
                        )
                    )
        return lax.ppermute(value, AXES, pairs)

    def gather_chips(self, value):
        return self.pieces([value] + [self.chip(value, j) for j in range(1, self.chips)])

    def gather_story(self, value, parity):
        return self.pieces([self.story(value, parity, j) for j in range(self.chips)])


def shards(
    record_ids,
    ground_table,
    mass_int,
    mass_face,
    pattern_int,
    pattern_face,
    disp_int,
    vel_int,
    acc_int,
    disp_face,
    vel_face,
    acc_face,
    interior_inverse,
    couple_below,
    couple_above,
    lower,
    pivot,
    upper,
):
    mv = Moves()
    library, records = ground_table.shape[0], record_ids.shape[0]
    half = records // 2
    cube_int = [value[0].T for value in (disp_int, vel_int, acc_int)]
    cube_face = [value[0].T for value in (disp_face, vel_face, acc_face)]
    own_int, own_face = cube_int[0].shape[1], cube_face[0].shape[1]
    load_int, ground = fetched(
        load_int_kernel,
        [(records, own_int), (records, 128)],
        [record_ids.reshape(1, records), ground_table.reshape(1, library), mass_int, pattern_int]
        + cube_int,
    )
    rows_int, rows_face = 2 * own_int, 2 * own_face
    faces = couple_above.shape[2]

    def others(matrix, after):
        return mv.core(lax.optimization_barrier([matrix, *after])[0])

    lower_other = mv.core(lower[0])
    across = [mv.chip(load_int, j) for j in range(1, mv.chips)]
    phase_rows = staged(interior_inverse[0], couple_above[0], after=[load_int])
    phase_rows, *across = lax.optimization_barrier([phase_rows, *across])
    beside = [mv.core(piece) for piece in [load_int] + across]
    pieces = [piece for pair in zip([load_int] + across, beside) for piece in pair]
    sofar, place = [], None
    if load_int.shape[1] % 128 == 0:
        places = [(j, i) for j in range(mv.chips) for i in range(2)]
        place, last_piece = places[-1], pieces[-1]
        kernel = functools.partial(loads_kernel, places[:-1])
        shape = [(records, own_int)]
        sofar = call(kernel, shape, pieces[:-1], [phase_rows], cost=4 << 20)
        pieces = [last_piece]
    else:
        pieces = [
            mv.by_chip([mv.by_core(pieces[2 * j], pieces[2 * j + 1], 1) for j in range(mv.chips)])
        ]
    mine, theirs = call(
        functools.partial(forces_kernel, place),
        [(2, half, faces)] * 2,
        pieces,
        [phase_rows],
        sofar,
        late=couple_below[0],
    )
    chunks = call(
        chunks_kernel,
        [(half, faces // mv.chips)] * (2 * mv.chips),
        [mine, mv.core(theirs)],
    )
    ground, _ = lax.optimization_barrier([ground, chunks[0]])
    mine_face, theirs_face = fetched(
        load_face_kernel, [(half, own_face)] * 2, [mass_face, pattern_face] + cube_face, ground
    )
    load_late, _ = lax.optimization_barrier([load_int, chunks[0]])
    mine_int, theirs_int = call(records_kernel, [(half, own_int)] * 2, [load_late])
    halves = lax.optimization_barrier([mv.core(theirs_face), mv.core(theirs_int)])
    load_face_half, load_int_half = [mine_face, halves[0]], [mine_int, halves[1]]
    forces = [mv.shift(chunks[mv.chips], -1, 0)]
    for j in range(1, mv.chips):
        forces += [mv.chip(chunks[j], j), mv.shift(chunks[mv.chips + j], -1, j)]
    shape = [(half, rows_face)]
    (condensed,) = call(condensed_kernel, shape, load_face_half, [chunks[0]] + forces)

    forward = condensed
    pivot_other = others(pivot[0], [condensed])
    for k in range(1, mv.stories):
        came = mv.gather_story(forward, (k - 1) % 2)
        if k == min(2, mv.stories - 1):
            upper_other = others(upper[0], [pivot_other, forward])
            came[-1], pivot_other = lax.optimization_barrier([came[-1], pivot_other])
        if k == mv.stories - 1:
            above_other = others(couple_above[0], [upper_other, forward])
            came[-1], upper_other = lax.optimization_barrier([came[-1], upper_other])
        (forward,) = call(
            functools.partial(step_kernel, from_chip(len(came), len(came) - 1), k),
            shape,
            *partial_sums(k, shape, came, [lower[0], lower_other]),
            [condensed, forward],
        )
    came = mv.gather_chips(forward)
    (pivoted,) = call(
        functools.partial(end_kernel, from_chip(len(came), len(came) - 1)),
        shape,
        *partial_sums(None, shape, came, [pivot[0], pivot_other]),
    )

    shape_int = [(half, rows_int)]
    face = pivoted
    for k in range(mv.stories - 2, -1, -1):
        came = mv.gather_story(face, k % 2)
        if k == mv.stories - 2:
            below_other = others(couple_below[0], [above_other, face])
            came[-1], above_other = lax.optimization_barrier([came[-1], above_other])
        if k == max(mv.stories - 3, 0):
            inverse_other = others(interior_inverse[0], [below_other, face])
            came[-1], below_other = lax.optimization_barrier([came[-1], below_other])
        if k == 0:
            early = []
            if face.shape[1] % 128 == 0:
                kernel = functools.partial(part_kernel, from_chip(mv.chips, 0), None)
                rows = [couple_above[0], above_other]
                early = call(kernel, shape_int, [face], rows, [], cost=4 << 20)
            late, came[0], *early = lax.optimization_barrier([face, came[0], *early])
            odd = mv.gather_story(late, 1)
        (face,) = call(
            functools.partial(step_kernel, from_chip(len(came), len(came) - 1), k),
            shape,
            *partial_sums(k, shape, came, [upper[0], upper_other]),
            [pivoted, face],
        )

    here = mv.gather_chips(face)
    here[0], *odd = lax.optimization_barrier([here[0], *odd])
    even = mv.gather_story(face, 0)
    even[-1], inverse_other = lax.optimization_barrier([even[-1], inverse_other])
    rows = [couple_above[0], above_other]
    sofar = []
    for j, piece in enumerate(here):
        kernel = functools.partial(part_kernel, from_chip(len(here), j), None)
        if j == 0 and early:
            kernel, sofar = functools.partial(first_kernel, from_chip(len(here), j)), early
        sofar = call(kernel, shape_int, [piece], rows, sofar, cost=4 << 20)
    rows = [couple_below[0], below_other]
    for j, pair in enumerate(zip(even, odd)):
        final = j == len(even) - 1
        sofar = call(
            functools.partial(coupled_kernel, from_chip(len(even), j), final),
            shape_int,
            load_int_half if final else [],
            list(pair),
            rows,
            sofar,
            cost=4 << 20,
        )
    (reduced,) = sofar

    mine, theirs = call(halves_kernel, [(half, own_face)] * 2, [face])
    new_face = call(
        outputs_kernel, [(records, own_face)] * 3, [mine, mv.core(theirs)], cube_face
    )
    came = mv.gather_chips(reduced)
    came[-1], f0, f1, f2 = lax.optimization_barrier([came[-1], *new_face])
    mine, theirs = call(
        functools.partial(last_kernel, from_chip(len(came), len(came) - 1)),
        [(half, own_int)] * 2,
        *partial_sums(None, shape_int, came, [interior_inverse[0], inverse_other]),
    )
    new_int = call(
        outputs_kernel, [(records, own_int)] * 3, [mine, mv.core(theirs)], cube_int
    )
    new_face = [f0, f1, f2]
    return tuple(out.T[None] for out in (*new_int, *new_face))


def solution(mesh):
    whole, rows, cube = P(), P(("groups", "story"), ("rec", "blk")), P(("groups", "story"), ("rec", "blk"), None)
    in_specs = (P("groups"), whole) + (rows,) * 4 + (cube,) * 12
    return jax.shard_map(shards, mesh=mesh, in_specs=in_specs, out_specs=(cube,) * 6, check_vma=False)
```

```python
import functools

import jax
import jax.numpy as jnp
from jax import lax
from jax.experimental import pallas as pl
from jax.experimental.pallas import tpu as pltpu
from jax.sharding import PartitionSpec as P

AXES = ("story", "rec", "blk")
TILE = 256
VMEM = pl.BlockSpec(memory_space=pltpu.VMEM)


def split(value):
    high = value.astype(jnp.bfloat16)
    return high, (value - high.astype(jnp.float32)).astype(jnp.bfloat16)


def stacked(value):
    return jnp.concatenate(split(value), axis=0)


def matmul(left, right, over):
    rows = left.shape[0] // 2
    total = None
    for part in reversed(split(right)):
        both = lax.dot_general(
            left, part, (((1,), (over,)), ((), ())), preferred_element_type=jnp.float32
        )
        both = both[rows:] + both[:rows]
        total = both if total is None else total + both
    return total


def times_rows(left, *refs, columns=slice(None)):
    left = stacked(left)
    count = refs[0].shape[0]
    ends = count * len(refs)
    results = []
    for start in range(0, ends, TILE):
        stop = min(start + TILE, ends)
        blocks = []
        for i, ref in enumerate(refs):
            low, high = max(start - i * count, 0), min(stop - i * count, count)
            if low < high:
                blocks.append(ref[low:high, columns])
        results.append(matmul(left, jnp.concatenate(blocks, axis=0), 1))
    return jnp.concatenate(results, axis=1)


def times(left, ref):
    left = stacked(left)
    width = ref.shape[1]
    columns = [matmul(left, ref[:, n : min(n + TILE, width)], 0) for n in range(0, width, TILE)]
    return jnp.concatenate(columns, axis=1)


def in_order(pieces, own):
    bit = 1
    while bit < len(pieces):
        swap = (own & bit) != 0
        pieces = [jnp.where(swap, pieces[j ^ bit], pieces[j]) for j in range(len(pieces))]
        bit *= 2
    return pieces


def joined(refs, axis="rec"):
    own = lax.axis_index(axis) if len(refs) > 1 else 0
    return jnp.concatenate(in_order([ref[...] for ref in refs], own), axis=1)


def store_rows(ref, value):
    half = value.shape[1] // 2
    swap = lax.axis_index("blk") == 1
    own, other = value[:, :half], value[:, half:]
    ref[...] = jnp.concatenate([jnp.where(swap, other, own), jnp.where(swap, own, other)], axis=1)


def call(kernel, shapes, *groups, cost=0, late=None):
    flat = [value for group in groups for value in group]

    def body(*refs):
        at, parts = 0, []
        for group in groups:
            parts.append(refs[at : at + len(group)])
            at += len(group)
        if late is None:
            kernel(*parts, *refs[at:])
            return
        buffer, sem = refs[-2:]
        copy = pltpu.make_async_copy(refs[at], buffer, sem)
        copy.start()
        kernel(*parts, *refs[at + 1 : -2], copy, buffer)

    out = [jax.ShapeDtypeStruct(shape, jnp.float32) for shape in shapes]
    last = [] if late is None else [pltpu.with_memory_space_constraint(late, pltpu.HBM)]
    return pl.pallas_call(
        body,
        in_specs=[VMEM] * len(flat) + [pl.BlockSpec(memory_space=pltpu.HBM)] * len(last),
        out_specs=[VMEM] * len(out),
        out_shape=out,
        compiler_params=pltpu.CompilerParams(vmem_limit_bytes=24 << 20),
        cost_estimate=pl.CostEstimate(flops=0, bytes_accessed=cost, transcendentals=0) if cost else None,
        scratch_shapes=[*(pltpu.VMEM(x.shape, x.dtype) for x in last), *[pltpu.SemaphoreType.DMA] * len(last)],
    )(*flat, *last)


def staged(*matrices, after):
    held = lax.optimization_barrier([*matrices, *after])[: len(matrices)]
    held = [pltpu.with_memory_space_constraint(matrix, pltpu.HBM) for matrix in held]
    count = len(held)
    rows = held[0].shape[0]
    ends = [0]
    for matrix in held:
        ends.append(ends[-1] + matrix.shape[1])

    def body(*refs):
        out, sems = refs[count:]
        copies = []
        for i in range(count):
            for j in range(2):
                part = pl.ds(j * (rows // 2), rows // 2)
                copies.append(
                    pltpu.make_async_copy(
                        refs[i].at[part, :],
                        out.at[part, ends[i] : ends[i + 1]],
                        sems.at[2 * i + j],
                    )
                )
        for copy in copies:
            copy.start()
        for copy in copies:
            copy.wait()

    return pl.pallas_call(
        body,
        in_specs=[pl.BlockSpec(memory_space=pltpu.HBM)] * count,
        out_specs=VMEM,
        out_shape=pltpu.VMEM((rows, ends[-1]), jnp.float32),
        scratch_shapes=[pltpu.SemaphoreType.DMA((2 * count,))],
        compiler_params=pltpu.CompilerParams(vmem_limit_bytes=24 << 20),
    )(*held)


def load_columns(chip, core, width):
    place = (lax.axis_index("rec") ^ chip) * 2 + (lax.axis_index("blk") ^ core)
    return pl.ds(pl.multiple_of(place * width, 128), width)


def loads_kernel(places, pieces, matrices, out):
    total = None
    for (chip, core), piece in zip(places, pieces):
        value = piece[...]
        part = times_rows(value, matrices[0], columns=load_columns(chip, core, value.shape[1]))
        total = part if total is None else total + part
    out[...] = total


def forces_kernel(place, pieces, matrices, sofar, mine, theirs):
    (rows,) = matrices
    faces = mine.shape[2]
    inner = rows.shape[1] - 2 * faces
    above = rows.at[:, inner : inner + faces]
    below = rows.at[:, inner + faces :]
    value = pieces[0][...]
    columns = slice(0, inner) if place is None else load_columns(*place, value.shape[1])
    part = plus(times_rows(value, rows, columns=columns), sofar)
    half = part.shape[0] // 2
    second = lax.axis_index("blk") == 1
    for i, matrix in enumerate((above, below)):
        force = times(part, matrix)
        mine[i] = jnp.where(second, force[half:], force[:half])
        theirs[i] = jnp.where(second, force[:half], force[half:])


def fetched(kernel, shapes, arrays, *held):
    count = len(arrays)
    arrays = [pltpu.with_memory_space_constraint(value, pltpu.HBM) for value in arrays]

    def body(*refs):
        sources, rest = refs[:count], refs[count:-1]
        buffers, sems = rest[len(held) + len(shapes) :], refs[-1]
        copies = [
            pltpu.make_async_copy(source, buffer, sems.at[i])
            for i, (source, buffer) in enumerate(zip(sources, buffers))
        ]
        for copy in copies:
            copy.start()
        for copy in copies:
            copy.wait()
        kernel(buffers, rest[: len(held)], *rest[len(held) : len(held) + len(shapes)])

    out = [jax.ShapeDtypeStruct(shape, jnp.float32) for shape in shapes]
    return pl.pallas_call(
        body,
        in_specs=[pl.BlockSpec(memory_space=pltpu.HBM)] * count + [VMEM] * len(held),
        out_specs=[VMEM] * len(out),
        out_shape=out,
        scratch_shapes=[pltpu.VMEM(value.shape, value.dtype) for value in arrays]
        + [pltpu.SemaphoreType.DMA((count,))],
        compiler_params=pltpu.CompilerParams(vmem_limit_bytes=24 << 20),
    )(*arrays, *held)


def newmark_load(mass, pattern, disp, vel, acc, ground):
    return mass[...] * (disp[...] + 2.0 * vel[...] + acc[...] - pattern[...] * ground)


def load_int_kernel(fetched_refs, held, load, ground_out):
    ids, table, *arrays = fetched_refs
    records, library = ids.shape[1], table.shape[1]
    shape = (records, records)
    diagonal = lax.broadcasted_iota(jnp.int32, shape, 0) == lax.broadcasted_iota(jnp.int32, shape, 1)
    row = jnp.broadcast_to(ids[...].astype(jnp.float32), shape)
    column = jnp.sum(jnp.where(diagonal, row, 0.0), axis=1, keepdims=True)
    index = lax.broadcasted_iota(jnp.int32, (records, library), 1).astype(jnp.float32)
    ground = jnp.sum(jnp.where(column == index, table[...], 0.0), axis=1, keepdims=True)
    ground_out[...] = jnp.broadcast_to(ground, ground_out.shape)
    load[...] = newmark_load(*arrays, ground)


def load_face_kernel(fetched_refs, held, mine, theirs):
    load = newmark_load(*fetched_refs, held[0][:, :1])
    half = load.shape[0] // 2
    second = lax.axis_index("blk") == 1
    mine[...] = jnp.where(second, load[half:], load[:half])
    theirs[...] = jnp.where(second, load[:half], load[half:])


def records_kernel(whole, mine, theirs):
    value = whole[0][...]
    half = value.shape[0] // 2
    second = lax.axis_index("blk") == 1
    mine[...] = jnp.where(second, value[half:], value[:half])
    theirs[...] = jnp.where(second, value[:half], value[half:])


def by_core(own, other, axis):
    second = lax.axis_index("blk") == 1
    return jnp.concatenate([jnp.where(second, other, own), jnp.where(second, own, other)], axis=axis)


def condensed_kernel(load, forces, out):
    value = by_core(load[0][...], load[1][...], 1)
    for force in forces:
        value = value - force[...]
    out[...] = value


def halves_kernel(whole, mine, theirs):
    value = whole[0][...]
    half = value.shape[1] // 2
    second = lax.axis_index("blk") == 1
    mine[...] = jnp.where(second, value[:, half:], value[:, :half])
    theirs[...] = jnp.where(second, value[:, :half], value[:, half:])


def outputs_kernel(halves, before, new_disp, new_vel, new_acc):
    disp, vel, acc = before
    value = by_core(halves[0][...], halves[1][...], 0)
    change = value - disp[...] - 2.0 * vel[...] - acc[...]
    new_disp[...] = value
    new_vel[...] = vel[...] + acc[...] + change
    new_acc[...] = change


def chunks_kernel(inputs, *outs):
    mine, came = inputs
    chips = len(outs) // 2
    for i in range(2):
        total = mine[i] + came[i]
        width = total.shape[1] // chips
        pieces = [total[:, j * width : (j + 1) * width] for j in range(chips)]
        for j, piece in enumerate(in_order(pieces, lax.axis_index("rec"))):
            outs[i * chips + j][...] = piece


def from_chip(count, j):
    def columns(width):
        if count == 1:
            return slice(None)
        start = (lax.axis_index("rec") ^ j) * width
        return pl.ds(pl.multiple_of(start, 128), width)

    return columns


def plus(value, sofar):
    return value + sofar[0][...] if sofar else value


def part_kernel(columns, story, piece, rows, sofar, out):
    def product():
        value = piece[0][...]
        out[...] = plus(times_rows(value, *rows, columns=columns(value.shape[1])), sofar)

    if story is None:
        product()
    else:
        pl.when(lax.axis_index("story") == story)(product)


def step_kernel(columns, story, piece, rows, sofar, terms, out):
    first, latest = terms

    @pl.when(lax.axis_index("story") == story)
    def _():
        value = piece[0][...]
        value = plus(times_rows(value, *rows, columns=columns(value.shape[1])), sofar)
        store_rows(out, value)
        out[...] = first[...] - out[...]

    @pl.when(lax.axis_index("story") != story)
    def _():
        out[...] = latest[...]


def end_kernel(columns, piece, rows, sofar, out):
    value = piece[0][...]
    store_rows(out, plus(times_rows(value, *rows, columns=columns(value.shape[1])), sofar))


def first_kernel(columns, piece, rows, early, out):
    @pl.when(lax.axis_index("story") == 0)
    def _():
        value = piece[0][...]
        out[...] = times_rows(value, *rows, columns=columns(value.shape[1]))

    @pl.when(lax.axis_index("story") > 0)
    def _():
        out[...] = early[0][...]


def coupled_kernel(columns, final, load, pair, rows, sofar, out):
    even, odd = pair
    story = lax.axis_index("story")

    def finish(value):
        if final:
            store_rows(out, value)
            out[...] = by_core(load[0][...], load[1][...], 1) - out[...]
        else:
            out[...] = value

    @pl.when(story == 0)
    def _():
        finish(sofar[0][...])

    @pl.when(story > 0)
    def _():
        value = jnp.where(lax.rem(story, 2) == 1, even[...], odd[...])
        finish(plus(times_rows(value, *rows, columns=columns(value.shape[1])), sofar))


def last_kernel(columns, piece, rows, sofar, mine, theirs):
    value = piece[0][...]
    value = plus(times_rows(value, *rows, columns=columns(value.shape[1])), sofar)
    half = value.shape[1] // 2
    mine[...] = value[:, :half]
    theirs[...] = value[:, half:]


def partial_sums(story, shape, pieces, rows):
    sofar = []
    for j, piece in enumerate(pieces[:-1]):
        kernel = functools.partial(part_kernel, from_chip(len(pieces), j), story)
        sofar = call(kernel, shape, [piece], rows, sofar, cost=4 << 20)
    return [pieces[-1]], rows, sofar


class Moves:
    def __init__(self):
        self.stories = lax.axis_size("story")
        self.chips = lax.axis_size("rec")
        self.cores = lax.axis_size("blk")
        assert self.cores == 2 and self.chips & (self.chips - 1) == 0
        self.s = lax.axis_index("story")
        self.r = lax.axis_index("rec")
        self.b = lax.axis_index("blk")

    def permute(self, value, target):
        pairs = []
        for s in range(self.stories):
            for r in range(self.chips):
                for b in range(self.cores):
                    t, q, c = target(s, r, b)
                    pairs.append(
                        (
                            (s * self.chips + r) * self.cores + b,
                            (t * self.chips + q) * self.cores + c,
                        )
                    )
        return lax.ppermute(value, AXES, pairs)

    def core(self, value):
        return self.permute(value, lambda s, r, b: (s, r, 1 - b))

    def chip(self, value, j):
        return self.permute(value, lambda s, r, b: (s, r ^ j, b))

    def story(self, value, parity, j):
        def target(s, r, b):
            t = s ^ 1 if parity == 0 else ((s - 1) ^ 1) + 1
            if t < 0 or t >= self.stories:
                return (s, r ^ 1, b) if self.chips > 1 else (s, r, 1 - b)
            return t, r ^ j, b

        return self.permute(value, target)

    def by_core(self, own, other, axis):
        first = jnp.where(self.b == 0, own, other)
        second = jnp.where(self.b == 0, other, own)
        return jnp.concatenate([first, second], axis=axis)

    def by_chip(self, pieces, axis=1):
        bit = 1
        while bit < self.chips:
            swap = (self.r & bit) != 0
            pieces = [jnp.where(swap, pieces[j ^ bit], pieces[j]) for j in range(self.chips)]
            bit *= 2
        return jnp.concatenate(pieces, axis=axis)

    def pieces(self, pieces):
        return pieces if pieces[0].shape[1] % 128 == 0 else [self.by_chip(pieces)]

    def shift(self, value, step, j):
        pairs = []
        for s in range(self.stories):
            if not 0 <= s + step < self.stories:
                continue
            for r in range(self.chips):
                for b in range(self.cores):
                    pairs.append(
                        (
                            (s * self.chips + r) * self.cores + b,
                            ((s + step) * self.chips + (r ^ j)) * self.cores + b,
                        )
                    )
        return lax.ppermute(value, AXES, pairs)

    def gather_chips(self, value):
        return self.pieces([value] + [self.chip(value, j) for j in range(1, self.chips)])

    def gather_story(self, value, parity):
        return self.pieces([self.story(value, parity, j) for j in range(self.chips)])


def shards(
    record_ids,
    ground_table,
    mass_int,
    mass_face,
    pattern_int,
    pattern_face,
    disp_int,
    vel_int,
    acc_int,
    disp_face,
    vel_face,
    acc_face,
    interior_inverse,
    couple_below,
    couple_above,
    lower,
    pivot,
    upper,
):
    mv = Moves()
    library, records = ground_table.shape[0], record_ids.shape[0]
    half = records // 2
    cube_int = [value[0].T for value in (disp_int, vel_int, acc_int)]
    cube_face = [value[0].T for value in (disp_face, vel_face, acc_face)]
    own_int, own_face = cube_int[0].shape[1], cube_face[0].shape[1]
    load_int, ground = fetched(
        load_int_kernel,
        [(records, own_int), (records, 128)],
        [record_ids.reshape(1, records), ground_table.reshape(1, library), mass_int, pattern_int]
        + cube_int,
    )
    rows_int, rows_face = 2 * own_int, 2 * own_face
    faces = couple_above.shape[2]

    def others(matrix, after):
        return mv.core(lax.optimization_barrier([matrix, *after])[0])

    lower_other = mv.core(lower[0])
    across = [mv.chip(load_int, j) for j in range(1, mv.chips)]
    phase_rows = staged(
        interior_inverse[0], couple_above[0], couple_below[0], after=[load_int]
    )
    phase_rows, *across = lax.optimization_barrier([phase_rows, *across])
    beside = [mv.core(piece) for piece in [load_int] + across]
    pieces = [piece for pair in zip([load_int] + across, beside) for piece in pair]
    sofar, place = [], None
    if load_int.shape[1] % 128 == 0:
        places = [(j, i) for j in range(mv.chips) for i in range(2)]
        place, last_piece = places[-1], pieces[-1]
        kernel = functools.partial(loads_kernel, places[:-1])
        shape = [(records, own_int)]
        sofar = call(kernel, shape, pieces[:-1], [phase_rows], cost=4 << 20)
        pieces = [last_piece]
    else:
        pieces = [
            mv.by_chip([mv.by_core(pieces[2 * j], pieces[2 * j + 1], 1) for j in range(mv.chips)])
        ]
    mine, theirs = call(
        functools.partial(forces_kernel, place),
        [(2, half, faces)] * 2,
        pieces,
        [phase_rows],
        sofar,
    )
    chunks = call(
        chunks_kernel,
        [(half, faces // mv.chips)] * (2 * mv.chips),
        [mine, mv.core(theirs)],
    )
    ground, _ = lax.optimization_barrier([ground, chunks[0]])
    mine_face, theirs_face = fetched(
        load_face_kernel, [(half, own_face)] * 2, [mass_face, pattern_face] + cube_face, ground
    )
    load_late, _ = lax.optimization_barrier([load_int, chunks[0]])
    mine_int, theirs_int = call(records_kernel, [(half, own_int)] * 2, [load_late])
    halves = lax.optimization_barrier([mv.core(theirs_face), mv.core(theirs_int)])
    load_face_half, load_int_half = [mine_face, halves[0]], [mine_int, halves[1]]
    forces = [mv.shift(chunks[mv.chips], -1, 0)]
    for j in range(1, mv.chips):
        forces += [mv.chip(chunks[j], j), mv.shift(chunks[mv.chips + j], -1, j)]
    shape = [(half, rows_face)]
    (condensed,) = call(condensed_kernel, shape, load_face_half, [chunks[0]] + forces)

    forward = condensed
    pivot_other = others(pivot[0], [condensed])
    for k in range(1, mv.stories):
        came = mv.gather_story(forward, (k - 1) % 2)
        if k == min(2, mv.stories - 1):
            upper_other = others(upper[0], [pivot_other, forward])
            came[-1], pivot_other = lax.optimization_barrier([came[-1], pivot_other])
        if k == mv.stories - 1:
            above_other = others(couple_above[0], [upper_other, forward])
            came[-1], upper_other = lax.optimization_barrier([came[-1], upper_other])
        (forward,) = call(
            functools.partial(step_kernel, from_chip(len(came), len(came) - 1), k),
            shape,
            *partial_sums(k, shape, came, [lower[0], lower_other]),
            [condensed, forward],
        )
    came = mv.gather_chips(forward)
    (pivoted,) = call(
        functools.partial(end_kernel, from_chip(len(came), len(came) - 1)),
        shape,
        *partial_sums(None, shape, came, [pivot[0], pivot_other]),
    )

    shape_int = [(half, rows_int)]
    face = pivoted
    for k in range(mv.stories - 2, -1, -1):
        came = mv.gather_story(face, k % 2)
        if k == mv.stories - 2:
            below_other = others(couple_below[0], [above_other, face])
            came[-1], above_other = lax.optimization_barrier([came[-1], above_other])
        if k == max(mv.stories - 3, 0):
            inverse_other = others(interior_inverse[0], [below_other, face])
            came[-1], below_other = lax.optimization_barrier([came[-1], below_other])
        if k == 0:
            early = []
            if face.shape[1] % 128 == 0:
                kernel = functools.partial(part_kernel, from_chip(mv.chips, 0), None)
                rows = [couple_above[0], above_other]
                early = call(kernel, shape_int, [face], rows, [], cost=4 << 20)
            late, came[0], *early = lax.optimization_barrier([face, came[0], *early])
            odd = mv.gather_story(late, 1)
        (face,) = call(
            functools.partial(step_kernel, from_chip(len(came), len(came) - 1), k),
            shape,
            *partial_sums(k, shape, came, [upper[0], upper_other]),
            [pivoted, face],
        )

    here = mv.gather_chips(face)
    here[0], *odd = lax.optimization_barrier([here[0], *odd])
    even = mv.gather_story(face, 0)
    even[-1], inverse_other = lax.optimization_barrier([even[-1], inverse_other])
    rows = [couple_above[0], above_other]
    sofar = []
    for j, piece in enumerate(here):
        kernel = functools.partial(part_kernel, from_chip(len(here), j), None)
        if j == 0 and early:
            kernel, sofar = functools.partial(first_kernel, from_chip(len(here), j)), early
        sofar = call(kernel, shape_int, [piece], rows, sofar, cost=4 << 20)
    rows = [couple_below[0], below_other]
    for j, pair in enumerate(zip(even, odd)):
        final = j == len(even) - 1
        sofar = call(
            functools.partial(coupled_kernel, from_chip(len(even), j), final),
            shape_int,
            load_int_half if final else [],
            list(pair),
            rows,
            sofar,
            cost=4 << 20,
        )
    (reduced,) = sofar

    mine, theirs = call(halves_kernel, [(half, own_face)] * 2, [face])
    new_face = call(
        outputs_kernel, [(records, own_face)] * 3, [mine, mv.core(theirs)], cube_face
    )
    came = mv.gather_chips(reduced)
    came[-1], f0, f1, f2 = lax.optimization_barrier([came[-1], *new_face])
    mine, theirs = call(
        functools.partial(last_kernel, from_chip(len(came), len(came) - 1)),
        [(half, own_int)] * 2,
        *partial_sums(None, shape_int, came, [interior_inverse[0], inverse_other]),
    )
    new_int = call(
        outputs_kernel, [(records, own_int)] * 3, [mine, mv.core(theirs)], cube_int
    )
    new_face = [f0, f1, f2]
    return tuple(out.T[None] for out in (*new_int, *new_face))


def solution(mesh):
    whole, rows, cube = P(), P(("groups", "story"), ("rec", "blk")), P(("groups", "story"), ("rec", "blk"), None)
    in_specs = (P("groups"), whole) + (rows,) * 4 + (cube,) * 12
    return jax.shard_map(shards, mesh=mesh, in_specs=in_specs, out_specs=(cube,) * 6, check_vma=False)
```
